32 devices in a mesh: section: 2 (over y), dp: 4 (over x, core), tensor: 4 (over z).
Axes of the slice: x: 2, y: 2, z: 4, core: 2. Of those that a mesh axis runs over, the one named last changes fastest.
Arguments:
- inputs: bfloat16 [4, 4096, 1536], P(None, ('dp', 'tensor')), may hold values from -6 to 6
- cotangent: bfloat16 [4, 4096, 1536], P(None, ('dp', 'tensor')), may hold values from -6 to 6
- attn_gain: float32 [2, 1536], P('section'), may hold values from 0.1 to 1.9
- w_query: bfloat16 [2, 1536, 1536], P('section', 'dp', 'tensor'), may hold values from -0.15625 to 0.15625
- w_key: bfloat16 [2, 1536, 768], P('section', 'dp'), may hold values from -0.15625 to 0.15625
- w_value: bfloat16 [2, 1536, 768], P('section', 'dp'), may hold values from -0.15625 to 0.15625
- w_out: bfloat16 [2, 1536, 1536], P('section', 'tensor', 'dp'), may hold values from -0.875 to 0.875
- mlp_gain: float32 [2, 1536], P('section'), may hold values from 0.1 to 1.9
- w_gate: bfloat16 [2, 1536, 4096], P('section', 'dp', 'tensor'), may hold values from -0.15625 to 0.15625
- w_up: bfloat16 [2, 1536, 4096], P('section', 'dp', 'tensor'), may hold values from -0.15625 to 0.15625
- w_down: bfloat16 [2, 4096, 1536], P('section', 'tensor', 'dp'), may hold values from -0.09375 to 0.09375
Outputs:
- outputs: bfloat16 [2, 4, 4096, 1536], P('section', None, ('dp', 'tensor'))
- input_grads: bfloat16 [2, 4, 4096, 1536], P('section', None, ('dp', 'tensor'))
- attn_gain_grad: float32 [2, 1536], P('section')
- w_query_grad: float32 [2, 1536, 1536], P('section', 'dp', 'tensor')
- w_key_grad: float32 [2, 1536, 768], P('section', 'dp')
- w_value_grad: float32 [2, 1536, 768], P('section', 'dp')
- w_out_grad: float32 [2, 1536, 1536], P('section', 'tensor', 'dp')
- mlp_gain_grad: float32 [2, 1536], P('section')
- w_gate_grad: float32 [2, 1536, 4096], P('section', 'dp', 'tensor')
- w_up_grad: float32 [2, 1536, 4096], P('section', 'dp', 'tensor')
- w_down_grad: float32 [2, 4096, 1536], P('section', 'tensor', 'dp')
The draws below stay inside these ranges and needn't reach their ends.
All inputs are finite; a program needn't handle non-finite values.
Results may differ from the reference program's by a relative error of at most 0.04.
Values may be sent and summed in bfloat16 or wider, within the bound.
No kernel may reach another device: no remote copies, remote signals or barrier semaphores. Data moves between devices by JAX's collectives and lax.ppermute only.
A program may use at most 448 MiB of HBM per device.

```python
import jax
import jax.numpy as jnp
from jax import lax

D = 1536
HEADS = 16
KV_HEADS = 8
HD = 96
FF = 4096
L = 1024
SEQS = 1
MB = 4
NTOK = 4096


def steps_of(own_key, extent, pieces, low, largest):
    level, own = 1.0, jax.random.fold_in(own_key, 6)
    for axis_at, shards_of in pieces:
        draws = jnp.exp(jax.random.uniform(jax.random.fold_in(own, axis_at), (shards_of,), jnp.float32, low / len(pieces), largest / len(pieces)))
        level = level * jnp.repeat(draws, extent[axis_at] // shards_of).reshape([-1 if axis == axis_at else 1 for axis in range(len(extent))])
    return level


def scatter_about(own_key, shape, deviation, bound, shards=(), kind=jnp.bfloat16):
    drawn = deviation * jax.random.normal(own_key, shape, jnp.float32)
    if shards:
        drawn = drawn * steps_of(own_key, shape, shards, -0.22, 0.18)
    return jnp.clip(drawn, -bound, bound).astype(kind)


def setup_inputs(seed: int = 0) -> dict:
    splits = jax.random.split(jax.random.key(seed), 12)
    return {
        "inputs": scatter_about(splits[0], (MB, NTOK, D), 1.0, 6.0, ((1, 16),)),
        "cotangent": scatter_about(splits[1], (MB, NTOK, D), 1.0, 6.0, ((1, 16),)),
        "attn_gain": jnp.clip(1.0 + 0.18 * jax.random.normal(splits[2], (2, D), jnp.float32), 0.1, 1.9),
        "w_query": scatter_about(splits[3], (2, D, HEADS * HD), D ** -0.5, 0.15625, ((0, 2), (1, 4), (2, 4))),
        "w_key": scatter_about(splits[4], (2, D, KV_HEADS * HD), D ** -0.5, 0.15625, ((0, 2), (1, 4))),
        "w_value": scatter_about(splits[5], (2, D, KV_HEADS * HD), D ** -0.5, 0.15625, ((0, 2), (1, 4))),
        "w_out": scatter_about(splits[6], (2, HEADS * HD, D), (D // 32) ** -0.5, 0.875, ((0, 2), (1, 4), (2, 4))),
        "mlp_gain": jnp.clip(1.0 + 0.18 * jax.random.normal(splits[7], (2, D), jnp.float32), 0.1, 1.9),
        "w_gate": scatter_about(splits[8], (2, D, FF), D ** -0.5, 0.15625, ((0, 2), (1, 4), (2, 4))),
        "w_up": scatter_about(splits[9], (2, D, FF), D ** -0.5, 0.15625, ((0, 2), (1, 4), (2, 4))),
        "w_down": scatter_about(splits[10], (2, FF, D), FF ** -0.5, 0.09375, ((0, 2), (1, 4), (2, 4))),
    }


@jax.custom_vjp
def low(v):
    return lax.optimization_barrier(v.astype(jnp.bfloat16)).astype(jnp.float32)

@jax.custom_vjp
def low_back(v):
    return v

def low_keep(v):
    return (low(v), None)

def low_pass(kept, grad):
    return (grad,)

def back_keep(v):
    return (v, None)

def back_low(kept, grad):
    return (low(grad),)
low.defvjp(low_keep, low_pass)
low_back.defvjp(back_keep, back_low)
epsilon = 1e-05
rope_base = 100000.0
highest = lax.Precision.HIGHEST

def matmul_high(left, right):
    return jnp.dot(left, right, precision=highest)

def rms_norm(rows, gain):
    return rows * lax.rsqrt(lax.optimization_barrier(jnp.mean(rows * rows, axis=-1, keepdims=True)) + epsilon) * gain

def rotate(values, positions):
    half = values.shape[-1] // 2
    freqs = rope_base ** (-jnp.arange(half, dtype=jnp.float32) / half)
    angles = positions.astype(jnp.float32)[:, None] * freqs[None, :]
    cosine = jnp.cos(angles)[:, None, :]
    sine = jnp.sin(angles)[:, None, :]
    first = values[..., :half]
    second = values[..., half:]
    return jnp.concatenate([first * cosine - second * sine, second * cosine + first * sine], axis=-1)

def attend_sequence(items):
    queries, keys, values = items
    scores = low_back(jnp.einsum('qhd,khd->hqk', queries, keys, precision=highest) * HD ** (-0.5))
    places = jnp.arange(L)
    causal = places[:, None] >= places[None, :]
    scores = jnp.where(causal[None], scores, -1000000000.0)
    probs = low(jax.nn.softmax(scores, axis=-1))
    return jnp.einsum('hqk,khd->qhd', probs, values, precision=highest)

def layer(rows, weights, positions):
    attn_gain, w_query, w_key, w_value, w_out, mlp_gain, w_gate, w_up, w_down = weights
    count = rows.shape[0]
    groups = HEADS // KV_HEADS
    normed = low(rms_norm(rows, attn_gain))
    queries = low_back(matmul_high(normed, w_query)).reshape(count, HEADS, HD)
    queries = low(rotate(queries, positions))
    keys = jnp.repeat(matmul_high(normed, w_key).reshape(count, KV_HEADS, HD), groups, axis=1)
    keys = low(rotate(low_back(keys), positions))
    values = jnp.repeat(matmul_high(normed, w_value).reshape(count, KV_HEADS, HD), groups, axis=1)
    values = low(low_back(values))
    shape = (count // L, L, HEADS, HD)
    mixed = lax.map(jax.checkpoint(attend_sequence), (queries.reshape(shape), keys.reshape(shape), values.reshape(shape)))
    mixed = low(low_back(mixed.reshape(count, HEADS * HD)))
    middle = rows + low_back(matmul_high(mixed, w_out))
    normed_mlp = low(rms_norm(middle, mlp_gain))
    gate = low_back(matmul_high(normed_mlp, w_gate))
    upward = low_back(matmul_high(normed_mlp, w_up))
    hidden = low(jax.nn.silu(gate) * upward)
    return middle + low_back(matmul_high(hidden, w_down))

def forward(inputs, nudge, first_weights, second_weights):
    group = SEQS * L
    blocks = inputs.reshape(-1, group, D)
    shifts = nudge.reshape(-1, group, D)
    positions = jnp.arange(group) % L

    def step(carry, items):
        block, shift = items
        first = low_back(low(layer(low_back(block), first_weights, positions)) + shift)
        second = low(layer(first, second_weights, positions))
        return (carry, (first, second))
    carry, (first, second) = lax.scan(jax.checkpoint(step), jnp.zeros((), jnp.float32), (blocks, shifts))
    return (first.reshape(inputs.shape), second.reshape(inputs.shape))

def reference(inputs, cotangent, attn_gain, w_query, w_key, w_value, w_out, mlp_gain, w_gate, w_up, w_down):
    params = [weight.astype(jnp.float32) for weight in (attn_gain, w_query, w_key, w_value, w_out, mlp_gain, w_gate, w_up, w_down)]
    first_weights = tuple((weight[0] for weight in params))
    second_weights = tuple((weight[1] for weight in params))
    start = inputs.astype(jnp.float32)
    nudge = jnp.zeros_like(start)
    (first, second), pull = jax.vjp(forward, start, nudge, first_weights, second_weights)
    input_grad, middle_grad, first_grads, second_grads = pull((jnp.zeros_like(first), cotangent.astype(jnp.float32)))
    outputs = jnp.stack([first, second]).astype(jnp.bfloat16)
    input_grads = jnp.stack([input_grad, middle_grad]).astype(jnp.bfloat16)
    grads = [jnp.stack([early, later]) for early, later in zip(first_grads, second_grads)]
    return (outputs, input_grads, grads[0], grads[1], grads[2], grads[3], grads[4], grads[5], grads[6], grads[7], grads[8])
```

```python
import jax
import jax.numpy as jnp
from jax import lax
from jax.sharding import PartitionSpec as P

HEADS = 16
KV_HEADS = 8
HD = 96
L = 1024

epsilon = 1e-05
rope_base = 100000.0
bf16 = jnp.bfloat16
f32 = jnp.float32


def shifted(array, axis, by):
    size = lax.axis_size(axis)
    pairs = [(i, i + by) for i in range(size) if 0 <= i + by < size]
    return lax.ppermute(array, axis, pairs)


def swapped(array, axis, bit):
    return lax.ppermute(array, axis, [(i, i ^ bit) for i in range(lax.axis_size(axis))])


def bits_of(size):
    return [1 << k for k in range(size.bit_length() - 1)]


def rotate(values, cosine, sine):
    half = values.shape[-1] // 2
    first = values[..., :half]
    second = values[..., half:]
    return jnp.concatenate(
        [first * cosine - second * sine, second * cosine + first * sine], axis=-1
    )


def mm(left, right):
    return jnp.dot(left, right, preferred_element_type=f32)


def mm_nt(left, right):
    return lax.dot_general(
        left, right, (((1,), (1,)), ((), ())), preferred_element_type=f32
    )


def mm_tn(left, right):
    return lax.dot_general(
        left, right, (((0,), (0,)), ((), ())), preferred_element_type=f32
    )


def norm_forward(rows, gain):
    inverse = lax.rsqrt(jnp.mean(rows * rows, axis=-1, keepdims=True) + epsilon)
    return (rows * inverse * gain, inverse)


def norm_backward(rows, inverse, gain, grad):
    scaled = grad * gain
    mean_term = jnp.mean(scaled * rows, axis=-1, keepdims=True)
    return scaled * inverse - rows * inverse * inverse * inverse * mean_term


def gain_sum(rows, inverse, grad):
    return jnp.sum(grad * rows * inverse, axis=0)


def attention_forward(queries, keys, values, causal):
    scale = HD ** (-0.5)

    def per_head(items):
        q, k, v = items
        scores = jnp.einsum("cqd,kd->cqk", q, k, preferred_element_type=f32) * scale
        scores = jnp.where(causal[None], scores, -1000000000.0)
        top = jnp.max(scores, axis=-1, keepdims=True)
        weights = jnp.exp(scores - top)
        totals = jnp.sum(weights, axis=-1, keepdims=True)
        probs = (weights / totals).astype(bf16)
        mixed = jnp.einsum("cqk,kd->cqd", probs, v, preferred_element_type=f32)
        return (mixed.astype(bf16), top + jnp.log(totals))

    return lax.map(per_head, (queries, keys, values))


def attention_backward(queries, keys, values, mixed_grad, log_totals, causal):
    scale = HD ** (-0.5)

    def per_head(items):
        q, k, v, g, lse = items
        scores = jnp.einsum("cqd,kd->cqk", q, k, preferred_element_type=f32) * scale
        scores = jnp.where(causal[None], scores, -1000000000.0)
        probs = jnp.exp(scores - lse)
        prob_grad = jnp.einsum("cqd,kd->cqk", g, v, preferred_element_type=f32)
        centre = jnp.sum(probs * prob_grad, axis=-1, keepdims=True)
        score_grad = (probs * (prob_grad - centre)).astype(bf16)
        query_grad = jnp.einsum("cqk,kd->cqd", score_grad, k, preferred_element_type=f32) * scale
        key_grad = jnp.einsum("cqk,cqd->kd", score_grad, q, preferred_element_type=f32) * scale
        value_grad = jnp.einsum("cqk,cqd->kd", probs.astype(bf16), g, preferred_element_type=f32)
        return (query_grad, key_grad, value_grad)

    return lax.map(per_head, (queries, keys, values, mixed_grad, log_totals))


def local(
    inputs, cotangent, attn_gain, w_query, w_key, w_value, w_out, mlp_gain, w_gate, w_up, w_down
):
    micro, nloc, width = inputs.shape
    tsize = lax.axis_size("tensor")
    dsize = lax.axis_size("dp")
    ranks = tsize // micro
    n = nloc * micro
    share = width // dsize
    first_section = lax.axis_index("section") == 0
    t = lax.axis_index("tensor")
    d = lax.axis_index("dp")
    seq = t % micro
    seg = t // micro
    copies = HEADS // KV_HEADS
    dims = KV_HEADS * HD
    same_seq = [[g + micro * r for r in range(ranks)] for g in range(micro)]

    def exchange(blocks):
        out = blocks
        for j in range(1, micro):
            sent = lax.dynamic_index_in_dim(blocks, seq ^ j, 0, keepdims=True)
            got = swapped(sent, "tensor", j)
            out = lax.dynamic_update_slice_in_dim(out, got, seq ^ j, 0)
        return out

    def reorder(array, axis):
        return jnp.concatenate(
            [lax.dynamic_slice_in_dim(array, (d ^ m) * share, share, axis) for m in range(dsize)],
            axis=axis,
        )

    def spread_rows(block):
        parts = {0: block}
        for bit in reversed(bits_of(dsize)):
            for m in sorted(parts):
                parts[m ^ bit] = swapped(parts[m], "dp", bit)
        return jnp.concatenate([parts[m] for m in range(dsize)], axis=0)

    def gather_weight(shard):
        whole = lax.all_gather(shard, "tensor", axis=0)
        whole = whole.transpose(1, 0, 2).reshape(share, tsize * shard.shape[1])
        return spread_rows(whole)

    def sum_rows(grad):
        parts = {m: grad[m * share : (m + 1) * share].astype(bf16) for m in range(dsize)}
        for bit in bits_of(dsize):
            for m in sorted(parts):
                if m & bit:
                    continue
                got = swapped(parts[m ^ bit], "dp", bit)
                parts[m] = (parts[m].astype(f32) + got.astype(f32)).astype(bf16)
            parts = {m: part for m, part in parts.items() if not m & bit}
        return parts[0]

    def scatter_weight(grad):
        part = sum_rows(grad)
        part = part.reshape(share, tsize, -1).transpose(1, 0, 2)
        return lax.psum_scatter(part, "tensor", scatter_dimension=0)

    rows_in = reorder(exchange(inputs).reshape(n, width), 1)
    attn_scale = reorder(attn_gain[0], 0)
    mlp_scale = reorder(mlp_gain[0], 0)

    wq = gather_weight(w_query[0])
    wkv = spread_rows(jnp.concatenate([w_key[0], w_value[0]], axis=1))
    wo = gather_weight(w_out[0].T)
    wg = gather_weight(w_gate[0])
    wu = gather_weight(w_up[0])
    wd = gather_weight(w_down[0].T)
    cot = reorder(exchange(cotangent).reshape(n, width), 1)

    places = seg * n + jnp.arange(n)
    half = HD // 2
    freqs = rope_base ** (-jnp.arange(half, dtype=f32) / half)
    angles = places.astype(f32)[:, None] * freqs[None, :]
    cosine = jnp.cos(angles)
    sine = jnp.sin(angles)
    causal = places[:, None] >= jnp.arange(L)[None, :]

    def all_keys(array):
        if ranks == 1:
            return array
        return lax.all_gather(
            array, "tensor", axis=1, tiled=True, axis_index_groups=same_seq
        )

    def own_keys(array):
        if ranks == 1:
            return array
        return lax.psum_scatter(
            array.astype(bf16),
            "tensor",
            scatter_dimension=1,
            tiled=True,
            axis_index_groups=same_seq,
        ).astype(f32)

    def forward(rows_bf):
        rows = rows_bf.astype(f32)
        normed, inverse = norm_forward(rows, attn_scale)
        normed = normed.astype(bf16)
        queries = mm(normed, wq).reshape(n, KV_HEADS, copies, HD).transpose(1, 2, 0, 3)
        queries = rotate(queries, cosine, sine).astype(bf16)
        both = mm(normed, wkv)
        keys = both[:, :dims].reshape(n, KV_HEADS, HD).transpose(1, 0, 2)
        keys = all_keys(rotate(keys, cosine, sine).astype(bf16))
        values = both[:, dims:].reshape(n, KV_HEADS, HD).transpose(1, 0, 2)
        values = all_keys(values.astype(bf16))
        mixed, log_totals = attention_forward(queries, keys, values, causal)
        mixed = mixed.transpose(2, 0, 1, 3).reshape(n, HEADS * HD)
        middle = rows + mm_nt(mixed, wo)
        normed_mlp, inverse_mlp = norm_forward(middle, mlp_scale)
        normed_mlp = normed_mlp.astype(bf16)
        gate = mm(normed_mlp, wg)
        upward = mm(normed_mlp, wu)
        hidden = (jax.nn.silu(gate) * upward).astype(bf16)
        outgoing = (middle + mm_nt(hidden, wd)).astype(bf16)
        kept = (
            rows_bf, inverse, normed, queries, keys, values, log_totals, mixed,
            middle, inverse_mlp, normed_mlp, gate.astype(bf16), upward.astype(bf16), hidden,
        )
        return outgoing, kept

    def backward(grad, kept, weights_too):
        (
            rows_bf, inverse, normed, queries, keys, values, log_totals, mixed,
            middle, inverse_mlp, normed_mlp, gate, upward, hidden,
        ) = kept
        rows = rows_bf.astype(f32)
        gate = gate.astype(f32)
        upward = upward.astype(f32)
        done = []
        if weights_too:
            done.append(scatter_weight(mm_tn(grad, hidden)))
        hidden_grad = mm(grad, wd)
        sigma = jax.nn.sigmoid(gate)
        gate_grad = (hidden_grad * upward * (sigma * (1.0 + gate * (1.0 - sigma)))).astype(bf16)
        up_grad = (hidden_grad * gate * sigma).astype(bf16)
        if weights_too:
            done.append(scatter_weight(mm_tn(normed_mlp, gate_grad)))
            done.append(scatter_weight(mm_tn(normed_mlp, up_grad)))
        mlp_back = mm_nt(gate_grad, wg) + mm_nt(up_grad, wu)
        middle_grad = grad.astype(f32) + norm_backward(middle, inverse_mlp, mlp_scale, mlp_back)
        middle_bf = middle_grad.astype(bf16)
        if weights_too:
            done.append(scatter_weight(mm_tn(middle_bf, mixed)))
        mixed_grad = mm(middle_bf, wo).astype(bf16)
        mixed_grad = mixed_grad.reshape(n, KV_HEADS, copies, HD).transpose(1, 2, 0, 3)
        dq, dk, dv = attention_backward(queries, keys, values, mixed_grad, log_totals, causal)
        dk = own_keys(dk)
        dv = own_keys(dv)
        dq = rotate(dq, cosine, -sine).transpose(2, 0, 1, 3).reshape(n, HEADS * HD).astype(bf16)
        dk = rotate(dk, cosine, -sine).transpose(1, 0, 2).reshape(n, dims)
        dkv = jnp.concatenate([dk, dv.transpose(1, 0, 2).reshape(n, dims)], axis=1).astype(bf16)
        if weights_too:
            done.append(scatter_weight(mm_tn(normed, dq)))
            done.append(scatter_weight(mm_tn(normed, dkv)))
        attn_back = mm_nt(dq, wq) + mm_nt(dkv, wkv)
        outgoing = middle_grad + norm_backward(rows, inverse, attn_scale, attn_back)
        if weights_too:
            done.append(gain_sum(rows, inverse, attn_back))
            done.append(gain_sum(middle, inverse_mlp, mlp_back))
        return outgoing.astype(bf16), done

    first_out, _ = forward(rows_in)
    received = shifted(first_out, "section", 1)
    second_out, kept = forward(jnp.where(first_section, rows_in, received))
    first_grad, _ = backward(cot, kept, False)
    returned = shifted(first_grad, "section", -1)
    second_grad, done = backward(jnp.where(first_section, returned, cot), kept, True)

    def to_places(rows):
        return exchange(reorder(rows, 1).reshape(micro, nloc, width))[None]

    outputs = to_places(second_out)
    input_grads = to_places(second_grad)
    down, gate, up, out, query, kv, attn_sum, mlp_sum = done
    kv = lax.all_gather(kv, "tensor", axis=0).transpose(1, 0, 2).reshape(share, 2 * dims)
    gains = jnp.stack([reorder(attn_sum, 0), reorder(mlp_sum, 0)])
    gains = lax.psum(gains, ("dp", "tensor"))
    return (
        outputs,
        input_grads,
        gains[:1],
        query.astype(f32)[None],
        kv[:, :dims].astype(f32)[None],
        kv[:, dims:].astype(f32)[None],
        out.astype(f32).T[None],
        gains[1:],
        gate.astype(f32)[None],
        up.astype(f32)[None],
        down.astype(f32).T[None],
    )


def solution(mesh):
    in_specs = (
        P(None, ("dp", "tensor"), None),
        P(None, ("dp", "tensor"), None),
        P("section", None),
        P("section", "dp", "tensor"),
        P("section", "dp", None),
        P("section", "dp", None),
        P("section", "tensor", "dp"),
        P("section", None),
        P("section", "dp", "tensor"),
        P("section", "dp", "tensor"),
        P("section", "tensor", "dp"),
    )
    out_specs = (
        P("section", None, ("dp", "tensor"), None),
        P("section", None, ("dp", "tensor"), None),
        P("section", None),
        P("section", "dp", "tensor"),
        P("section", "dp", None),
        P("section", "dp", None),
        P("section", "tensor", "dp"),
        P("section", None),
        P("section", "dp", "tensor"),
        P("section", "dp", "tensor"),
        P("section", "tensor", "dp"),
    )
    return jax.shard_map(local, mesh=mesh, in_specs=in_specs, out_specs=out_specs, check_vma=False)
```

```python
import functools

import jax
import jax.numpy as jnp
from jax import lax
from jax.experimental import pallas as pl
from jax.experimental.pallas import tpu as pltpu
from jax.sharding import PartitionSpec as P

HEADS = 16
KV_HEADS = 8
HD = 96
L = 1024

epsilon = 1e-05
rope_base = 100000.0
bf16 = jnp.bfloat16
f32 = jnp.float32


def shifted(array, axis, by):
    size = lax.axis_size(axis)
    pairs = [(i, i + by) for i in range(size) if 0 <= i + by < size]
    return lax.ppermute(array, axis, pairs)


def swapped(array, axis, bit):
    return lax.ppermute(array, axis, [(i, i ^ bit) for i in range(lax.axis_size(axis))])


def bits_of(size):
    return [1 << k for k in range(size.bit_length() - 1)]


def rotate(values, cosine, sine):
    half = values.shape[-1] // 2
    first = values[..., :half]
    second = values[..., half:]
    return jnp.concatenate(
        [first * cosine - second * sine, second * cosine + first * sine], axis=-1
    )


def mm(left, right):
    return jnp.dot(left, right, preferred_element_type=f32)


def mm_nt(left, right):
    return lax.dot_general(
        left, right, (((1,), (1,)), ((), ())), preferred_element_type=f32
    )


def mm_tn(left, right):
    return lax.dot_general(
        left, right, (((0,), (0,)), ((), ())), preferred_element_type=f32
    )


def norm_forward(rows, gain):
    inverse = lax.rsqrt(jnp.mean(rows * rows, axis=-1, keepdims=True) + epsilon)
    return (rows * inverse * gain, inverse)


def norm_backward(rows, inverse, gain, grad):
    scaled = grad * gain
    mean_term = jnp.mean(scaled * rows, axis=-1, keepdims=True)
    return scaled * inverse - rows * inverse * inverse * inverse * mean_term


def gain_sum(rows, inverse, grad):
    return jnp.sum(grad * rows * inverse, axis=0)


QB = 256
LOG2E = 1.4426950408889634


def score_parts(offset_ref, k_ref, q, i, size, single):
    cols = q.shape[0]
    first = i * size if single else 0
    count = size if single else k_ref.shape[1]
    parts = []
    if first:
        parts.append((0, first, mm_nt(k_ref[0, :first], q)))
    diagonal = mm_nt(k_ref[0, first : first + count], q)
    key_at = first + lax.broadcasted_iota(jnp.int32, (count, cols), 0)
    query_at = i * size + lax.rem(lax.broadcasted_iota(jnp.int32, (count, cols), 1), size)
    if not single:
        query_at = query_at + offset_ref[0]
    diagonal = jnp.where(key_at <= query_at, diagonal, -1e30)
    parts.append((first, count, diagonal))
    return parts


def attend_forward_kernel(offset_ref, q_ref, k_ref, vt_ref, o_ref, lse_ref, *, single):
    copies, n, size_h = q_ref.shape[1:]
    size = min(QB, n)
    factor = HD ** (-0.5) * LOG2E
    for i in range(n // size):
        rows = slice(i * size, (i + 1) * size)
        q = q_ref[0, :, rows, :].reshape(copies * size, size_h)
        parts = score_parts(offset_ref, k_ref, q, i, size, single)
        top = functools.reduce(
            jnp.maximum, [jnp.max(part, axis=0, keepdims=True) for _, _, part in parts]
        )
        total = 0.0
        mixed = 0.0
        for first, count, part in parts:
            weights = jnp.exp2((part - top) * factor)
            total = total + jnp.sum(weights, axis=0, keepdims=True)
            mixed = mixed + mm(vt_ref[0, :, first : first + count], weights.astype(bf16))
        mixed = (mixed * (1.0 / total)).T.astype(bf16)
        o_ref[0, :, rows, :] = mixed.reshape(copies, size, size_h)
        lse_ref[0, i] = top * factor + jnp.log2(total)


def attend_backward_kernel(
    offset_ref, q_ref, k_ref, kt_ref, v_ref, g_ref, lse_ref, dq_ref, dk_ref, dv_ref,
    dk_acc, dv_acc, *, single
):
    copies, n, size_h = q_ref.shape[1:]
    size = min(QB, n)
    scale = HD ** (-0.5)
    factor = scale * LOG2E
    dk_acc[...] = jnp.zeros_like(dk_acc)
    dv_acc[...] = jnp.zeros_like(dv_acc)
    for i in range(n // size):
        rows = slice(i * size, (i + 1) * size)
        q = q_ref[0, :, rows, :].reshape(copies * size, size_h)
        g = g_ref[0, :, rows, :].reshape(copies * size, size_h)
        lse = lse_ref[0, i]
        kept = []
        centre = 0.0
        for first, count, part in score_parts(offset_ref, k_ref, q, i, size, single):
            keys = slice(first, first + count)
            probs = jnp.exp2(part * factor - lse)
            prob_grad = mm_nt(v_ref[0, keys], g)
            dv_acc[keys] += mm(probs.astype(bf16), g)
            centre = centre + jnp.sum(probs * prob_grad, axis=0, keepdims=True)
            kept.append((keys, probs, prob_grad))
        dqt = 0.0
        for keys, probs, prob_grad in kept:
            score_grad = (probs * (prob_grad - centre)).astype(bf16)
            dk_acc[keys] += mm(score_grad, q)
            dqt = dqt + mm(kt_ref[0, :, keys], score_grad)
        dq = (dqt * scale).T.astype(bf16)
        dq_ref[0, :, rows, :] = dq.reshape(copies, size, size_h)
    dk_ref[0] = (dk_acc[...] * scale).astype(dk_ref.dtype)
    dv_ref[0] = dv_acc[...].astype(dv_ref.dtype)


def block_of(shape):
    rest = (0,) * (len(shape) - 1)
    return pl.BlockSpec((1,) + tuple(shape[1:]), lambda h: (h,) + rest)


def attention_forward(queries, keys, values_t, offset, single):
    kv, copies, n, size_h = queries.shape
    size = min(QB, n)
    out_shape = (
        jax.ShapeDtypeStruct(queries.shape, bf16),
        jax.ShapeDtypeStruct((kv, n // size, 1, copies * size), f32),
    )
    operands = (queries, keys, values_t)
    return pl.pallas_call(
        functools.partial(attend_forward_kernel, single=single),
        grid=(kv,),
        in_specs=[pl.BlockSpec(memory_space=pltpu.SMEM)] + [block_of(a.shape) for a in operands],
        out_specs=[block_of(a.shape) for a in out_shape],
        out_shape=out_shape,
        compiler_params=pltpu.CompilerParams(vmem_limit_bytes=40 * 2**20),
        cost_estimate=pl.CostEstimate(
            flops=8 * kv * copies * n * L * HD,
            bytes_accessed=8 * kv * n * 128 * copies,
            transcendentals=kv * copies * n * L,
        ),
        name="attend_forward",
    )(offset, *operands)


def attention_backward(queries, keys, values, mixed_grad, lse, offset, single):
    kv, copies, n, size_h = queries.shape
    count = keys.shape[1]
    out_shape = (
        jax.ShapeDtypeStruct(queries.shape, bf16),
        jax.ShapeDtypeStruct(keys.shape, bf16),
        jax.ShapeDtypeStruct(keys.shape, bf16),
    )
    operands = (queries, keys, keys.transpose(0, 2, 1), values, mixed_grad, lse)
    return pl.pallas_call(
        functools.partial(attend_backward_kernel, single=single),
        grid=(kv,),
        in_specs=[pl.BlockSpec(memory_space=pltpu.SMEM)] + [block_of(a.shape) for a in operands],
        out_specs=[block_of(a.shape) for a in out_shape],
        out_shape=out_shape,
        scratch_shapes=[pltpu.VMEM((count, size_h), f32), pltpu.VMEM((count, size_h), f32)],
        compiler_params=pltpu.CompilerParams(vmem_limit_bytes=40 * 2**20),
        cost_estimate=pl.CostEstimate(
            flops=20 * kv * copies * n * L * HD,
            bytes_accessed=16 * kv * n * 128 * copies,
            transcendentals=kv * copies * n * L,
        ),
        name="attend_backward",
    )(offset, *operands)


def local(
    inputs, cotangent, attn_gain, w_query, w_key, w_value, w_out, mlp_gain, w_gate, w_up, w_down
):
    micro, nloc, width = inputs.shape
    tsize = lax.axis_size("tensor")
    dsize = lax.axis_size("dp")
    ranks = tsize // micro
    n = nloc * micro
    share = width // dsize
    first_section = lax.axis_index("section") == 0
    t = lax.axis_index("tensor")
    d = lax.axis_index("dp")
    seq = t % micro
    seg = t // micro
    copies = HEADS // KV_HEADS
    dims = KV_HEADS * HD
    same_seq = [[g + micro * r for r in range(ranks)] for g in range(micro)]

    def exchange(blocks):
        out = blocks
        for j in range(1, micro):
            sent = lax.dynamic_index_in_dim(blocks, seq ^ j, 0, keepdims=True)
            got = swapped(sent, "tensor", j)
            out = lax.dynamic_update_slice_in_dim(out, got, seq ^ j, 0)
        return out

    def reorder(array, axis):
        return jnp.concatenate(
            [lax.dynamic_slice_in_dim(array, (d ^ m) * share, share, axis) for m in range(dsize)],
            axis=axis,
        )

    def spread_rows(block):
        parts = {0: block}
        for bit in reversed(bits_of(dsize)):
            for m in sorted(parts):
                parts[m ^ bit] = swapped(parts[m], "dp", bit)
        return jnp.concatenate([parts[m] for m in range(dsize)], axis=0)

    def gather_weight(shard):
        whole = lax.all_gather(shard, "tensor", axis=0)
        whole = whole.transpose(1, 0, 2).reshape(share, tsize * shard.shape[1])
        return spread_rows(whole)

    def spread_inputs(array):
        side = lax.axis_index("section")
        mine = exchange(lax.dynamic_slice_in_dim(array, side * (width // 2), width // 2, 2))
        other = swapped(mine, "section", 1)
        whole = jnp.concatenate(
            [jnp.where(first_section, mine, other), jnp.where(first_section, other, mine)], axis=2
        )
        return reorder(whole.reshape(n, width), 1)

    def split_rows(grad):
        return {m: grad[m * share : (m + 1) * share].astype(bf16) for m in range(dsize)}

    def add_partner(parts, bit):
        summed = {}
        for m in sorted(parts):
            if not m & bit:
                got = swapped(parts[m ^ bit], "dp", bit)
                summed[m] = (parts[m].astype(f32) + got.astype(f32)).astype(bf16)
        return summed

    def scatter_columns(part):
        part = part.reshape(share, tsize, -1).transpose(1, 0, 2)
        return lax.psum_scatter(part, "tensor", scatter_dimension=0)

    def finish_rows(parts, bits):
        for bit in bits:
            parts = add_partner(parts, bit)
        return parts

    rows_in = spread_inputs(inputs)
    attn_scale = reorder(attn_gain[0], 0)
    mlp_scale = reorder(mlp_gain[0], 0)

    wq = gather_weight(w_query[0])
    wkv = spread_rows(jnp.concatenate([w_key[0], w_value[0]], axis=1))
    wo = gather_weight(w_out[0].T)
    wg = gather_weight(w_gate[0])
    wu = gather_weight(w_up[0])
    wd = gather_weight(w_down[0].T)

    places = seg * n + jnp.arange(n)
    half = HD // 2
    freqs = rope_base ** (-jnp.arange(half, dtype=f32) / half)
    angles = places.astype(f32)[:, None] * freqs[None, :]
    cosine = jnp.cos(angles)
    sine = jnp.sin(angles)
    single = ranks == 1
    offset = (seg * n).astype(jnp.int32).reshape(1)

    def all_keys(array):
        if single:
            return array
        return lax.all_gather(
            array, "tensor", axis=1, tiled=True, axis_index_groups=same_seq
        )

    def own_keys(array):
        if single:
            return array.astype(f32)
        return lax.psum_scatter(
            array,
            "tensor",
            scatter_dimension=1,
            tiled=True,
            axis_index_groups=same_seq,
        ).astype(f32)

    def token_chunks(count):
        step = n // count
        return [slice(i * step, (i + 1) * step) for i in range(count)]

    def forward(rows_bf):
        rows = rows_bf.astype(f32)
        normed, inverse = norm_forward(rows, attn_scale)
        normed = normed.astype(bf16)
        queries = mm(normed, wq).reshape(n, KV_HEADS, copies, HD).transpose(1, 2, 0, 3)
        queries = rotate(queries, cosine, sine).astype(bf16)
        both = mm(normed, wkv)
        keys = both[:, :dims].reshape(n, KV_HEADS, HD).transpose(1, 0, 2)
        keys = all_keys(rotate(keys, cosine, sine).astype(bf16))
        values = both[:, dims:].reshape(n, KV_HEADS, HD).transpose(1, 0, 2)
        values = all_keys(values.astype(bf16))
        mixed, lse = attention_forward(queries, keys, values.transpose(0, 2, 1), offset, single)
        mixed = mixed.transpose(2, 0, 1, 3).reshape(n, HEADS * HD)
        middle = rows + mm_nt(mixed, wo)
        normed_mlp, inverse_mlp = norm_forward(middle, mlp_scale)
        normed_mlp = normed_mlp.astype(bf16)
        gate = mm(normed_mlp, wg)
        upward = mm(normed_mlp, wu)
        hidden = (jax.nn.silu(gate) * upward).astype(bf16)
        kept = (
            rows_bf, inverse, normed, queries, keys, values, lse, mixed,
            middle, inverse_mlp, normed_mlp, gate.astype(bf16), upward.astype(bf16), hidden,
        )
        return kept

    def layer_output(kept, chunk):
        middle, hidden = kept[8], kept[13]
        return (middle[chunk] + mm_nt(hidden[chunk], wd)).astype(bf16)

    def backward(grad, kept, weights_too):
        (
            rows_bf, inverse, normed, queries, keys, values, lse, mixed,
            middle, inverse_mlp, normed_mlp, gate, upward, hidden,
        ) = kept
        rows = rows_bf.astype(f32)
        gate = gate.astype(f32)
        upward = upward.astype(f32)
        done = None
        low_bits = bits_of(dsize)[:1]
        high_bits = bits_of(dsize)[1:]
        if weights_too:
            down = mm_tn(grad, hidden).astype(bf16)
            grad, down = lax.optimization_barrier((grad, down))
            down = split_rows(down)
        hidden_grad = mm(grad, wd)
        sigma = jax.nn.sigmoid(gate)
        gate_grad = (hidden_grad * upward * (sigma * (1.0 + gate * (1.0 - sigma)))).astype(bf16)
        up_grad = (hidden_grad * gate * sigma).astype(bf16)
        if weights_too:
            down = finish_rows(down, low_bits)
            gate_up = mm_tn(normed_mlp, gate_grad).astype(bf16)
            up_up = mm_tn(normed_mlp, up_grad).astype(bf16)
            gate_grad, up_grad, gate_up, up_up, down = lax.optimization_barrier(
                (gate_grad, up_grad, gate_up, up_up, down)
            )
            gate_up = split_rows(gate_up)
            up_up = split_rows(up_up)
        mlp_back = mm_nt(gate_grad, wg) + mm_nt(up_grad, wu)
        middle_grad = grad.astype(f32) + norm_backward(middle, inverse_mlp, mlp_scale, mlp_back)
        middle_bf = middle_grad.astype(bf16)
        if weights_too:
            out_up = mm_tn(middle_bf, mixed).astype(bf16)
            gate_up = finish_rows(gate_up, low_bits)
            up_up = finish_rows(up_up, low_bits)
            middle_bf, out_up, gate_up, up_up = lax.optimization_barrier(
                (middle_bf, out_up, gate_up, up_up)
            )
            out_up = split_rows(out_up)
        mixed_grad = mm(middle_bf, wo).astype(bf16)
        mixed_grad = mixed_grad.reshape(n, KV_HEADS, copies, HD).transpose(1, 2, 0, 3)
        dq, dk, dv = attention_backward(queries, keys, values, mixed_grad, lse, offset, single)
        dk = own_keys(dk)
        dv = own_keys(dv)
        dq = rotate(dq.astype(f32), cosine, -sine)
        dq = dq.transpose(2, 0, 1, 3).reshape(n, HEADS * HD).astype(bf16)
        dk = rotate(dk, cosine, -sine).transpose(1, 0, 2).reshape(n, dims)
        dkv = jnp.concatenate([dk, dv.transpose(1, 0, 2).reshape(n, dims)], axis=1).astype(bf16)
        if not weights_too:
            outgoing = []
            for chunk in token_chunks(4):
                attn_back = mm_nt(dq[chunk], wq) + mm_nt(dkv[chunk], wkv)
                branch = norm_backward(rows[chunk], inverse[chunk], attn_scale, attn_back)
                outgoing.append((middle_grad[chunk] + branch).astype(bf16))
            return outgoing
        query_up = mm_tn(normed, dq).astype(bf16)
        kv_up = mm_tn(normed, dkv).astype(bf16)
        dq, dkv, query_up, kv_up = lax.optimization_barrier((dq, dkv, query_up, kv_up))
        attn_back = mm_nt(dq, wq) + mm_nt(dkv, wkv)
        outgoing = middle_grad + norm_backward(rows, inverse, attn_scale, attn_back)
        sums = [
            scatter_columns(finish_rows(parts, bits)[0])
            for parts, bits in (
                (down, high_bits), (gate_up, high_bits), (up_up, high_bits),
                (out_up, bits_of(dsize)),
                (split_rows(query_up), bits_of(dsize)),
                (split_rows(kv_up), bits_of(dsize)),
            )
        ]
        gains = jnp.stack(
            [gain_sum(rows, inverse, attn_back), gain_sum(middle, inverse_mlp, mlp_back)]
        )
        return outgoing.astype(bf16), sums, gains

    def to_places(rows):
        return exchange(reorder(rows, 1).reshape(micro, nloc, width))[None]

    kept = forward(rows_in)
    received = jnp.concatenate(
        [shifted(layer_output(kept, chunk), "section", 1) for chunk in token_chunks(4)], axis=0
    )
    received, late_cotangent = lax.optimization_barrier((received, cotangent))
    kept = forward(jnp.where(first_section, rows_in, received))
    second_out = layer_output(kept, slice(0, n))
    cot = spread_inputs(late_cotangent)
    first_grad = backward(cot, kept, False)
    outputs = to_places(second_out)
    returned = jnp.concatenate([shifted(part, "section", -1) for part in first_grad], axis=0)
    returned, outputs = lax.optimization_barrier((returned, outputs))
    second_grad, sums, gains = backward(jnp.where(first_section, returned, cot), kept, True)
    input_grads = to_places(second_grad)
    down, gate, up, out, query, kv = sums
    kv = lax.all_gather(kv, "tensor", axis=0).transpose(1, 0, 2).reshape(share, 2 * dims)
    gains = reorder(gains, 1)
    for axis, size in (("dp", dsize), ("tensor", tsize)):
        for bit in bits_of(size):
            gains = gains + swapped(gains, axis, bit)
    return (
        outputs,
        input_grads,
        gains[:1],
        query.astype(f32)[None],
        kv[:, :dims].astype(f32)[None],
        kv[:, dims:].astype(f32)[None],
        out.astype(f32).T[None],
        gains[1:],
        gate.astype(f32)[None],
        up.astype(f32)[None],
        down.astype(f32).T[None],
    )


def solution(mesh):
    in_specs = (
        P(None, ("dp", "tensor"), None),
        P(None, ("dp", "tensor"), None),
        P("section", None),
        P("section", "dp", "tensor"),
        P("section", "dp", None),
        P("section", "dp", None),
        P("section", "tensor", "dp"),
        P("section", None),
        P("section", "dp", "tensor"),
        P("section", "dp", "tensor"),
        P("section", "tensor", "dp"),
    )
    out_specs = (
        P("section", None, ("dp", "tensor"), None),
        P("section", None, ("dp", "tensor"), None),
        P("section", None),
        P("section", "dp", "tensor"),
        P("section", "dp", None),
        P("section", "dp", None),
        P("section", "tensor", "dp"),
        P("section", None),
        P("section", "dp", "tensor"),
        P("section", "dp", "tensor"),
        P("section", "tensor", "dp"),
    )
    return jax.shard_map(local, mesh=mesh, in_specs=in_specs, out_specs=out_specs, check_vma=False)
```

```python
import functools

import jax
import jax.numpy as jnp
from jax import lax
from jax.experimental import pallas as pl
from jax.experimental.pallas import tpu as pltpu
from jax.sharding import PartitionSpec as P

HEADS = 16
KV_HEADS = 8
HD = 96
L = 1024

epsilon = 1e-05
rope_base = 100000.0
bf16 = jnp.bfloat16
f32 = jnp.float32


def shifted(array, axis, by):
    size = lax.axis_size(axis)
    pairs = [(i, i + by) for i in range(size) if 0 <= i + by < size]
    return lax.ppermute(array, axis, pairs)


def swapped(array, axis, bit):
    return lax.ppermute(array, axis, [(i, i ^ bit) for i in range(lax.axis_size(axis))])


def bits_of(size):
    return [1 << k for k in range(size.bit_length() - 1)]


def rotate(values, cosine, sine):
    half = values.shape[-1] // 2
    first = values[..., :half]
    second = values[..., half:]
    return jnp.concatenate(
        [first * cosine - second * sine, second * cosine + first * sine], axis=-1
    )


def mm(left, right):
    return jnp.dot(left, right, preferred_element_type=f32)


def mm_nt(left, right):
    return lax.dot_general(
        left, right, (((1,), (1,)), ((), ())), preferred_element_type=f32
    )


def mm_tn(left, right):
    return lax.dot_general(
        left, right, (((0,), (0,)), ((), ())), preferred_element_type=f32
    )


def norm_forward(rows, gain):
    inverse = lax.rsqrt(jnp.mean(rows * rows, axis=-1, keepdims=True) + epsilon)
    return (rows * inverse * gain, inverse)


def norm_backward(rows, inverse, gain, grad):
    scaled = grad * gain
    mean_term = jnp.mean(scaled * rows, axis=-1, keepdims=True)
    return scaled * inverse - rows * inverse * inverse * inverse * mean_term


def gain_sum(rows, inverse, grad):
    return jnp.sum(grad * rows * inverse, axis=0)


QB = 256
LOG2E = 1.4426950408889634


def score_parts(offset_ref, k_ref, q, i, size, single):
    cols = q.shape[0]
    first = i * size if single else 0
    count = size if single else k_ref.shape[1]
    parts = []
    if first:
        parts.append((0, first, mm_nt(k_ref[0, :first], q)))
    diagonal = mm_nt(k_ref[0, first : first + count], q)
    key_at = first + lax.broadcasted_iota(jnp.int32, (count, cols), 0)
    query_at = i * size + lax.rem(lax.broadcasted_iota(jnp.int32, (count, cols), 1), size)
    if not single:
        query_at = query_at + offset_ref[0]
    diagonal = jnp.where(key_at <= query_at, diagonal, -1e30)
    parts.append((first, count, diagonal))
    return parts


def attend_forward_kernel(offset_ref, q_ref, k_ref, vt_ref, o_ref, lse_ref, *, single):
    copies, n, size_h = q_ref.shape[1:]
    size = min(QB, n)
    factor = HD ** (-0.5) * LOG2E
    for i in range(n // size):
        rows = slice(i * size, (i + 1) * size)
        q = q_ref[0, :, rows, :].reshape(copies * size, size_h)
        parts = score_parts(offset_ref, k_ref, q, i, size, single)
        top = functools.reduce(
            jnp.maximum, [jnp.max(part, axis=0, keepdims=True) for _, _, part in parts]
        )
        total = 0.0
        mixed = 0.0
        for first, count, part in parts:
            weights = jnp.exp2((part - top) * factor)
            total = total + jnp.sum(weights, axis=0, keepdims=True)
            mixed = mixed + mm(vt_ref[0, :, first : first + count], weights.astype(bf16))
        mixed = (mixed * (1.0 / total)).T.astype(bf16)
        o_ref[0, :, rows, :] = mixed.reshape(copies, size, size_h)
        lse_ref[0, i] = top * factor + jnp.log2(total)


def attend_backward_kernel(
    offset_ref, q_ref, k_ref, kt_ref, v_ref, g_ref, lse_ref, dq_ref, dk_ref, dv_ref,
    dk_acc, dv_acc, *, single
):
    copies, n, size_h = q_ref.shape[1:]
    size = min(QB, n)
    scale = HD ** (-0.5)
    factor = scale * LOG2E
    dk_acc[...] = jnp.zeros_like(dk_acc)
    dv_acc[...] = jnp.zeros_like(dv_acc)
    for i in range(n // size):
        rows = slice(i * size, (i + 1) * size)
        q = q_ref[0, :, rows, :].reshape(copies * size, size_h)
        g = g_ref[0, :, rows, :].reshape(copies * size, size_h)
        lse = lse_ref[0, i]
        kept = []
        centre = 0.0
        for first, count, part in score_parts(offset_ref, k_ref, q, i, size, single):
            keys = slice(first, first + count)
            probs = jnp.exp2(part * factor - lse)
            prob_grad = mm_nt(v_ref[0, keys], g)
            dv_acc[keys] += mm(probs.astype(bf16), g)
            centre = centre + jnp.sum(probs * prob_grad, axis=0, keepdims=True)
            kept.append((keys, probs, prob_grad))
        dqt = 0.0
        for keys, probs, prob_grad in kept:
            score_grad = (probs * (prob_grad - centre)).astype(bf16)
            dk_acc[keys] += mm(score_grad, q)
            dqt = dqt + mm(kt_ref[0, :, keys], score_grad)
        dq = (dqt * scale).T.astype(bf16)
        dq_ref[0, :, rows, :] = dq.reshape(copies, size, size_h)
    dk_ref[0] = (dk_acc[...] * scale).astype(dk_ref.dtype)
    dv_ref[0] = dv_acc[...].astype(dv_ref.dtype)


def block_of(shape):
    rest = (0,) * (len(shape) - 1)
    return pl.BlockSpec((1,) + tuple(shape[1:]), lambda h: (h,) + rest)


def attention_forward(queries, keys, values_t, offset, single):
    kv, copies, n, size_h = queries.shape
    size = min(QB, n)
    out_shape = (
        jax.ShapeDtypeStruct(queries.shape, bf16),
        jax.ShapeDtypeStruct((kv, n // size, 1, copies * size), f32),
    )
    operands = (queries, keys, values_t)
    return pl.pallas_call(
        functools.partial(attend_forward_kernel, single=single),
        grid=(kv,),
        in_specs=[pl.BlockSpec(memory_space=pltpu.SMEM)] + [block_of(a.shape) for a in operands],
        out_specs=[block_of(a.shape) for a in out_shape],
        out_shape=out_shape,
        compiler_params=pltpu.CompilerParams(vmem_limit_bytes=40 * 2**20),
        cost_estimate=pl.CostEstimate(
            flops=8 * kv * copies * n * L * HD,
            bytes_accessed=8 * kv * n * 128 * copies,
            transcendentals=kv * copies * n * L,
        ),
        name="attend_forward",
    )(offset, *operands)


def attention_backward(queries, keys, values, mixed_grad, lse, offset, single):
    kv, copies, n, size_h = queries.shape
    count = keys.shape[1]
    out_shape = (
        jax.ShapeDtypeStruct(queries.shape, bf16),
        jax.ShapeDtypeStruct(keys.shape, bf16),
        jax.ShapeDtypeStruct(keys.shape, bf16),
    )
    operands = (queries, keys, keys.transpose(0, 2, 1), values, mixed_grad, lse)
    return pl.pallas_call(
        functools.partial(attend_backward_kernel, single=single),
        grid=(kv,),
        in_specs=[pl.BlockSpec(memory_space=pltpu.SMEM)] + [block_of(a.shape) for a in operands],
        out_specs=[block_of(a.shape) for a in out_shape],
        out_shape=out_shape,
        scratch_shapes=[pltpu.VMEM((count, size_h), f32), pltpu.VMEM((count, size_h), f32)],
        compiler_params=pltpu.CompilerParams(vmem_limit_bytes=40 * 2**20),
        cost_estimate=pl.CostEstimate(
            flops=20 * kv * copies * n * L * HD,
            bytes_accessed=16 * kv * n * 128 * copies,
            transcendentals=kv * copies * n * L,
        ),
        name="attend_backward",
    )(offset, *operands)


def local(
    inputs, cotangent, attn_gain, w_query, w_key, w_value, w_out, mlp_gain, w_gate, w_up, w_down
):
    micro, nloc, width = inputs.shape
    tsize = lax.axis_size("tensor")
    dsize = lax.axis_size("dp")
    ranks = tsize // micro
    n = nloc * micro
    share = width // dsize
    first_section = lax.axis_index("section") == 0
    t = lax.axis_index("tensor")
    d = lax.axis_index("dp")
    seq = t % micro
    seg = t // micro
    copies = HEADS // KV_HEADS
    dims = KV_HEADS * HD
    low_bits = bits_of(dsize)[:1]
    high_bits = bits_of(dsize)[1:]
    same_seq = [[g + micro * r for r in range(ranks)] for g in range(micro)]

    def exchange(blocks):
        out = blocks
        for j in range(1, micro):
            sent = lax.dynamic_index_in_dim(blocks, seq ^ j, 0, keepdims=True)
            got = swapped(sent, "tensor", j)
            out = lax.dynamic_update_slice_in_dim(out, got, seq ^ j, 0)
        return out

    def reorder(array, axis):
        return jnp.concatenate(
            [lax.dynamic_slice_in_dim(array, (d ^ m) * share, share, axis) for m in range(dsize)],
            axis=axis,
        )

    def swap_in(parts, bit):
        parts = dict(parts)
        for m in sorted(parts):
            parts[m ^ bit] = swapped(parts[m], "dp", bit)
        return parts

    def spread_far(block):
        parts = {0: block}
        for bit in reversed(high_bits):
            parts = swap_in(parts, bit)
        return parts

    def spread_near(parts):
        for bit in low_bits:
            parts = swap_in(parts, bit)
        return jnp.concatenate([parts[m] for m in range(dsize)], axis=0)

    def gather_columns(shard):
        whole = lax.all_gather(shard, "tensor", axis=0)
        return whole.transpose(1, 0, 2).reshape(share, tsize * shard.shape[1])

    def tied(*arrays):
        return lax.optimization_barrier(arrays)

    def exchange_half(array):
        side = lax.axis_index("section")
        return exchange(lax.dynamic_slice_in_dim(array, side * (width // 2), width // 2, 2))

    def join_halves(mine):
        other = swapped(mine, "section", 1)
        whole = jnp.concatenate(
            [jnp.where(first_section, mine, other), jnp.where(first_section, other, mine)], axis=2
        )
        return reorder(whole.reshape(n, width), 1)

    def split_rows(grad):
        return {m: grad[m * share : (m + 1) * share].astype(bf16) for m in range(dsize)}

    def add_partner(parts, bits):
        for bit in bits:
            summed = {}
            for m in sorted(parts):
                if not m & bit:
                    got = swapped(parts[m ^ bit], "dp", bit)
                    summed[m] = (parts[m].astype(f32) + got.astype(f32)).astype(bf16)
            parts = summed
        return parts

    def scatter_columns(part):
        part = part.reshape(share, tsize, -1).transpose(1, 0, 2)
        return lax.psum_scatter(part, "tensor", scatter_dimension=0)

    PIECES = 2
    cols = w_gate.shape[2] // PIECES

    def pieces_of(array):
        return [array[:, i * cols : (i + 1) * cols] for i in range(PIECES)]

    attn_scale = reorder(attn_gain[0], 0)
    mlp_scale = reorder(mlp_gain[0], 0)
    mine = exchange_half(inputs)
    far_kv = spread_far(jnp.concatenate([w_key[0], w_value[0]], axis=1))
    mine, far_kv = tied(mine, far_kv)
    rows_in = join_halves(mine)
    wkv = spread_near(far_kv)
    wq = spread_near(spread_far(gather_columns(w_query[0])))
    wo = spread_near(spread_far(gather_columns(w_out[0].T)))
    far_gate = [spread_far(gather_columns(part)) for part in pieces_of(w_gate[0])]
    far_up = [spread_far(gather_columns(part)) for part in pieces_of(w_up[0])]
    far_down = [spread_far(gather_columns(part)) for part in pieces_of(w_down[0].T)]
    wg = [spread_near(part) for part in far_gate]
    wu = [spread_near(part) for part in far_up]

    places = seg * n + jnp.arange(n)
    half = HD // 2
    freqs = rope_base ** (-jnp.arange(half, dtype=f32) / half)
    angles = places.astype(f32)[:, None] * freqs[None, :]
    cosine = jnp.cos(angles)
    sine = jnp.sin(angles)
    single = ranks == 1
    offset = (seg * n).astype(jnp.int32).reshape(1)

    def all_keys(array):
        if single:
            return array
        return lax.all_gather(
            array, "tensor", axis=1, tiled=True, axis_index_groups=same_seq
        )

    def own_keys(array):
        if single:
            return array.astype(f32)
        return lax.psum_scatter(
            array,
            "tensor",
            scatter_dimension=1,
            tiled=True,
            axis_index_groups=same_seq,
        ).astype(f32)

    def token_chunks(count):
        step = n // count
        return [slice(i * step, (i + 1) * step) for i in range(count)]

    def forward(rows_bf, extra=None):
        rows = rows_bf.astype(f32)
        normed, inverse = norm_forward(rows, attn_scale)
        normed = normed.astype(bf16)
        queries = mm(normed, wq).reshape(n, KV_HEADS, copies, HD).transpose(1, 2, 0, 3)
        queries = rotate(queries, cosine, sine).astype(bf16)
        both = mm(normed, wkv)
        keys = both[:, :dims].reshape(n, KV_HEADS, HD).transpose(1, 0, 2)
        keys = all_keys(rotate(keys, cosine, sine).astype(bf16))
        values = both[:, dims:].reshape(n, KV_HEADS, HD).transpose(1, 0, 2)
        values = all_keys(values.astype(bf16))
        mixed, lse = attention_forward(queries, keys, values.transpose(0, 2, 1), offset, single)
        mixed = mixed.transpose(2, 0, 1, 3).reshape(n, HEADS * HD)
        if extra is not None:
            mixed, extra = tied(mixed, extra)
        middle = rows + mm_nt(mixed, wo)
        normed_mlp, inverse_mlp = norm_forward(middle, mlp_scale)
        normed_mlp = normed_mlp.astype(bf16)
        gates, ups, hiddens = [], [], []
        for w1, w2 in zip(wg, wu):
            gate = mm(normed_mlp, w1)
            upward = mm(normed_mlp, w2)
            hiddens.append((jax.nn.silu(gate) * upward).astype(bf16))
            gates.append(gate.astype(bf16))
            ups.append(upward.astype(bf16))
        kept = (
            rows_bf, inverse, normed, queries, keys, values, lse, mixed,
            middle, inverse_mlp, normed_mlp, gates, ups, hiddens,
        )
        return kept, extra

    def layer_output(kept, chunk):
        middle, hiddens = kept[8], kept[13]
        total = middle[chunk]
        for hidden, w in zip(hiddens, wd):
            total = total + mm_nt(hidden[chunk], w)
        return total.astype(bf16)

    def backward(grad, kept, weights_too, extra=None):
        (
            rows_bf, inverse, normed, queries, keys, values, lse, mixed,
            middle, inverse_mlp, normed_mlp, gates, ups, hiddens,
        ) = kept
        rows = rows_bf.astype(f32)
        near_bits = low_bits
        if weights_too:
            downs = [mm_tn(grad, hidden).astype(bf16) for hidden in hiddens]
            grad, downs = tied(grad, downs)
            downs = [add_partner(split_rows(part), near_bits) for part in downs]
        gate_grads, up_grads = [], []
        for gate, upward, w in zip(gates, ups, wd):
            gate = gate.astype(f32)
            hidden_grad = mm(grad, w)
            sigma = jax.nn.sigmoid(gate)
            gate_grads.append(
                (hidden_grad * upward.astype(f32) * (sigma * (1.0 + gate * (1.0 - sigma)))).astype(bf16)
            )
            up_grads.append((hidden_grad * gate * sigma).astype(bf16))
        if weights_too:
            gate_grads, up_grads, downs = tied(gate_grads, up_grads, downs)
            downs = [add_partner(part, high_bits) for part in downs]
            gate_ups = [mm_tn(normed_mlp, part).astype(bf16) for part in gate_grads]
            gate_grads, up_grads, gate_ups = tied(gate_grads, up_grads, gate_ups)
            up_ups = [mm_tn(normed_mlp, part).astype(bf16) for part in up_grads]
            gate_ups = [add_partner(split_rows(part), near_bits) for part in gate_ups]
            gate_grads, up_grads, gate_ups, up_ups = tied(gate_grads, up_grads, gate_ups, up_ups)
            gate_ups = [add_partner(part, high_bits) for part in gate_ups]
            up_ups = [add_partner(split_rows(part), near_bits) for part in up_ups]
        mlp_back = 0.0
        for gate_grad, up_grad, w1, w2 in zip(gate_grads, up_grads, wg, wu):
            mlp_back = mlp_back + mm_nt(gate_grad, w1) + mm_nt(up_grad, w2)
        middle_grad = grad.astype(f32) + norm_backward(middle, inverse_mlp, mlp_scale, mlp_back)
        middle_bf = middle_grad.astype(bf16)
        if weights_too:
            middle_bf, downs, up_ups = tied(middle_bf, downs, up_ups)
            downs = [scatter_columns(part[0]) for part in downs]
            up_ups = [add_partner(part, high_bits) for part in up_ups]
            out_up = mm_tn(middle_bf, mixed).astype(bf16)
            middle_bf, out_up = tied(middle_bf, out_up)
            out_up = add_partner(split_rows(out_up), near_bits)
        mixed_grad = mm(middle_bf, wo).astype(bf16)
        mixed_grad = mixed_grad.reshape(n, KV_HEADS, copies, HD).transpose(1, 2, 0, 3)
        if extra is not None:
            mixed_grad, extra = tied(mixed_grad, extra)
        dq, dk, dv = attention_backward(queries, keys, values, mixed_grad, lse, offset, single)
        if weights_too:
            dq, dk, dv, gate_ups, out_up = tied(dq, dk, dv, gate_ups, out_up)
            gate_ups = [scatter_columns(part[0]) for part in gate_ups]
            out_up = add_partner(out_up, high_bits)
        dk = own_keys(dk)
        dv = own_keys(dv)
        dq = rotate(dq.astype(f32), cosine, -sine)
        dq = dq.transpose(2, 0, 1, 3).reshape(n, HEADS * HD).astype(bf16)
        dk = rotate(dk, cosine, -sine).transpose(1, 0, 2).reshape(n, dims)
        dkv = jnp.concatenate([dk, dv.transpose(1, 0, 2).reshape(n, dims)], axis=1).astype(bf16)
        if not weights_too:
            outgoing = []
            for chunk in token_chunks(4):
                attn_back = mm_nt(dq[chunk], wq) + mm_nt(dkv[chunk], wkv)
                branch = norm_backward(rows[chunk], inverse[chunk], attn_scale, attn_back)
                outgoing.append((middle_grad[chunk] + branch).astype(bf16))
            return outgoing, extra
        kv_up = mm_tn(normed, dkv).astype(bf16)
        dq, dkv, kv_up = tied(dq, dkv, kv_up)
        query_up = mm_tn(normed, dq).astype(bf16)
        dq, dkv, query_up = tied(dq, dkv, query_up)
        attn_back = mm_nt(dq, wq) + mm_nt(dkv, wkv)
        outgoing = middle_grad + norm_backward(rows, inverse, attn_scale, attn_back)
        all_bits = low_bits + high_bits
        kv = scatter_columns(add_partner(split_rows(kv_up), all_bits)[0])
        query = scatter_columns(add_partner(split_rows(query_up), all_bits)[0])
        up_ups = [scatter_columns(part[0]) for part in up_ups]
        out = scatter_columns(out_up[0])
        gains = jnp.stack(
            [gain_sum(rows, inverse, attn_back), gain_sum(middle, inverse_mlp, mlp_back)]
        )
        sums = [jnp.concatenate(parts, axis=1) for parts in (downs, gate_ups, up_ups)]
        return outgoing.astype(bf16), sums + [out, query, kv], gains

    def to_places(rows):
        return exchange(reorder(rows, 1).reshape(micro, nloc, width))[None]

    kept, _ = forward(rows_in)
    hiddens, far_down = tied(kept[13][:1], far_down)
    kept = kept[:13] + (hiddens + kept[13][1:],)
    wd = [spread_near(part) for part in far_down]
    received = jnp.concatenate(
        [shifted(layer_output(kept, chunk), "section", 1) for chunk in token_chunks(4)], axis=0
    )
    received, late_cotangent = tied(received, cotangent)
    half_cot = exchange_half(late_cotangent)
    kept, cot = forward(jnp.where(first_section, rows_in, received), join_halves(half_cot))
    second_out = layer_output(kept, slice(0, n))
    first_grad, outputs = backward(cot, kept, False, to_places(second_out))
    returned = jnp.concatenate([shifted(part, "section", -1) for part in first_grad], axis=0)
    second_grad, sums, gains = backward(jnp.where(first_section, returned, cot), kept, True)
    input_grads = to_places(second_grad)
    down, gate, up, out, query, kv = sums
    kv = lax.all_gather(kv, "tensor", axis=0).transpose(1, 0, 2).reshape(share, 2 * dims)
    gains = reorder(gains, 1)
    for axis, size in (("dp", dsize), ("tensor", tsize)):
        for bit in bits_of(size):
            gains = gains + swapped(gains, axis, bit)
    return (
        outputs,
        input_grads,
        gains[:1],
        query.astype(f32)[None],
        kv[:, :dims].astype(f32)[None],
        kv[:, dims:].astype(f32)[None],
        out.astype(f32).T[None],
        gains[1:],
        gate.astype(f32)[None],
        up.astype(f32)[None],
        down.astype(f32).T[None],
    )


def solution(mesh):
    in_specs = (
        P(None, ("dp", "tensor"), None),
        P(None, ("dp", "tensor"), None),
        P("section", None),
        P("section", "dp", "tensor"),
        P("section", "dp", None),
        P("section", "dp", None),
        P("section", "tensor", "dp"),
        P("section", None),
        P("section", "dp", "tensor"),
        P("section", "dp", "tensor"),
        P("section", "tensor", "dp"),
    )
    out_specs = (
        P("section", None, ("dp", "tensor"), None),
        P("section", None, ("dp", "tensor"), None),
        P("section", None),
        P("section", "dp", "tensor"),
        P("section", "dp", None),
        P("section", "dp", None),
        P("section", "tensor", "dp"),
        P("section", None),
        P("section", "dp", "tensor"),
        P("section", "dp", "tensor"),
        P("section", "tensor", "dp"),
    )
    return jax.shard_map(local, mesh=mesh, in_specs=in_specs, out_specs=out_specs, check_vma=False)
```

```python
import functools

import jax
import jax.numpy as jnp
from jax import lax
from jax.experimental import pallas as pl
from jax.experimental.pallas import tpu as pltpu
from jax.sharding import PartitionSpec as P

HEADS = 16
KV_HEADS = 8
HD = 96
L = 1024

epsilon = 1e-05
rope_base = 100000.0
bf16 = jnp.bfloat16
f32 = jnp.float32


def shifted(array, axis, by):
    size = lax.axis_size(axis)
    pairs = [(i, i + by) for i in range(size) if 0 <= i + by < size]
    return lax.ppermute(array, axis, pairs)


def swapped(array, axis, bit):
    return lax.ppermute(array, axis, [(i, i ^ bit) for i in range(lax.axis_size(axis))])


def bits_of(size):
    return [1 << k for k in range(size.bit_length() - 1)]


def rotate(values, cosine, sine):
    half = values.shape[-1] // 2
    first = values[..., :half]
    second = values[..., half:]
    return jnp.concatenate(
        [first * cosine - second * sine, second * cosine + first * sine], axis=-1
    )


def mm(left, right):
    return jnp.dot(left, right, preferred_element_type=f32)


def mm_nt(left, right):
    return lax.dot_general(
        left, right, (((1,), (1,)), ((), ())), preferred_element_type=f32
    )


def mm_tn(left, right):
    return lax.dot_general(
        left, right, (((0,), (0,)), ((), ())), preferred_element_type=f32
    )


def norm_forward(rows, gain):
    inverse = lax.rsqrt(jnp.mean(rows * rows, axis=-1, keepdims=True) + epsilon)
    return (rows * inverse * gain, inverse)


def norm_backward(rows, inverse, gain, grad):
    scaled = grad * gain
    mean_term = jnp.mean(scaled * rows, axis=-1, keepdims=True)
    return scaled * inverse - rows * inverse * inverse * inverse * mean_term


def gain_sum(rows, inverse, grad):
    return jnp.sum(grad * rows * inverse, axis=0)


QB = 256
LOG2E = 1.4426950408889634


def score_parts(offset_ref, k_ref, q, i, size, single):
    cols = q.shape[0]
    first = i * size if single else 0
    count = size if single else k_ref.shape[1]
    parts = []
    if first:
        parts.append((0, first, mm_nt(k_ref[0, :first], q)))
    diagonal = mm_nt(k_ref[0, first : first + count], q)
    key_at = first + lax.broadcasted_iota(jnp.int32, (count, cols), 0)
    query_at = i * size + lax.rem(lax.broadcasted_iota(jnp.int32, (count, cols), 1), size)
    if not single:
        query_at = query_at + offset_ref[0]
    diagonal = jnp.where(key_at <= query_at, diagonal, -1e30)
    parts.append((first, count, diagonal))
    return parts


def attend_forward_kernel(offset_ref, q_ref, k_ref, vt_ref, o_ref, lse_ref, *, single):
    copies, n, size_h = q_ref.shape[1:]
    size = min(QB, n)
    factor = HD ** (-0.5) * LOG2E
    for i in range(n // size):
        rows = slice(i * size, (i + 1) * size)
        q = q_ref[0, :, rows, :].reshape(copies * size, size_h)
        parts = score_parts(offset_ref, k_ref, q, i, size, single)
        top = functools.reduce(
            jnp.maximum, [jnp.max(part, axis=0, keepdims=True) for _, _, part in parts]
        )
        total = 0.0
        mixed = 0.0
        for first, count, part in parts:
            weights = jnp.exp2((part - top) * factor)
            total = total + jnp.sum(weights, axis=0, keepdims=True)
            mixed = mixed + mm(vt_ref[0, :, first : first + count], weights.astype(bf16))
        mixed = (mixed * (1.0 / total)).T.astype(bf16)
        o_ref[0, :, rows, :] = mixed.reshape(copies, size, size_h)
        lse_ref[0, i] = top * factor + jnp.log2(total)


def attend_backward_kernel(
    offset_ref, q_ref, k_ref, kt_ref, v_ref, g_ref, lse_ref, dq_ref, dk_ref, dv_ref,
    dk_acc, dv_acc, *, single
):
    copies, n, size_h = q_ref.shape[1:]
    size = min(QB, n)
    scale = HD ** (-0.5)
    factor = scale * LOG2E
    dk_acc[...] = jnp.zeros_like(dk_acc)
    dv_acc[...] = jnp.zeros_like(dv_acc)
    for i in range(n // size):
        rows = slice(i * size, (i + 1) * size)
        q = q_ref[0, :, rows, :].reshape(copies * size, size_h)
        g = g_ref[0, :, rows, :].reshape(copies * size, size_h)
        lse = lse_ref[0, i]
        kept = []
        centre = 0.0
        for first, count, part in score_parts(offset_ref, k_ref, q, i, size, single):
            keys = slice(first, first + count)
            probs = jnp.exp2(part * factor - lse)
            prob_grad = mm_nt(v_ref[0, keys], g)
            dv_acc[keys] += mm(probs.astype(bf16), g)
            centre = centre + jnp.sum(probs * prob_grad, axis=0, keepdims=True)
            kept.append((keys, probs, prob_grad))
        dqt = 0.0
        for keys, probs, prob_grad in kept:
            score_grad = (probs * (prob_grad - centre)).astype(bf16)
            dk_acc[keys] += mm(score_grad, q)
            dqt = dqt + mm(kt_ref[0, :, keys], score_grad)
        dq = (dqt * scale).T.astype(bf16)
        dq_ref[0, :, rows, :] = dq.reshape(copies, size, size_h)
    dk_ref[0] = (dk_acc[...] * scale).astype(dk_ref.dtype)
    dv_ref[0] = dv_acc[...].astype(dv_ref.dtype)


def block_of(shape):
    rest = (0,) * (len(shape) - 1)
    return pl.BlockSpec((1,) + tuple(shape[1:]), lambda h: (h,) + rest)


def attention_forward(queries, keys, values_t, offset, single):
    kv, copies, n, size_h = queries.shape
    size = min(QB, n)
    out_shape = (
        jax.ShapeDtypeStruct(queries.shape, bf16),
        jax.ShapeDtypeStruct((kv, n // size, 1, copies * size), f32),
    )
    operands = (queries, keys, values_t)
    return pl.pallas_call(
        functools.partial(attend_forward_kernel, single=single),
        grid=(kv,),
        in_specs=[pl.BlockSpec(memory_space=pltpu.SMEM)] + [block_of(a.shape) for a in operands],
        out_specs=[block_of(a.shape) for a in out_shape],
        out_shape=out_shape,
        compiler_params=pltpu.CompilerParams(vmem_limit_bytes=40 * 2**20),
        cost_estimate=pl.CostEstimate(
            flops=8 * kv * copies * n * L * HD,
            bytes_accessed=8 * kv * n * 128 * copies,
            transcendentals=kv * copies * n * L,
        ),
        name="attend_forward",
    )(offset, *operands)


def attention_backward(queries, keys, values, mixed_grad, lse, offset, single):
    kv, copies, n, size_h = queries.shape
    count = keys.shape[1]
    out_shape = (
        jax.ShapeDtypeStruct(queries.shape, bf16),
        jax.ShapeDtypeStruct(keys.shape, bf16),
        jax.ShapeDtypeStruct(keys.shape, bf16),
    )
    operands = (queries, keys, keys.transpose(0, 2, 1), values, mixed_grad, lse)
    return pl.pallas_call(
        functools.partial(attend_backward_kernel, single=single),
        grid=(kv,),
        in_specs=[pl.BlockSpec(memory_space=pltpu.SMEM)] + [block_of(a.shape) for a in operands],
        out_specs=[block_of(a.shape) for a in out_shape],
        out_shape=out_shape,
        scratch_shapes=[pltpu.VMEM((count, size_h), f32), pltpu.VMEM((count, size_h), f32)],
        compiler_params=pltpu.CompilerParams(vmem_limit_bytes=40 * 2**20),
        cost_estimate=pl.CostEstimate(
            flops=20 * kv * copies * n * L * HD,
            bytes_accessed=16 * kv * n * 128 * copies,
            transcendentals=kv * copies * n * L,
        ),
        name="attend_backward",
    )(offset, *operands)


def local(
    inputs, cotangent, attn_gain, w_query, w_key, w_value, w_out, mlp_gain, w_gate, w_up, w_down
):
    micro, nloc, width = inputs.shape
    tsize = lax.axis_size("tensor")
    dsize = lax.axis_size("dp")
    ranks = tsize // micro
    n = nloc * micro
    share = width // dsize
    first_section = lax.axis_index("section") == 0
    t = lax.axis_index("tensor")
    d = lax.axis_index("dp")
    seq = t % micro
    seg = t // micro
    copies = HEADS // KV_HEADS
    dims = KV_HEADS * HD
    low_bits = bits_of(dsize)[:1]
    high_bits = bits_of(dsize)[1:]
    same_seq = [[g + micro * r for r in range(ranks)] for g in range(micro)]

    def exchange(blocks):
        out = blocks
        for j in range(1, micro):
            sent = lax.dynamic_index_in_dim(blocks, seq ^ j, 0, keepdims=True)
            got = swapped(sent, "tensor", j)
            out = lax.dynamic_update_slice_in_dim(out, got, seq ^ j, 0)
        return out

    def reorder(array, axis):
        return jnp.concatenate(
            [lax.dynamic_slice_in_dim(array, (d ^ m) * share, share, axis) for m in range(dsize)],
            axis=axis,
        )

    def swap_in(parts, bit):
        parts = dict(parts)
        for m in sorted(parts):
            parts[m ^ bit] = swapped(parts[m], "dp", bit)
        return parts

    def spread_far(block):
        parts = {0: block}
        for bit in reversed(high_bits):
            parts = swap_in(parts, bit)
        return parts

    def spread_near(parts):
        for bit in low_bits:
            parts = swap_in(parts, bit)
        return jnp.concatenate([parts[m] for m in range(dsize)], axis=0)

    def gather_columns(shard):
        whole = lax.all_gather(shard, "tensor", axis=0)
        return whole.transpose(1, 0, 2).reshape(share, tsize * shard.shape[1])

    def tied(*arrays):
        return lax.optimization_barrier(arrays)

    def exchange_half(array):
        side = lax.axis_index("section")
        return exchange(lax.dynamic_slice_in_dim(array, side * (width // 2), width // 2, 2))

    def join_halves(mine):
        other = swapped(mine, "section", 1)
        whole = jnp.concatenate(
            [jnp.where(first_section, mine, other), jnp.where(first_section, other, mine)], axis=2
        )
        return reorder(whole.reshape(n, width), 1)

    def split_rows(grad):
        return {m: grad[m * share : (m + 1) * share].astype(bf16) for m in range(dsize)}

    def add_partner(parts, bits):
        for bit in bits:
            summed = {}
            for m in sorted(parts):
                if not m & bit:
                    got = swapped(parts[m ^ bit], "dp", bit)
                    summed[m] = (parts[m].astype(f32) + got.astype(f32)).astype(bf16)
            parts = summed
        return parts

    def scatter_columns(part):
        part = part.reshape(share, tsize, -1).transpose(1, 0, 2)
        return lax.psum_scatter(part, "tensor", scatter_dimension=0)

    attn_scale = reorder(attn_gain[0], 0)
    mlp_scale = reorder(mlp_gain[0], 0)
    mine = exchange_half(inputs)
    last = spread_far(jnp.concatenate([w_key[0], w_value[0]], axis=1))
    mine, last = tied(mine, last)
    wkv = spread_near(last)
    rows_in = join_halves(mine)

    def spread_weight(shard, pieces, last):
        rows = share // pieces
        fars = []
        for i in range(pieces):
            whole = lax.all_gather(shard[i * rows : (i + 1) * rows], "tensor", axis=0)
            whole, last = tied(whole, last)
            if fars:
                fars[-1] = last
            whole = whole.transpose(1, 0, 2).reshape(rows, tsize * shard.shape[1])
            last = spread_far(whole)
            fars.append(last)
        return fars, last

    def settle(fars):
        parts = [dict(far) for far in fars]
        for bit in low_bits:
            parts = [swap_in(part, bit) for part in parts]
        return jnp.concatenate([part[m] for m in range(dsize) for part in parts], axis=0)

    fars, last = spread_weight(w_query[0], 1, last)
    wq = settle(fars)
    fars, last = spread_weight(w_out[0].T, 1, last)
    wo = settle(fars)
    fars, last = spread_weight(w_gate[0], 2, last)
    wg = settle(fars)
    fars, last = spread_weight(w_up[0], 2, last)
    wu = settle(fars)
    far_down, last = spread_weight(w_down[0].T, 2, last)

    places = seg * n + jnp.arange(n)
    half = HD // 2
    freqs = rope_base ** (-jnp.arange(half, dtype=f32) / half)
    angles = places.astype(f32)[:, None] * freqs[None, :]
    cosine = jnp.cos(angles)
    sine = jnp.sin(angles)
    single = ranks == 1
    offset = (seg * n).astype(jnp.int32).reshape(1)

    def all_keys(array):
        if single:
            return array
        return lax.all_gather(
            array, "tensor", axis=1, tiled=True, axis_index_groups=same_seq
        )

    def own_keys(array):
        if single:
            return array.astype(f32)
        return lax.psum_scatter(
            array,
            "tensor",
            scatter_dimension=1,
            tiled=True,
            axis_index_groups=same_seq,
        ).astype(f32)

    def token_chunks(count):
        step = n // count
        return [slice(i * step, (i + 1) * step) for i in range(count)]

    def forward(rows_bf, extra=None):
        rows = rows_bf.astype(f32)
        normed, inverse = norm_forward(rows, attn_scale)
        normed = normed.astype(bf16)
        queries = mm(normed, wq).reshape(n, KV_HEADS, copies, HD).transpose(1, 2, 0, 3)
        queries = rotate(queries, cosine, sine).astype(bf16)
        both = mm(normed, wkv)
        keys = both[:, :dims].reshape(n, KV_HEADS, HD).transpose(1, 0, 2)
        keys = all_keys(rotate(keys, cosine, sine).astype(bf16))
        values = both[:, dims:].reshape(n, KV_HEADS, HD).transpose(1, 0, 2)
        values = all_keys(values.astype(bf16))
        mixed, lse = attention_forward(queries, keys, values.transpose(0, 2, 1), offset, single)
        mixed = mixed.transpose(2, 0, 1, 3).reshape(n, HEADS * HD)
        if extra is not None:
            mixed, extra = tied(mixed, extra)
        middle = rows + mm_nt(mixed, wo)
        normed_mlp, inverse_mlp = norm_forward(middle, mlp_scale)
        normed_mlp = normed_mlp.astype(bf16)
        gate = mm(normed_mlp, wg)
        upward = mm(normed_mlp, wu)
        hidden = (jax.nn.silu(gate) * upward).astype(bf16)
        kept = (
            rows_bf, inverse, normed, queries, keys, values, lse, mixed,
            middle, inverse_mlp, normed_mlp, gate.astype(bf16), upward.astype(bf16), hidden,
        )
        return kept, extra

    def layer_output(kept, chunk):
        middle, hidden = kept[8], kept[13]
        return (middle[chunk] + mm_nt(hidden[chunk], wd)).astype(bf16)

    def backward(grad, kept, weights_too, extra=None):
        (
            rows_bf, inverse, normed, queries, keys, values, lse, mixed,
            middle, inverse_mlp, normed_mlp, gate, upward, hidden,
        ) = kept
        rows = rows_bf.astype(f32)
        if weights_too:
            down = mm_tn(grad, hidden).astype(bf16)
            grad, down = tied(grad, down)
            down = add_partner(split_rows(down), low_bits)
        gate = gate.astype(f32)
        hidden_grad = mm(grad, wd)
        sigma = jax.nn.sigmoid(gate)
        gate_grad = (
            hidden_grad * upward.astype(f32) * (sigma * (1.0 + gate * (1.0 - sigma)))
        ).astype(bf16)
        up_grad = (hidden_grad * gate * sigma).astype(bf16)
        if weights_too:
            gate_grad, up_grad, down = tied(gate_grad, up_grad, down)
            down = add_partner(down, high_bits)
            gate_sum = mm_tn(normed_mlp, gate_grad).astype(bf16)
            gate_grad, up_grad, gate_sum = tied(gate_grad, up_grad, gate_sum)
            gate_sum = add_partner(split_rows(gate_sum), low_bits)
            up_sum = mm_tn(normed_mlp, up_grad).astype(bf16)
            gate_grad, up_grad, up_sum = tied(gate_grad, up_grad, up_sum)
            up_sum = add_partner(split_rows(up_sum), low_bits)
        mlp_back = mm_nt(gate_grad, wg)
        if weights_too:
            mlp_back, down, gate_sum = tied(mlp_back, down, gate_sum)
            gate_sum = add_partner(gate_sum, high_bits)
        mlp_back = mlp_back + mm_nt(up_grad, wu)
        middle_grad = grad.astype(f32) + norm_backward(middle, inverse_mlp, mlp_scale, mlp_back)
        middle_bf = middle_grad.astype(bf16)
        if weights_too:
            down = scatter_columns(down[0])
            out = mm_tn(middle_bf, mixed).astype(bf16)
            middle_bf, out, up_sum = tied(middle_bf, out, up_sum)
            out = add_partner(split_rows(out), low_bits)
        mixed_grad = mm(middle_bf, wo).astype(bf16)
        mixed_grad = mixed_grad.reshape(n, KV_HEADS, copies, HD).transpose(1, 2, 0, 3)
        if extra is not None:
            mixed_grad, extra = tied(mixed_grad, extra)
        if weights_too:
            mixed_grad, gate_sum, out = tied(mixed_grad, gate_sum, out)
            gate_sum = scatter_columns(gate_sum[0])
            up_sum = add_partner(up_sum, high_bits)
        dq, dk, dv = attention_backward(queries, keys, values, mixed_grad, lse, offset, single)
        dk = own_keys(dk)
        dv = own_keys(dv)
        dq = rotate(dq.astype(f32), cosine, -sine)
        dq = dq.transpose(2, 0, 1, 3).reshape(n, HEADS * HD).astype(bf16)
        dk = rotate(dk, cosine, -sine).transpose(1, 0, 2).reshape(n, dims)
        dkv = jnp.concatenate([dk, dv.transpose(1, 0, 2).reshape(n, dims)], axis=1).astype(bf16)
        if not weights_too:
            outgoing = []
            for chunk in token_chunks(4):
                attn_back = mm_nt(dq[chunk], wq) + mm_nt(dkv[chunk], wkv)
                branch = norm_backward(rows[chunk], inverse[chunk], attn_scale, attn_back)
                outgoing.append((middle_grad[chunk] + branch).astype(bf16))
            return outgoing, extra
        kv = mm_tn(normed, dkv).astype(bf16)
        query = mm_tn(normed, dq).astype(bf16)
        dq, dkv, kv, query, down, up_sum = tied(dq, dkv, kv, query, down, up_sum)
        up_sum = scatter_columns(up_sum[0])
        kv = add_partner(split_rows(kv), low_bits)
        query = add_partner(split_rows(query), low_bits)
        attn_back = mm_nt(dq, wq) + mm_nt(dkv, wkv)
        outgoing = middle_grad + norm_backward(rows, inverse, attn_scale, attn_back)
        outgoing = outgoing.astype(bf16)
        outgoing, kv, query = tied(outgoing, kv, query)
        kv = add_partner(kv, high_bits)[0]
        out = add_partner(out, high_bits)[0]
        query = add_partner(query, high_bits)[0]
        pair = jnp.concatenate(
            [out.reshape(share, tsize, -1), query.reshape(share, tsize, -1)], axis=2
        )
        pair, gate_sum = tied(pair, gate_sum)
        pair = scatter_columns(pair)
        gains = jnp.stack(
            [gain_sum(rows, inverse, attn_back), gain_sum(middle, inverse_mlp, mlp_back)]
        )
        half_cols = pair.shape[1] // 2
        sums = [down, gate_sum, up_sum, pair[:, :half_cols], pair[:, half_cols:]]
        return outgoing, sums + [sum_over_tensor(kv)], gains

    def sum_over_tensor(array):
        bits = bits_of(tsize)
        for bit in bits:
            side = (t & bit) != 0
            size = array.shape[1] // 2
            low, high = array[:, :size], array[:, size:]
            got = swapped(jnp.where(side, low, high), "tensor", bit)
            kept_half = jnp.where(side, high, low)
            array = (kept_half.astype(f32) + got.astype(f32)).astype(bf16)
        for bit in reversed(bits):
            side = (t & bit) != 0
            got = swapped(array, "tensor", bit)
            array = jnp.concatenate(
                [jnp.where(side, got, array), jnp.where(side, array, got)], axis=1
            )
        return array

    def to_places(rows):
        return exchange(reorder(rows, 1).reshape(micro, nloc, width))[None]

    kept, _ = forward(rows_in)
    far_down[-1], hidden = tied(far_down[-1], kept[13])
    kept = kept[:13] + (hidden,)
    wd = settle(far_down)
    received = jnp.concatenate(
        [shifted(layer_output(kept, chunk), "section", 1) for chunk in token_chunks(4)], axis=0
    )
    received, late_cotangent = tied(received, cotangent)
    half_cot = exchange_half(late_cotangent)
    kept, cot = forward(jnp.where(first_section, rows_in, received), join_halves(half_cot))
    second_out = layer_output(kept, slice(0, n))
    first_grad, outputs = backward(cot, kept, False, to_places(second_out))
    returned = jnp.concatenate([shifted(part, "section", -1) for part in first_grad], axis=0)
    second_grad, sums, gains = backward(jnp.where(first_section, returned, cot), kept, True)
    input_grads = to_places(second_grad)
    down, gate, up, out, query, kv = sums
    gains = reorder(gains, 1)
    for axis, size in (("dp", dsize), ("tensor", tsize)):
        for bit in bits_of(size):
            gains = gains + swapped(gains, axis, bit)
    return (
        outputs,
        input_grads,
        gains[:1],
        query.astype(f32)[None],
        kv[:, :dims].astype(f32)[None],
        kv[:, dims:].astype(f32)[None],
        out.astype(f32).T[None],
        gains[1:],
        gate.astype(f32)[None],
        up.astype(f32)[None],
        down.astype(f32).T[None],
    )


def solution(mesh):
    in_specs = (
        P(None, ("dp", "tensor"), None),
        P(None, ("dp", "tensor"), None),
        P("section", None),
        P("section", "dp", "tensor"),
        P("section", "dp", None),
        P("section", "dp", None),
        P("section", "tensor", "dp"),
        P("section", None),
        P("section", "dp", "tensor"),
        P("section", "dp", "tensor"),
        P("section", "tensor", "dp"),
    )
    out_specs = (
        P("section", None, ("dp", "tensor"), None),
        P("section", None, ("dp", "tensor"), None),
        P("section", None),
        P("section", "dp", "tensor"),
        P("section", "dp", None),
        P("section", "dp", None),
        P("section", "tensor", "dp"),
        P("section", None),
        P("section", "dp", "tensor"),
        P("section", "dp", "tensor"),
        P("section", "tensor", "dp"),
    )
    return jax.shard_map(local, mesh=mesh, in_specs=in_specs, out_specs=out_specs, check_vma=False)
```

```python
import functools

import jax
import jax.numpy as jnp
from jax import lax
from jax.experimental import pallas as pl
from jax.experimental.pallas import tpu as pltpu
from jax.sharding import PartitionSpec as P

HEADS = 16
KV_HEADS = 8
HD = 96
L = 1024

epsilon = 1e-05
rope_base = 100000.0
bf16 = jnp.bfloat16
f32 = jnp.float32


def shifted(array, axis, by):
    size = lax.axis_size(axis)
    pairs = [(i, i + by) for i in range(size) if 0 <= i + by < size]
    return lax.ppermute(array, axis, pairs)


def swapped(array, axis, bit):
    return lax.ppermute(array, axis, [(i, i ^ bit) for i in range(lax.axis_size(axis))])


def bits_of(size):
    return [1 << k for k in range(size.bit_length() - 1)]


def mm(left, right):
    return jnp.dot(left, right, preferred_element_type=f32)


def mm_nt(left, right):
    return lax.dot_general(
        left, right, (((1,), (1,)), ((), ())), preferred_element_type=f32
    )


def mm_tn(left, right):
    return lax.dot_general(
        left, right, (((0,), (0,)), ((), ())), preferred_element_type=f32
    )


QB = 256
HP = 128
LOG2E = 1.4426950408889634
MIB = 2**20


def whole(shape):
    rest = (0,) * len(shape)
    return pl.BlockSpec(tuple(shape), lambda *_: rest, pipeline_mode=pl.Buffered(1))


def rows_of(shape, first=0):
    return pl.BlockSpec(tuple(shape), lambda i: (first + i, 0))


def columns_of(shape, first=0):
    return pl.BlockSpec(tuple(shape), lambda i: (0, first + i))


def kernel_call(kernel, grid, in_specs, out_specs, out_shape, flops, name, scratch=(), trans=0):
    moved = sum(2 * shape.size for shape in out_shape)
    return pl.pallas_call(
        kernel,
        grid=grid,
        in_specs=in_specs,
        out_specs=out_specs,
        out_shape=out_shape,
        scratch_shapes=scratch,
        compiler_params=pltpu.CompilerParams(vmem_limit_bytes=56 * MIB),
        cost_estimate=pl.CostEstimate(
            flops=int(flops), bytes_accessed=int(moved + flops // 512), transcendentals=int(trans)
        ),
        name=name,
    )


def turned(values, cosine, sine):
    parts = []
    for at in range(0, values.shape[1], HP):
        head = values[:, at : at + HP]
        parts.append(head * cosine + pltpu.roll(head, HP // 2, 1) * sine)
    return parts[0] if len(parts) == 1 else jnp.concatenate(parts, axis=1)


def project_kernel(h_ref, gain_ref, w_ref, cos_ref, sin_ref, out_ref, normed_ref, *, turning):
    step = pl.program_id(0)

    @pl.when(step == 0)
    def _():
        rows = h_ref[...].astype(f32)
        inverse = lax.rsqrt(jnp.mean(rows * rows, axis=-1, keepdims=True) + epsilon)
        normed_ref[...] = (rows * inverse * gain_ref[...]).astype(bf16)

    values = mm(normed_ref[...], w_ref[...])

    @pl.when(step < turning)
    def _():
        out_ref[...] = turned(values, cos_ref[...], sin_ref[...]).astype(bf16)

    @pl.when(step >= turning)
    def _():
        out_ref[...] = values.astype(bf16)


def project(h, gain, w, cosine, sine, turned_columns):
    n, width = h.shape
    total = w.shape[1]
    block = 512
    out_shape = (
        jax.ShapeDtypeStruct((n, total), bf16),
        jax.ShapeDtypeStruct((n, width), bf16),
    )
    return kernel_call(
        functools.partial(project_kernel, turning=turned_columns // block),
        (total // block,),
        [
            whole(h.shape), whole(gain.shape), columns_of((width, block)),
            whole(cosine.shape), whole(sine.shape),
        ],
        [columns_of((n, block)), whole((n, width))],
        out_shape,
        2 * n * width * total,
        "project",
    )(h, gain, w, cosine, sine)


def join_kernel(mixed_ref, h_ref, w_ref, gain_ref, middle_ref, normed_ref):
    middle = h_ref[...].astype(f32) + mm_nt(mixed_ref[...], w_ref[...])
    middle_ref[...] = middle
    inverse = lax.rsqrt(jnp.mean(middle * middle, axis=-1, keepdims=True) + epsilon)
    normed_ref[...] = (middle * inverse * gain_ref[...]).astype(bf16)


def join(mixed, h, w, gain):
    n, width = h.shape
    block = min(QB, n)
    out_shape = (
        jax.ShapeDtypeStruct((n, width), f32),
        jax.ShapeDtypeStruct((n, width), bf16),
    )
    return kernel_call(
        join_kernel,
        (n // block,),
        [
            rows_of((block, mixed.shape[1])), rows_of((block, width)),
            whole(w.shape), whole(gain.shape),
        ],
        [rows_of((block, width))] * 2,
        out_shape,
        2 * n * width * mixed.shape[1],
        "join",
    )(mixed, h, w, gain)


def gate_up_kernel(x_ref, wg_ref, wu_ref, gate_ref, up_ref, hidden_ref):
    x = x_ref[...]
    gate = mm(x, wg_ref[...])
    upward = mm(x, wu_ref[...])
    gate_ref[...] = gate.astype(bf16)
    up_ref[...] = upward.astype(bf16)
    hidden_ref[...] = (gate * jax.nn.sigmoid(gate) * upward).astype(bf16)


def gate_up(x, wg, wu):
    n, width = x.shape
    total = wg.shape[1]
    block = 512
    return kernel_call(
        gate_up_kernel,
        (total // block,),
        [whole(x.shape), columns_of((width, block)), columns_of((width, block))],
        [columns_of((n, block))] * 3,
        (jax.ShapeDtypeStruct((n, total), bf16),) * 3,
        4 * n * width * total,
        "gate_up",
        trans=n * total,
    )(x, wg, wu)


def down_kernel(hidden_ref, middle_ref, w_ref, out_ref):
    out_ref[...] = (middle_ref[...] + mm_nt(hidden_ref[...], w_ref[...])).astype(bf16)


def down_rows(hidden, middle, w, first, count):
    n, width = middle.shape
    block = min(QB, n)
    return kernel_call(
        down_kernel,
        (count,),
        [
            rows_of((block, hidden.shape[1]), first), rows_of((block, width), first),
            whole(w.shape),
        ],
        [rows_of((block, width))],
        (jax.ShapeDtypeStruct((count * block, width), bf16),),
        2 * count * block * width * hidden.shape[1],
        "down_rows",
    )(hidden, middle, w)[0]


def feed_back_kernel(
    grad_ref, gate_ref, up_ref, wd_ref, wg_ref, wu_ref, middle_ref, gain_ref,
    total_ref, low_ref, sum_ref, *grad_refs
):
    step = pl.program_id(0)
    gate = gate_ref[...].astype(f32)
    hidden_grad = mm(grad_ref[...], wd_ref[...])
    sigma = jax.nn.sigmoid(gate)
    gate_grad = hidden_grad * up_ref[...].astype(f32) * (sigma * (1.0 + gate * (1.0 - sigma)))
    gate_grad = gate_grad.astype(bf16)
    up_grad = (hidden_grad * gate * sigma).astype(bf16)
    for ref, value in zip(grad_refs, (gate_grad, up_grad)):
        ref[...] = value
    part = mm_nt(gate_grad, wg_ref[...]) + mm_nt(up_grad, wu_ref[...])

    @pl.when(step == 0)
    def _():
        total_ref[...] = part

    @pl.when(step > 0)
    def _():
        total_ref[...] += part

    @pl.when(step == pl.num_programs(0) - 1)
    def _():
        n = total_ref.shape[0]
        size = min(QB, n)
        sums = 0.0
        for at in range(0, n, size):
            rows = slice(at, at + size)
            middle = middle_ref[rows]
            back = total_ref[rows]
            inverse = lax.rsqrt(jnp.mean(middle * middle, axis=-1, keepdims=True) + epsilon)
            sums = sums + jnp.sum(back * middle * inverse, axis=0, keepdims=True)
            scaled = back * gain_ref[...]
            mean_term = jnp.mean(scaled * middle, axis=-1, keepdims=True)
            branch = scaled * inverse - middle * (inverse * inverse * inverse * mean_term)
            result = grad_ref[rows].astype(f32) + branch
            total_ref[rows] = result
            low_ref[rows] = result.astype(bf16)
        sum_ref[...] = sums


def feed_back(grad, gate, upward, wd, wg, wu, middle, gain, with_grads):
    n, width = grad.shape
    total = wg.shape[1]
    block = 512
    out_shape = (
        jax.ShapeDtypeStruct((n, width), f32),
        jax.ShapeDtypeStruct((n, width), bf16),
        jax.ShapeDtypeStruct((1, width), f32),
    )
    out_specs = [whole((n, width)), whole((n, width)), whole((1, width))]
    if with_grads:
        out_shape += (jax.ShapeDtypeStruct((n, total), bf16),) * 2
        out_specs += [columns_of((n, block))] * 2
    return kernel_call(
        feed_back_kernel,
        (total // block,),
        [
            whole(grad.shape), columns_of((n, block)), columns_of((n, block)),
            columns_of((width, block)), columns_of((width, block)), columns_of((width, block)),
            whole(middle.shape), whole(gain.shape),
        ],
        out_specs,
        out_shape,
        6 * n * width * total,
        "feed_back",
        trans=n * total,
    )(grad, gate, upward, wd, wg, wu, middle, gain)


def heads_back_kernel(
    dq_ref, dk_ref, dv_ref, w_ref, h_ref, grad_ref, gain_ref, out_ref, sum_ref
):
    step = pl.program_id(0)
    back = 0.0
    at = 0
    for ref in (dq_ref, dk_ref, dv_ref):
        back = back + mm_nt(ref[...], w_ref[:, at : at + ref.shape[1]])
        at += ref.shape[1]
    rows = h_ref[...].astype(f32)
    inverse = lax.rsqrt(jnp.mean(rows * rows, axis=-1, keepdims=True) + epsilon)
    sums = jnp.sum(back * rows * inverse, axis=0, keepdims=True)
    scaled = back * gain_ref[...]
    mean_term = jnp.mean(scaled * rows, axis=-1, keepdims=True)
    branch = scaled * inverse - rows * (inverse * inverse * inverse * mean_term)
    out_ref[...] = (grad_ref[...] + branch).astype(bf16)

    @pl.when(step == 0)
    def _():
        sum_ref[...] = sums

    @pl.when(step > 0)
    def _():
        sum_ref[...] += sums


def heads_back(dq, dk, dv, w, h, grad, gain, first, count):
    n, width = h.shape
    block = min(QB, n)
    out_shape = (
        jax.ShapeDtypeStruct((count * block, width), bf16),
        jax.ShapeDtypeStruct((1, width), f32),
    )
    return kernel_call(
        heads_back_kernel,
        (count,),
        [rows_of((block, a.shape[1]), first) for a in (dq, dk, dv)]
        + [
            whole(w.shape), rows_of((block, width), first), rows_of((block, width), first),
            whole(gain.shape),
        ],
        [rows_of((block, width)), whole((1, width))],
        out_shape,
        2 * count * block * width * w.shape[1],
        "heads_back",
    )(dq, dk, dv, w, h, grad, gain)


def two_heads(ref, rows):
    return jnp.concatenate([ref[rows, :HP], ref[rows, HP:]], axis=0)


def score_parts(offset_ref, k_ref, q, i, size, single):
    cols = q.shape[0]
    first = i * size if single else 0
    count = size if single else k_ref.shape[0]
    parts = []
    if first:
        parts.append((0, first, mm_nt(k_ref[:first], q)))
    diagonal = mm_nt(k_ref[first : first + count], q)
    key_at = first + lax.broadcasted_iota(jnp.int32, (count, cols), 0)
    query_at = i * size + lax.rem(lax.broadcasted_iota(jnp.int32, (count, cols), 1), size)
    if not single:
        query_at = query_at + offset_ref[0]
    diagonal = jnp.where(key_at <= query_at, diagonal, -1e30)
    parts.append((first, count, diagonal))
    return parts


def attend_forward_kernel(offset_ref, q_ref, k_ref, v_ref, o_ref, lse_ref, *, single):
    n = q_ref.shape[0]
    size = min(QB, n)
    factor = HD ** (-0.5) * LOG2E
    vt = v_ref[...].T
    for i in range(n // size):
        rows = slice(i * size, (i + 1) * size)
        q = two_heads(q_ref, rows)
        parts = score_parts(offset_ref, k_ref, q, i, size, single)
        top = functools.reduce(
            jnp.maximum, [jnp.max(part, axis=0, keepdims=True) for _, _, part in parts]
        )
        total = 0.0
        mixed = 0.0
        for first, count, part in parts:
            weights = jnp.exp2((part - top) * factor)
            total = total + jnp.sum(weights, axis=0, keepdims=True)
            mixed = mixed + mm(vt[:, first : first + count], weights.astype(bf16))
        mixed = (mixed * (1.0 / total)).T.astype(bf16)
        o_ref[rows, :HP] = mixed[:size]
        o_ref[rows, HP:] = mixed[size:]
        lse_ref[0, i] = top * factor + jnp.log2(total)


def attend_backward_kernel(
    offset_ref, q_ref, k_ref, v_ref, g_ref, lse_ref, cosq_ref, sinq_ref, cosk_ref, sink_ref,
    dq_ref, dk_ref, dv_ref, dk_acc, dv_acc, *, single
):
    n = q_ref.shape[0]
    size = min(QB, n)
    scale = HD ** (-0.5)
    factor = scale * LOG2E
    kt = k_ref[...].T
    dk_acc[...] = jnp.zeros_like(dk_acc)
    dv_acc[...] = jnp.zeros_like(dv_acc)
    for i in range(n // size):
        rows = slice(i * size, (i + 1) * size)
        q = two_heads(q_ref, rows)
        g = two_heads(g_ref, rows)
        lse = lse_ref[0, i]
        kept = []
        centre = 0.0
        for first, count, part in score_parts(offset_ref, k_ref, q, i, size, single):
            keys = slice(first, first + count)
            probs = jnp.exp2(part * factor - lse)
            prob_grad = mm_nt(v_ref[keys], g)
            dv_acc[keys] += mm(probs.astype(bf16), g)
            centre = centre + jnp.sum(probs * prob_grad, axis=0, keepdims=True)
            kept.append((keys, probs, prob_grad))
        dqt = 0.0
        for keys, probs, prob_grad in kept:
            score_grad = (probs * (prob_grad - centre)).astype(bf16)
            dk_acc[keys] += mm(score_grad, q)
            dqt = dqt + mm(kt[:, keys], score_grad)
        dq = (dqt * scale).T
        for c in range(2):
            head = turned(dq[c * size : (c + 1) * size], cosq_ref[rows], sinq_ref[rows])
            dq_ref[rows, c * HP : (c + 1) * HP] = head.astype(bf16)
    dk_ref[...] = turned(dk_acc[...] * scale, cosk_ref[...], sink_ref[...]).astype(bf16)
    dv_ref[...] = dv_acc[...].astype(bf16)


SCALAR = pl.BlockSpec(memory_space=pltpu.SMEM)


def attention_forward(q, k, v, offset, single):
    n = q[0].shape[0]
    size = min(QB, n)
    count = k[0].shape[0]
    out_shape = (
        jax.ShapeDtypeStruct((n, HEADS * HP), bf16),
        jax.ShapeDtypeStruct((KV_HEADS, n // size, 1, 2 * size), f32),
    )
    return kernel_call(
        functools.partial(attend_forward_kernel, single=single),
        (KV_HEADS,),
        [
            SCALAR, columns_of((n, 2 * HP), q[1] // 2), columns_of((count, HP), k[1]),
            columns_of((count, HP), v[1]),
        ],
        [
            columns_of((n, 2 * HP)),
            pl.BlockSpec((1, n // size, 1, 2 * size), lambda h: (h, 0, 0, 0)),
        ],
        out_shape,
        4 * HEADS * n * count * HP,
        "attend_forward",
        trans=HEADS * n * count,
    )(offset, q[0], k[0], v[0])


def attention_backward(q, k, v, mixed_grad, lse, query_tables, key_tables, offset, single):
    n = q[0].shape[0]
    size = min(QB, n)
    count = k[0].shape[0]
    out_shape = (
        jax.ShapeDtypeStruct((n, HEADS * HP), bf16),
        jax.ShapeDtypeStruct((count, KV_HEADS * HP), bf16),
        jax.ShapeDtypeStruct((count, KV_HEADS * HP), bf16),
    )
    return kernel_call(
        functools.partial(attend_backward_kernel, single=single),
        (KV_HEADS,),
        [
            SCALAR, columns_of((n, 2 * HP), q[1] // 2), columns_of((count, HP), k[1]),
            columns_of((count, HP), v[1]), columns_of((n, 2 * HP)),
            pl.BlockSpec((1, n // size, 1, 2 * size), lambda h: (h, 0, 0, 0)),
        ]
        + [whole(table.shape) for table in query_tables + key_tables],
        [columns_of((n, 2 * HP)), columns_of((count, HP)), columns_of((count, HP))],
        out_shape,
        10 * HEADS * n * count * HP,
        "attend_backward",
        scratch=[pltpu.VMEM((count, HP), f32), pltpu.VMEM((count, HP), f32)],
        trans=HEADS * n * count,
    )(offset, q[0], k[0], v[0], mixed_grad, lse, *query_tables, *key_tables)


def padded(array):
    rows = array.shape[0]
    parts = array.reshape(rows, -1, HD // 2)
    parts = jnp.pad(parts, ((0, 0), (0, 0), (0, HP // 2 - HD // 2)))
    return parts.reshape(rows, -1)


def unpadded(array):
    rows = array.shape[0]
    return array.reshape(rows, -1, HP // 2)[:, :, : HD // 2].reshape(rows, -1)


def local(
    inputs, cotangent, attn_gain, w_query, w_key, w_value, w_out, mlp_gain, w_gate, w_up, w_down
):
    micro, nloc, width = inputs.shape
    tsize = lax.axis_size("tensor")
    dsize = lax.axis_size("dp")
    ranks = tsize // micro
    n = nloc * micro
    share = width // dsize
    first_section = lax.axis_index("section") == 0
    t = lax.axis_index("tensor")
    d = lax.axis_index("dp")
    seq = t % micro
    seg = t // micro
    copies = HEADS // KV_HEADS
    dims = KV_HEADS * HD
    low_bits = bits_of(dsize)[:1]
    high_bits = bits_of(dsize)[1:]
    same_seq = [[g + micro * r for r in range(ranks)] for g in range(micro)]

    def exchange(blocks):
        out = blocks
        for j in range(1, micro):
            sent = lax.dynamic_index_in_dim(blocks, seq ^ j, 0, keepdims=True)
            got = swapped(sent, "tensor", j)
            out = lax.dynamic_update_slice_in_dim(out, got, seq ^ j, 0)
        return out

    def reorder(array, axis):
        return jnp.concatenate(
            [lax.dynamic_slice_in_dim(array, (d ^ m) * share, share, axis) for m in range(dsize)],
            axis=axis,
        )

    def swap_in(parts, bit):
        parts = dict(parts)
        for m in sorted(parts):
            parts[m ^ bit] = swapped(parts[m], "dp", bit)
        return parts

    def spread_far(block):
        parts = {0: block}
        for bit in reversed(high_bits):
            parts = swap_in(parts, bit)
        return parts

    def spread_near(parts):
        for bit in low_bits:
            parts = swap_in(parts, bit)
        return jnp.concatenate([parts[m] for m in range(dsize)], axis=0)

    def gather_columns(shard):
        whole = lax.all_gather(shard, "tensor", axis=0)
        return whole.transpose(1, 0, 2).reshape(share, tsize * shard.shape[1])

    def tied(*arrays):
        return lax.optimization_barrier(arrays)

    def exchange_half(array):
        side = lax.axis_index("section")
        return exchange(lax.dynamic_slice_in_dim(array, side * (width // 2), width // 2, 2))

    def join_halves(mine):
        other = swapped(mine, "section", 1)
        whole = jnp.concatenate(
            [jnp.where(first_section, mine, other), jnp.where(first_section, other, mine)], axis=2
        )
        return reorder(whole.reshape(n, width), 1)

    def split_rows(grad):
        return {m: grad[m * share : (m + 1) * share].astype(bf16) for m in range(dsize)}

    def add_partner(parts, bits):
        for bit in bits:
            summed = {}
            for m in sorted(parts):
                if not m & bit:
                    got = swapped(parts[m ^ bit], "dp", bit)
                    summed[m] = (parts[m].astype(f32) + got.astype(f32)).astype(bf16)
            parts = summed
        return parts

    def rows_to_send(array):
        return jnp.concatenate(
            [array[:, m * share : (m + 1) * share] for m in range(dsize) if m & 1], axis=1
        )

    def rows_to_keep(array):
        return jnp.concatenate(
            [array[:, m * share : (m + 1) * share] for m in range(dsize) if not m & 1], axis=1
        )

    def swap_low(array):
        return swapped(array, "dp", 1)

    def add_low(mine, got):
        total = (mine.astype(f32) + got.astype(f32)).astype(bf16)
        return {2 * i: total[i * share : (i + 1) * share] for i in range(dsize // 2)}

    def send_far(parts):
        size = share // 2
        pairs = []
        for i in range(2):
            half = {m: part[i * size : (i + 1) * size] for m, part in parts.items()}
            bit = high_bits[0]
            kept = {m: part for m, part in half.items() if not m & bit}
            pairs.append([kept, {m: swapped(half[m ^ bit], "dp", bit) for m in kept}])
        return pairs

    def receive_far(pair):
        kept, got = pair
        parts = {m: (kept[m].astype(f32) + got[m].astype(f32)).astype(bf16) for m in kept}
        return add_partner(parts, high_bits[1:])[0]

    def scatter_columns(part):
        part = part.reshape(share, tsize, -1).transpose(1, 0, 2)
        return lax.psum_scatter(part, "tensor", scatter_dimension=0)

    attn_scale = reorder(attn_gain[0], 0)
    mlp_scale = reorder(mlp_gain[0], 0)
    mine = exchange_half(inputs)
    last = spread_far(jnp.concatenate([w_key[0], w_value[0]], axis=1))
    mine, last = tied(mine, last)
    wkv = spread_near(last)
    rows_in = join_halves(mine)

    def spread_weight(shard, pieces, last):
        rows = share // pieces
        fars = []
        for i in range(pieces):
            whole = lax.all_gather(shard[i * rows : (i + 1) * rows], "tensor", axis=0)
            whole, last = tied(whole, last)
            if fars:
                fars[-1] = last
            whole = whole.transpose(1, 0, 2).reshape(rows, tsize * shard.shape[1])
            last = spread_far(whole)
            fars.append(last)
        return fars, last

    def settle(fars):
        parts = [dict(far) for far in fars]
        for bit in low_bits:
            parts = [swap_in(part, bit) for part in parts]
        return jnp.concatenate([part[m] for m in range(dsize) for part in parts], axis=0)

    fars, last = spread_weight(w_query[0], 1, last)
    wqkv = jnp.concatenate([padded(settle(fars)), padded(wkv)], axis=1)
    fars, last = spread_weight(w_out[0].T, 1, last)
    wo = padded(settle(fars))
    fars, last = spread_weight(w_gate[0], 2, last)
    wg = settle(fars)
    fars, last = spread_weight(w_up[0], 2, last)
    wu = settle(fars)
    far_down, last = spread_weight(w_down[0].T, 2, last)

    def tables(positions):
        half = HD // 2
        freqs = rope_base ** (-jnp.arange(half, dtype=f32) / half)
        angles = positions.astype(f32)[:, None] * freqs[None, :]
        blank = ((0, 0), (0, HP // 2 - half))
        cosine = jnp.pad(jnp.cos(angles), blank)
        sine = jnp.pad(jnp.sin(angles), blank)
        return (
            jnp.concatenate([cosine, cosine], axis=1),
            jnp.concatenate([-sine, sine], axis=1),
        )

    query_tables = tables(seg * n + jnp.arange(n))
    single = ranks == 1
    offset = (seg * n).astype(jnp.int32).reshape(1)

    back_tables = (query_tables[0], -query_tables[1])
    if single:
        key_tables = back_tables
    else:
        key_tables = tables(jnp.arange(L))
        key_tables = (key_tables[0], -key_tables[1])
    q_lanes = HEADS * HP
    k_lanes = KV_HEADS * HP
    blocks = n // min(QB, n)
    attn_row = attn_scale[None]
    mlp_row = mlp_scale[None]

    def head_arrays(qkv):
        if single:
            return (qkv, 0), (qkv, HEADS), (qkv, HEADS + KV_HEADS)
        both = lax.all_gather(
            qkv[:, q_lanes:], "tensor", axis=0, tiled=True, axis_index_groups=same_seq
        )
        return (qkv, 0), (both, 0), (both, KV_HEADS)

    def own_rows(array):
        if single:
            return array
        return lax.psum_scatter(
            array, "tensor", scatter_dimension=0, tiled=True, axis_index_groups=same_seq
        )

    def forward(h, extra=None):
        qkv, normed = project(h, attn_row, wqkv, *query_tables, q_lanes + k_lanes)
        heads = head_arrays(qkv)
        mixed, lse = attention_forward(*heads, offset, single)
        if extra is not None:
            mixed, extra = tied(mixed, extra)
        middle, normed_mlp = join(mixed, h, wo, mlp_row)
        gate, upward, hidden = gate_up(normed_mlp, wg, wu)
        kept = (h, normed, heads, lse, mixed, middle, normed_mlp, gate, upward, hidden)
        return kept, extra

    def backward(grad, kept, weights_too, extra=None):
        h, normed, heads, lse, mixed, middle, normed_mlp, gate, upward, hidden = kept
        if weights_too:
            odd, even = rows_to_send(grad), rows_to_keep(grad)
            odd = mm_tn(odd, hidden).astype(bf16)
            even, odd = tied(even, odd)
            got = swap_low(odd)
            even = mm_tn(even, hidden).astype(bf16)
            even, grad = tied(even, grad)
            grad, down = tied(grad, add_low(even, got))
            first, second = send_far(down)
            down = receive_far(first)
        middle_grad, middle_bf, mlp_sum, *grads = feed_back(
            grad, gate, upward, wd, wg, wu, middle, mlp_row, weights_too
        )
        if weights_too:
            gate_grad, up_grad = grads
            gate_grad, up_grad, down, second[0] = tied(gate_grad, up_grad, down, second[0])
            down = [down, receive_far(second)]
            odd = mm_tn(rows_to_send(normed_mlp), gate_grad).astype(bf16)
            gate_grad, odd = tied(gate_grad, odd)
            got = swap_low(odd)
            even = mm_tn(rows_to_keep(normed_mlp), gate_grad).astype(bf16)
            even, up_grad = tied(even, up_grad)
            up_grad, gate_sum, down[1] = tied(up_grad, add_low(even, got), down[1])
            down = scatter_columns(jnp.concatenate(down, axis=0))
            first, second = send_far(gate_sum)
            gate_sum = receive_far(first)
            up_sum = mm_tn(normed_mlp, up_grad).astype(bf16)
            middle_bf, up_sum, gate_sum, second[0] = tied(middle_bf, up_sum, gate_sum, second[0])
            gate_sum = [gate_sum, receive_far(second)]
            up_sum = add_partner(split_rows(up_sum), low_bits)
            out = unpadded(mm_tn(middle_bf, mixed).astype(bf16))
            middle_bf, out = tied(middle_bf, out)
            out = add_partner(split_rows(out), low_bits)
        mixed_grad = mm(middle_bf, wo).astype(bf16)
        if extra is not None:
            mixed_grad, extra = tied(mixed_grad, extra)
        if weights_too:
            mixed_grad, gate_sum[1], up_sum, out = tied(mixed_grad, gate_sum[1], up_sum, out)
            gate_sum = scatter_columns(jnp.concatenate(gate_sum, axis=0))
            first, second = send_far(up_sum)
            up_sum = receive_far(first)
        dq, dk, dv = attention_backward(
            *heads, mixed_grad, lse, back_tables, key_tables, offset, single
        )
        dk = own_rows(dk)
        dv = own_rows(dv)
        if not weights_too:
            outgoing = [
                heads_back(dq, dk, dv, wqkv, h, middle_grad, attn_row, i, 1)[0]
                for i in range(blocks)
            ]
            return outgoing, extra
        dq, dk, dv, down, up_sum, second[0] = tied(dq, dk, dv, down, up_sum, second[0])
        up_sum = [up_sum, receive_far(second)]
        kv = jnp.concatenate(
            [unpadded(mm_tn(normed, dk).astype(bf16)), unpadded(mm_tn(normed, dv).astype(bf16))],
            axis=1,
        )
        query = unpadded(mm_tn(normed, dq).astype(bf16))
        dq, kv, query, up_sum[1] = tied(dq, kv, query, up_sum[1])
        up_sum = scatter_columns(jnp.concatenate(up_sum, axis=0))
        out = add_partner(out, high_bits)[0]
        kv = add_partner(split_rows(kv), low_bits)
        query = add_partner(split_rows(query), low_bits)
        outgoing, attn_sum = heads_back(dq, dk, dv, wqkv, h, middle_grad, attn_row, 0, blocks)
        outgoing, kv, query, out, gate_sum = tied(outgoing, kv, query, out, gate_sum)
        kv = add_partner(kv, high_bits)[0]
        query = add_partner(query, high_bits)[0]
        pair = jnp.concatenate(
            [out.reshape(share, tsize, -1), query.reshape(share, tsize, -1)], axis=2
        )
        pair, up_sum = tied(pair, up_sum)
        pair = scatter_columns(pair)
        gains = jnp.concatenate([attn_sum, mlp_sum], axis=0)
        half_cols = pair.shape[1] // 2
        sums = [down, gate_sum, up_sum, pair[:, :half_cols], pair[:, half_cols:]]
        return outgoing, sums + [sum_over_tensor(kv)], gains

    def sum_over_tensor(array):
        bits = bits_of(tsize)
        for bit in bits:
            side = (t & bit) != 0
            size = array.shape[1] // 2
            low, high = array[:, :size], array[:, size:]
            got = swapped(jnp.where(side, low, high), "tensor", bit)
            kept_half = jnp.where(side, high, low)
            array = (kept_half.astype(f32) + got.astype(f32)).astype(bf16)
        for bit in reversed(bits):
            side = (t & bit) != 0
            got = swapped(array, "tensor", bit)
            array = jnp.concatenate(
                [jnp.where(side, got, array), jnp.where(side, array, got)], axis=1
            )
        return array

    def to_places(rows):
        return exchange(reorder(rows, 1).reshape(micro, nloc, width))[None]

    kept, _ = forward(rows_in)
    far_down[-1], hidden = tied(far_down[-1], kept[-1])
    middle = kept[5]
    wd = settle(far_down)
    received = jnp.concatenate(
        [
            shifted(down_rows(hidden, middle, wd, i, 1), "section", 1)
            for i in range(blocks)
        ],
        axis=0,
    )
    received, late_cotangent = tied(received, cotangent)
    half_cot = exchange_half(late_cotangent)
    kept, cot = forward(jnp.where(first_section, rows_in, received), join_halves(half_cot))
    second_out = down_rows(kept[-1], kept[5], wd, 0, blocks)
    first_grad, outputs = backward(cot, kept, False, to_places(second_out))
    returned = jnp.concatenate([shifted(part, "section", -1) for part in first_grad], axis=0)
    second_grad, sums, gains = backward(jnp.where(first_section, returned, cot), kept, True)
    input_grads = to_places(second_grad)
    down, gate, up, out, query, kv = sums
    gains = reorder(gains, 1)
    for axis, size in (("dp", dsize), ("tensor", tsize)):
        for bit in bits_of(size):
            gains = gains + swapped(gains, axis, bit)
    return (
        outputs,
        input_grads,
        gains[:1],
        query.astype(f32)[None],
        kv[:, :dims].astype(f32)[None],
        kv[:, dims:].astype(f32)[None],
        out.astype(f32).T[None],
        gains[1:],
        gate.astype(f32)[None],
        up.astype(f32)[None],
        down.astype(f32).T[None],
    )


def solution(mesh):
    in_specs = (
        P(None, ("dp", "tensor"), None),
        P(None, ("dp", "tensor"), None),
        P("section", None),
        P("section", "dp", "tensor"),
        P("section", "dp", None),
        P("section", "dp", None),
        P("section", "tensor", "dp"),
        P("section", None),
        P("section", "dp", "tensor"),
        P("section", "dp", "tensor"),
        P("section", "tensor", "dp"),
    )
    out_specs = (
        P("section", None, ("dp", "tensor"), None),
        P("section", None, ("dp", "tensor"), None),
        P("section", None),
        P("section", "dp", "tensor"),
        P("section", "dp", None),
        P("section", "dp", None),
        P("section", "tensor", "dp"),
        P("section", None),
        P("section", "dp", "tensor"),
        P("section", "dp", "tensor"),
        P("section", "tensor", "dp"),
    )
    return jax.shard_map(local, mesh=mesh, in_specs=in_specs, out_specs=out_specs, check_vma=False)
```

```python
import functools

import jax
import jax.numpy as jnp
from jax import lax
from jax.experimental import pallas as pl
from jax.experimental.pallas import tpu as pltpu
from jax.sharding import PartitionSpec as P

HEADS = 16
KV_HEADS = 8
HD = 96
L = 1024

epsilon = 1e-05
rope_base = 100000.0
bf16 = jnp.bfloat16
f32 = jnp.float32


def shifted(array, axis, by):
    size = lax.axis_size(axis)
    pairs = [(i, i + by) for i in range(size) if 0 <= i + by < size]
    return lax.ppermute(array, axis, pairs)


def swapped(array, axis, bit):
    return lax.ppermute(array, axis, [(i, i ^ bit) for i in range(lax.axis_size(axis))])


def bits_of(size):
    return [1 << k for k in range(size.bit_length() - 1)]


def mm(left, right):
    return jnp.dot(left, right, preferred_element_type=f32)


def mm_nt(left, right):
    return lax.dot_general(
        left, right, (((1,), (1,)), ((), ())), preferred_element_type=f32
    )


def mm_tn(left, right):
    return lax.dot_general(
        left, right, (((0,), (0,)), ((), ())), preferred_element_type=f32
    )


QB = 256
HP = 128
LOG2E = 1.4426950408889634
MIB = 2**20


def whole(shape):
    rest = (0,) * len(shape)
    return pl.BlockSpec(tuple(shape), lambda *_: rest, pipeline_mode=pl.Buffered(1))


def rows_of(shape, first=0):
    return pl.BlockSpec(tuple(shape), lambda i: (first + i, 0))


def columns_of(shape, first=0):
    return pl.BlockSpec(tuple(shape), lambda i: (0, first + i))


def kernel_call(kernel, grid, in_specs, out_specs, out_shape, flops, name, scratch=(), trans=0):
    moved = sum(2 * shape.size for shape in out_shape)
    return pl.pallas_call(
        kernel,
        grid=grid,
        in_specs=in_specs,
        out_specs=out_specs,
        out_shape=out_shape,
        scratch_shapes=scratch,
        compiler_params=pltpu.CompilerParams(vmem_limit_bytes=56 * MIB),
        cost_estimate=pl.CostEstimate(
            flops=int(flops), bytes_accessed=int(moved + flops // 512), transcendentals=int(trans)
        ),
        name=name,
    )


def turned(values, cosine, sine):
    parts = []
    for at in range(0, values.shape[1], HP):
        head = values[:, at : at + HP]
        parts.append(head * cosine + pltpu.roll(head, HP // 2, 1) * sine)
    return parts[0] if len(parts) == 1 else jnp.concatenate(parts, axis=1)


def project_kernel(h_ref, gain_ref, w_ref, cos_ref, sin_ref, out_ref, normed_ref, *, turning):
    step = pl.program_id(0)

    @pl.when(step == 0)
    def _():
        rows = h_ref[...].astype(f32)
        inverse = lax.rsqrt(jnp.mean(rows * rows, axis=-1, keepdims=True) + epsilon)
        normed_ref[...] = (rows * inverse * gain_ref[...]).astype(bf16)

    values = mm(normed_ref[...], w_ref[...])

    @pl.when(step < turning)
    def _():
        out_ref[...] = turned(values, cos_ref[...], sin_ref[...]).astype(bf16)

    @pl.when(step >= turning)
    def _():
        out_ref[...] = values.astype(bf16)


def project(h, gain, w, cosine, sine, turned_columns):
    n, width = h.shape
    total = w.shape[1]
    block = 512
    out_shape = (
        jax.ShapeDtypeStruct((n, total), bf16),
        jax.ShapeDtypeStruct((n, width), bf16),
    )
    return kernel_call(
        functools.partial(project_kernel, turning=turned_columns // block),
        (total // block,),
        [
            whole(h.shape), whole(gain.shape), columns_of((width, block)),
            whole(cosine.shape), whole(sine.shape),
        ],
        [columns_of((n, block)), whole((n, width))],
        out_shape,
        2 * n * width * total,
        "project",
    )(h, gain, w, cosine, sine)


def join_kernel(mixed_ref, h_ref, w_ref, gain_ref, middle_ref, normed_ref):
    middle = h_ref[...].astype(f32) + mm_nt(mixed_ref[...], w_ref[...])
    middle_ref[...] = middle
    inverse = lax.rsqrt(jnp.mean(middle * middle, axis=-1, keepdims=True) + epsilon)
    normed_ref[...] = (middle * inverse * gain_ref[...]).astype(bf16)


def join(mixed, h, w, gain):
    n, width = h.shape
    block = min(QB, n)
    out_shape = (
        jax.ShapeDtypeStruct((n, width), f32),
        jax.ShapeDtypeStruct((n, width), bf16),
    )
    return kernel_call(
        join_kernel,
        (n // block,),
        [
            rows_of((block, mixed.shape[1])), rows_of((block, width)),
            whole(w.shape), whole(gain.shape),
        ],
        [rows_of((block, width))] * 2,
        out_shape,
        2 * n * width * mixed.shape[1],
        "join",
    )(mixed, h, w, gain)


def gate_up_kernel(x_ref, wg_ref, wu_ref, gate_ref, up_ref, hidden_ref):
    x = x_ref[...]
    gate = mm(x, wg_ref[...])
    upward = mm(x, wu_ref[...])
    gate_ref[...] = gate.astype(bf16)
    up_ref[...] = upward.astype(bf16)
    hidden_ref[...] = (gate * jax.nn.sigmoid(gate) * upward).astype(bf16)


def gate_up(x, wg, wu):
    n, width = x.shape
    total = wg.shape[1]
    block = 512
    return kernel_call(
        gate_up_kernel,
        (total // block,),
        [whole(x.shape), columns_of((width, block)), columns_of((width, block))],
        [columns_of((n, block))] * 3,
        (jax.ShapeDtypeStruct((n, total), bf16),) * 3,
        4 * n * width * total,
        "gate_up",
        trans=n * total,
    )(x, wg, wu)


def down_kernel(hidden_ref, middle_ref, w_ref, out_ref):
    out_ref[...] = (middle_ref[...] + mm_nt(hidden_ref[...], w_ref[...])).astype(bf16)


def down_rows(hidden, middle, w, first, count):
    n, width = middle.shape
    block = min(QB, n)
    return kernel_call(
        down_kernel,
        (count,),
        [
            rows_of((block, hidden.shape[1]), first), rows_of((block, width), first),
            whole(w.shape),
        ],
        [rows_of((block, width))],
        (jax.ShapeDtypeStruct((count * block, width), bf16),),
        2 * count * block * width * hidden.shape[1],
        "down_rows",
    )(hidden, middle, w)[0]


def feed_back_kernel(
    grad_ref, gate_ref, up_ref, wd_ref, wg_ref, wu_ref, middle_ref, gain_ref,
    total_ref, low_ref, sum_ref, *grad_refs
):
    step = pl.program_id(0)
    gate = gate_ref[...].astype(f32)
    hidden_grad = mm(grad_ref[...], wd_ref[...])
    sigma = jax.nn.sigmoid(gate)
    gate_grad = hidden_grad * up_ref[...].astype(f32) * (sigma * (1.0 + gate * (1.0 - sigma)))
    gate_grad = gate_grad.astype(bf16)
    up_grad = (hidden_grad * gate * sigma).astype(bf16)
    for ref, value in zip(grad_refs, (gate_grad, up_grad)):
        ref[...] = value
    part = mm_nt(gate_grad, wg_ref[...]) + mm_nt(up_grad, wu_ref[...])

    @pl.when(step == 0)
    def _():
        total_ref[...] = part

    @pl.when(step > 0)
    def _():
        total_ref[...] += part

    @pl.when(step == pl.num_programs(0) - 1)
    def _():
        n = total_ref.shape[0]
        size = min(QB, n)
        sums = 0.0
        for at in range(0, n, size):
            rows = slice(at, at + size)
            middle = middle_ref[rows]
            back = total_ref[rows]
            inverse = lax.rsqrt(jnp.mean(middle * middle, axis=-1, keepdims=True) + epsilon)
            sums = sums + jnp.sum(back * middle * inverse, axis=0, keepdims=True)
            scaled = back * gain_ref[...]
            mean_term = jnp.mean(scaled * middle, axis=-1, keepdims=True)
            branch = scaled * inverse - middle * (inverse * inverse * inverse * mean_term)
            result = grad_ref[rows].astype(f32) + branch
            total_ref[rows] = result
            low_ref[rows] = result.astype(bf16)
        sum_ref[...] = sums


def feed_back(grad, gate, upward, wd, wg, wu, middle, gain, with_grads):
    n, width = grad.shape
    total = wg.shape[1]
    block = 512
    out_shape = (
        jax.ShapeDtypeStruct((n, width), f32),
        jax.ShapeDtypeStruct((n, width), bf16),
        jax.ShapeDtypeStruct((1, width), f32),
    )
    out_specs = [whole((n, width)), whole((n, width)), whole((1, width))]
    if with_grads:
        out_shape += (jax.ShapeDtypeStruct((n, total), bf16),) * 2
        out_specs += [columns_of((n, block))] * 2
    return kernel_call(
        feed_back_kernel,
        (total // block,),
        [
            whole(grad.shape), columns_of((n, block)), columns_of((n, block)),
            columns_of((width, block)), columns_of((width, block)), columns_of((width, block)),
            whole(middle.shape), whole(gain.shape),
        ],
        out_specs,
        out_shape,
        6 * n * width * total,
        "feed_back",
        trans=n * total,
    )(grad, gate, upward, wd, wg, wu, middle, gain)


def heads_back_kernel(
    dq_ref, dk_ref, dv_ref, w_ref, h_ref, grad_ref, gain_ref, out_ref, sum_ref
):
    step = pl.program_id(0)
    back = 0.0
    at = 0
    for ref in (dq_ref, dk_ref, dv_ref):
        back = back + mm_nt(ref[...], w_ref[:, at : at + ref.shape[1]])
        at += ref.shape[1]
    rows = h_ref[...].astype(f32)
    inverse = lax.rsqrt(jnp.mean(rows * rows, axis=-1, keepdims=True) + epsilon)
    sums = jnp.sum(back * rows * inverse, axis=0, keepdims=True)
    scaled = back * gain_ref[...]
    mean_term = jnp.mean(scaled * rows, axis=-1, keepdims=True)
    branch = scaled * inverse - rows * (inverse * inverse * inverse * mean_term)
    out_ref[...] = (grad_ref[...] + branch).astype(bf16)

    @pl.when(step == 0)
    def _():
        sum_ref[...] = sums

    @pl.when(step > 0)
    def _():
        sum_ref[...] += sums


def heads_back(dq, dk, dv, w, h, grad, gain, first, count):
    n, width = h.shape
    block = min(QB, n)
    out_shape = (
        jax.ShapeDtypeStruct((count * block, width), bf16),
        jax.ShapeDtypeStruct((1, width), f32),
    )
    return kernel_call(
        heads_back_kernel,
        (count,),
        [rows_of((block, a.shape[1]), first) for a in (dq, dk, dv)]
        + [
            whole(w.shape), rows_of((block, width), first), rows_of((block, width), first),
            whole(gain.shape),
        ],
        [rows_of((block, width)), whole((1, width))],
        out_shape,
        2 * count * block * width * w.shape[1],
        "heads_back",
    )(dq, dk, dv, w, h, grad, gain)


def two_heads(ref, rows):
    return jnp.concatenate([ref[rows, :HP], ref[rows, HP:]], axis=0)


def score_parts(offset_ref, k_ref, q, i, size, single):
    cols = q.shape[0]
    first = i * size if single else 0
    count = size if single else k_ref.shape[0]
    parts = []
    if first:
        parts.append((0, first, mm_nt(k_ref[:first], q)))
    diagonal = mm_nt(k_ref[first : first + count], q)
    key_at = first + lax.broadcasted_iota(jnp.int32, (count, cols), 0)
    query_at = i * size + lax.rem(lax.broadcasted_iota(jnp.int32, (count, cols), 1), size)
    if not single:
        query_at = query_at + offset_ref[0]
    diagonal = jnp.where(key_at <= query_at, diagonal, -1e30)
    parts.append((first, count, diagonal))
    return parts


def attend_forward_kernel(offset_ref, q_ref, k_ref, v_ref, o_ref, lse_ref, *, single):
    n = q_ref.shape[0]
    size = min(QB, n)
    factor = HD ** (-0.5) * LOG2E
    vt = v_ref[...].T
    for i in range(n // size):
        rows = slice(i * size, (i + 1) * size)
        q = two_heads(q_ref, rows)
        parts = score_parts(offset_ref, k_ref, q, i, size, single)
        top = functools.reduce(
            jnp.maximum, [jnp.max(part, axis=0, keepdims=True) for _, _, part in parts]
        )
        total = 0.0
        mixed = 0.0
        for first, count, part in parts:
            weights = jnp.exp2((part - top) * factor)
            total = total + jnp.sum(weights, axis=0, keepdims=True)
            mixed = mixed + mm(vt[:, first : first + count], weights.astype(bf16))
        mixed = (mixed * (1.0 / total)).T.astype(bf16)
        o_ref[rows, :HP] = mixed[:size]
        o_ref[rows, HP:] = mixed[size:]
        lse_ref[0, i] = top * factor + jnp.log2(total)


def attend_backward_kernel(
    offset_ref, q_ref, k_ref, v_ref, g_ref, lse_ref, cosq_ref, sinq_ref, cosk_ref, sink_ref,
    dq_ref, dk_ref, dv_ref, dk_acc, dv_acc, *, single
):
    n = q_ref.shape[0]
    size = min(QB, n)
    scale = HD ** (-0.5)
    factor = scale * LOG2E
    kt = k_ref[...].T
    dk_acc[...] = jnp.zeros_like(dk_acc)
    dv_acc[...] = jnp.zeros_like(dv_acc)
    for i in range(n // size):
        rows = slice(i * size, (i + 1) * size)
        q = two_heads(q_ref, rows)
        g = two_heads(g_ref, rows)
        lse = lse_ref[0, i]
        kept = []
        centre = 0.0
        for first, count, part in score_parts(offset_ref, k_ref, q, i, size, single):
            keys = slice(first, first + count)
            probs = jnp.exp2(part * factor - lse)
            prob_grad = mm_nt(v_ref[keys], g)
            dv_acc[keys] += mm(probs.astype(bf16), g)
            centre = centre + jnp.sum(probs * prob_grad, axis=0, keepdims=True)
            kept.append((keys, probs, prob_grad))
        dqt = 0.0
        for keys, probs, prob_grad in kept:
            score_grad = (probs * (prob_grad - centre)).astype(bf16)
            dk_acc[keys] += mm(score_grad, q)
            dqt = dqt + mm(kt[:, keys], score_grad)
        dq = (dqt * scale).T
        for c in range(2):
            head = turned(dq[c * size : (c + 1) * size], cosq_ref[rows], sinq_ref[rows])
            dq_ref[rows, c * HP : (c + 1) * HP] = head.astype(bf16)
    dk_ref[...] = turned(dk_acc[...] * scale, cosk_ref[...], sink_ref[...]).astype(bf16)
    dv_ref[...] = dv_acc[...].astype(bf16)


SCALAR = pl.BlockSpec(memory_space=pltpu.SMEM)


def attention_forward(q, k, v, offset, single):
    n = q[0].shape[0]
    size = min(QB, n)
    count = k[0].shape[0]
    out_shape = (
        jax.ShapeDtypeStruct((n, HEADS * HP), bf16),
        jax.ShapeDtypeStruct((KV_HEADS, n // size, 1, 2 * size), f32),
    )
    return kernel_call(
        functools.partial(attend_forward_kernel, single=single),
        (KV_HEADS,),
        [
            SCALAR, columns_of((n, 2 * HP), q[1] // 2), columns_of((count, HP), k[1]),
            columns_of((count, HP), v[1]),
        ],
        [
            columns_of((n, 2 * HP)),
            pl.BlockSpec((1, n // size, 1, 2 * size), lambda h: (h, 0, 0, 0)),
        ],
        out_shape,
        4 * HEADS * n * count * HP,
        "attend_forward",
        trans=HEADS * n * count,
    )(offset, q[0], k[0], v[0])


def attention_backward(q, k, v, mixed_grad, lse, query_tables, key_tables, offset, single):
    n = q[0].shape[0]
    size = min(QB, n)
    count = k[0].shape[0]
    out_shape = (
        jax.ShapeDtypeStruct((n, HEADS * HP), bf16),
        jax.ShapeDtypeStruct((count, KV_HEADS * HP), bf16),
        jax.ShapeDtypeStruct((count, KV_HEADS * HP), bf16),
    )
    return kernel_call(
        functools.partial(attend_backward_kernel, single=single),
        (KV_HEADS,),
        [
            SCALAR, columns_of((n, 2 * HP), q[1] // 2), columns_of((count, HP), k[1]),
            columns_of((count, HP), v[1]), columns_of((n, 2 * HP)),
            pl.BlockSpec((1, n // size, 1, 2 * size), lambda h: (h, 0, 0, 0)),
        ]
        + [whole(table.shape) for table in query_tables + key_tables],
        [columns_of((n, 2 * HP)), columns_of((count, HP)), columns_of((count, HP))],
        out_shape,
        10 * HEADS * n * count * HP,
        "attend_backward",
        scratch=[pltpu.VMEM((count, HP), f32), pltpu.VMEM((count, HP), f32)],
        trans=HEADS * n * count,
    )(offset, q[0], k[0], v[0], mixed_grad, lse, *query_tables, *key_tables)


def padded(array):
    rows = array.shape[0]
    parts = array.reshape(rows, -1, HD // 2)
    parts = jnp.pad(parts, ((0, 0), (0, 0), (0, HP // 2 - HD // 2)))
    return parts.reshape(rows, -1)


def unpadded(array):
    rows = array.shape[0]
    return array.reshape(rows, -1, HP // 2)[:, :, : HD // 2].reshape(rows, -1)


def local(
    inputs, cotangent, attn_gain, w_query, w_key, w_value, w_out, mlp_gain, w_gate, w_up, w_down
):
    micro, nloc, width = inputs.shape
    tsize = lax.axis_size("tensor")
    dsize = lax.axis_size("dp")
    ranks = tsize // micro
    n = nloc * micro
    share = width // dsize
    first_section = lax.axis_index("section") == 0
    t = lax.axis_index("tensor")
    d = lax.axis_index("dp")
    seq = t % micro
    seg = t // micro
    copies = HEADS // KV_HEADS
    dims = KV_HEADS * HD
    low_bits = bits_of(dsize)[:1]
    high_bits = bits_of(dsize)[1:]
    same_seq = [[g + micro * r for r in range(ranks)] for g in range(micro)]

    def exchange(blocks):
        out = blocks
        for j in range(1, micro):
            sent = lax.dynamic_index_in_dim(blocks, seq ^ j, 0, keepdims=True)
            got = swapped(sent, "tensor", j)
            out = lax.dynamic_update_slice_in_dim(out, got, seq ^ j, 0)
        return out

    def reorder(array, axis):
        return jnp.concatenate(
            [lax.dynamic_slice_in_dim(array, (d ^ m) * share, share, axis) for m in range(dsize)],
            axis=axis,
        )

    def swap_in(parts, bit):
        parts = dict(parts)
        for m in sorted(parts):
            parts[m ^ bit] = swapped(parts[m], "dp", bit)
        return parts

    def spread_far(block):
        parts = {0: block}
        for bit in reversed(high_bits):
            parts = swap_in(parts, bit)
        return parts

    def spread_near(parts):
        for bit in low_bits:
            parts = swap_in(parts, bit)
        return jnp.concatenate([parts[m] for m in range(dsize)], axis=0)

    def gather_columns(shard):
        whole = lax.all_gather(shard, "tensor", axis=0)
        return whole.transpose(1, 0, 2).reshape(share, tsize * shard.shape[1])

    def tied(*arrays):
        return lax.optimization_barrier(arrays)

    def exchange_half(array):
        side = lax.axis_index("section")
        return exchange(lax.dynamic_slice_in_dim(array, side * (width // 2), width // 2, 2))

    def join_halves(mine):
        other = swapped(mine, "section", 1)
        whole = jnp.concatenate(
            [jnp.where(first_section, mine, other), jnp.where(first_section, other, mine)], axis=2
        )
        return reorder(whole.reshape(n, width), 1)

    def split_rows(grad):
        return {m: grad[m * share : (m + 1) * share].astype(bf16) for m in range(dsize)}

    def add_partner(parts, bits):
        for bit in bits:
            summed = {}
            for m in sorted(parts):
                if not m & bit:
                    got = swapped(parts[m ^ bit], "dp", bit)
                    summed[m] = (parts[m].astype(f32) + got.astype(f32)).astype(bf16)
            parts = summed
        return parts

    def rows_to_send(array):
        return jnp.concatenate(
            [array[:, m * share : (m + 1) * share] for m in range(dsize) if m & 1], axis=1
        )

    def rows_to_keep(array):
        return jnp.concatenate(
            [array[:, m * share : (m + 1) * share] for m in range(dsize) if not m & 1], axis=1
        )

    def swap_low(array):
        return swapped(array, "dp", 1)

    def add_low(mine, got):
        total = (mine.astype(f32) + got.astype(f32)).astype(bf16)
        return {2 * i: total[i * share : (i + 1) * share] for i in range(dsize // 2)}

    def send_far(parts):
        size = share // 2
        pairs = []
        for i in range(2):
            half = {m: part[i * size : (i + 1) * size] for m, part in parts.items()}
            bit = high_bits[0]
            kept = {m: part for m, part in half.items() if not m & bit}
            pairs.append([kept, {m: swapped(half[m ^ bit], "dp", bit) for m in kept}])
        return pairs

    def receive_far(pair):
        kept, got = pair
        parts = {m: (kept[m].astype(f32) + got[m].astype(f32)).astype(bf16) for m in kept}
        return add_partner(parts, high_bits[1:])[0]

    def scatter_columns(part):
        part = part.reshape(share, tsize, -1).transpose(1, 0, 2)
        return lax.psum_scatter(part, "tensor", scatter_dimension=0)

    attn_scale = reorder(attn_gain[0], 0)
    mlp_scale = reorder(mlp_gain[0], 0)
    mine = exchange_half(inputs)
    last = spread_far(jnp.concatenate([w_key[0], w_value[0]], axis=1))
    mine, last = tied(mine, last)
    wkv = spread_near(last)
    rows_in = join_halves(mine)

    def spread_weight(shard, pieces, last):
        rows = share // pieces
        fars = []
        for i in range(pieces):
            whole = lax.all_gather(shard[i * rows : (i + 1) * rows], "tensor", axis=0)
            whole, last = tied(whole, last)
            if fars:
                fars[-1] = last
            whole = whole.transpose(1, 0, 2).reshape(rows, tsize * shard.shape[1])
            last = spread_far(whole)
            fars.append(last)
        return fars, last

    def settle(fars):
        parts = [dict(far) for far in fars]
        for bit in low_bits:
            parts = [swap_in(part, bit) for part in parts]
        return jnp.concatenate([part[m] for m in range(dsize) for part in parts], axis=0)

    fars, last = spread_weight(w_query[0], 1, last)
    wqkv = jnp.concatenate([padded(settle(fars)), padded(wkv)], axis=1)
    fars, last = spread_weight(w_out[0].T, 1, last)
    wo = padded(settle(fars))
    fars, last = spread_weight(w_gate[0], 2, last)
    waits = list(fars)
    wg = settle(fars)
    fars, last = spread_weight(w_up[0], 2, last)
    waits.append(fars[0])
    wu = settle(fars)
    far_down, last = spread_weight(w_down[0].T, 2, last)

    def tables(positions):
        half = HD // 2
        freqs = rope_base ** (-jnp.arange(half, dtype=f32) / half)
        angles = positions.astype(f32)[:, None] * freqs[None, :]
        blank = ((0, 0), (0, HP // 2 - half))
        cosine = jnp.pad(jnp.cos(angles), blank)
        sine = jnp.pad(jnp.sin(angles), blank)
        return (
            jnp.concatenate([cosine, cosine], axis=1),
            jnp.concatenate([-sine, sine], axis=1),
        )

    query_tables = tables(seg * n + jnp.arange(n))
    single = ranks == 1
    offset = (seg * n).astype(jnp.int32).reshape(1)

    back_tables = (query_tables[0], -query_tables[1])
    if single:
        key_tables = back_tables
    else:
        key_tables = tables(jnp.arange(L))
        key_tables = (key_tables[0], -key_tables[1])
    q_lanes = HEADS * HP
    k_lanes = KV_HEADS * HP
    blocks = n // min(QB, n)
    attn_row = attn_scale[None]
    mlp_row = mlp_scale[None]

    def head_arrays(qkv):
        if single:
            return (qkv, 0), (qkv, HEADS), (qkv, HEADS + KV_HEADS)
        both = lax.all_gather(
            qkv[:, q_lanes:], "tensor", axis=0, tiled=True, axis_index_groups=same_seq
        )
        return (qkv, 0), (both, 0), (both, KV_HEADS)

    def own_rows(array):
        if single:
            return array
        return lax.psum_scatter(
            array, "tensor", scatter_dimension=0, tiled=True, axis_index_groups=same_seq
        )

    def forward(h, extra=None, waits=None):
        if waits:
            h = tied(h, waits[0])[0]
        qkv, normed = project(h, attn_row, wqkv, *query_tables, q_lanes + k_lanes)
        if waits:
            qkv = tied(qkv, waits[1])[0]
        heads = head_arrays(qkv)
        mixed, lse = attention_forward(*heads, offset, single)
        if extra is not None:
            mixed, extra = tied(mixed, extra)
        if waits:
            mixed = tied(mixed, waits[2])[0]
        middle, normed_mlp = join(mixed, h, wo, mlp_row)
        gate, upward, hidden = gate_up(normed_mlp, wg, wu)
        kept = (h, normed, heads, lse, mixed, middle, normed_mlp, gate, upward, hidden)
        return kept, extra

    def sum_over_tensor(array):
        bits = bits_of(tsize)
        for bit in bits:
            side = (t & bit) != 0
            size = array.shape[1] // 2
            low, high = array[:, :size], array[:, size:]
            got = swapped(jnp.where(side, low, high), "tensor", bit)
            kept_half = jnp.where(side, high, low)
            array = (kept_half.astype(f32) + got.astype(f32)).astype(bf16)
        for bit in reversed(bits):
            side = (t & bit) != 0
            got = swapped(array, "tensor", bit)
            array = jnp.concatenate(
                [jnp.where(side, got, array), jnp.where(side, array, got)], axis=1
            )
        return array

    def to_places(rows):
        return exchange(reorder(rows, 1).reshape(micro, nloc, width))[None]

    def backward(grad, kept, weights_too, extra=None):
        h, normed, heads, lse, mixed, middle, normed_mlp, gate, upward, hidden = kept
        if weights_too:
            odd, even = rows_to_send(grad), rows_to_keep(grad)
            odd = mm_tn(odd, hidden).astype(bf16)
            even, odd = tied(even, odd)
            got = swap_low(odd)
            even = mm_tn(even, hidden).astype(bf16)
            even, grad = tied(even, grad)
            grad, down = tied(grad, add_low(even, got))
            down = add_partner(down, high_bits)[0]
        middle_grad, middle_bf, mlp_sum, *grads = feed_back(
            grad, gate, upward, wd, wg, wu, middle, mlp_row, weights_too
        )
        if weights_too:
            gate_grad, up_grad = grads
            gate_grad, up_grad, down = tied(gate_grad, up_grad, down)
            down = scatter_columns(down)
            odd = mm_tn(rows_to_send(normed_mlp), gate_grad).astype(bf16)
            gate_grad, odd = tied(gate_grad, odd)
            got = swap_low(odd)
            even = mm_tn(rows_to_keep(normed_mlp), gate_grad).astype(bf16)
            even, up_grad = tied(even, up_grad)
            up_grad, gate_sum = tied(up_grad, add_low(even, got))
            first, second = send_far(gate_sum)
            gate_sum = receive_far(first)
            up_sum = mm_tn(normed_mlp, up_grad).astype(bf16)
            middle_bf, up_sum, gate_sum, second[0] = tied(middle_bf, up_sum, gate_sum, second[0])
            gate_sum = [gate_sum, receive_far(second)]
            up_sum = add_partner(split_rows(up_sum), low_bits)
            out = unpadded(mm_tn(middle_bf, mixed).astype(bf16))
            middle_bf, out = tied(middle_bf, out)
            out = add_partner(split_rows(out), low_bits)
        mixed_grad = mm(middle_bf, wo).astype(bf16)
        if extra is not None:
            mixed_grad, extra = tied(mixed_grad, extra)
        if weights_too:
            mixed_grad, gate_sum[1], up_sum, out = tied(mixed_grad, gate_sum[1], up_sum, out)
            gate_sum = scatter_columns(jnp.concatenate(gate_sum, axis=0))
            first, second = send_far(up_sum)
            up_sum = receive_far(first)
        dq, dk, dv = attention_backward(
            *heads, mixed_grad, lse, back_tables, key_tables, offset, single
        )
        dk = own_rows(dk)
        dv = own_rows(dv)
        if not weights_too:
            return (dq, dk, dv, middle_grad), extra
        dq, dk, dv, down, up_sum, second[0] = tied(dq, dk, dv, down, up_sum, second[0])
        up_sum = [up_sum, receive_far(second)]
        kv = jnp.concatenate(
            [unpadded(mm_tn(normed, dk).astype(bf16)), unpadded(mm_tn(normed, dv).astype(bf16))],
            axis=1,
        )
        dq, kv = tied(dq, kv)
        kv = add_partner(split_rows(kv), low_bits)
        query = unpadded(mm_tn(normed, dq).astype(bf16))
        dq, kv, query, up_sum[1] = tied(dq, kv, query, up_sum[1])
        up_sum, dq = tied(jnp.concatenate(up_sum, axis=0), dq)
        up_sum = scatter_columns(up_sum)
        kv = add_partner(kv, high_bits)[0]
        query = add_partner(split_rows(query), low_bits)
        outgoing, attn_sum = heads_back(dq, dk, dv, wqkv, h, middle_grad, attn_row, 0, blocks)
        outgoing, kv, query, gate_sum = tied(outgoing, kv, query, gate_sum)
        out = add_partner(out, high_bits)[0]
        query = add_partner(query, high_bits)[0]
        input_grads = to_places(outgoing)
        kv = sum_over_tensor(kv)
        pair = jnp.concatenate(
            [out.reshape(share, tsize, -1), query.reshape(share, tsize, -1)], axis=2
        )
        pair, up_sum, input_grads, kv, attn_sum = tied(pair, up_sum, input_grads, kv, attn_sum)
        pair = scatter_columns(pair)
        gains = jnp.concatenate([attn_sum, mlp_sum], axis=0)
        half_cols = pair.shape[1] // 2
        sums = [down, gate_sum, up_sum, pair[:, :half_cols], pair[:, half_cols:]]
        return input_grads, sums + [kv], gains

    def row_chunks():
        if blocks < 2:
            return [(0, blocks)]
        return [(0, blocks // 2), (blocks // 2, blocks - blocks // 2)]

    def send_chunks(make, by, source):
        got = []
        for first, count in row_chunks():
            chunk, source = make(source, first, count)
            if got:
                chunk, got[-1] = tied(chunk, got[-1])
            source, chunk = tied(source, chunk)
            got.append(shifted(chunk, "section", by))
        return jnp.concatenate(got, axis=0)

    kept, _ = forward(rows_in, None, waits)
    far_down[-1], hidden, late_cotangent = tied(far_down[-1], kept[-1], cotangent)
    middle = kept[5]
    wd = settle(far_down)
    half_cot = exchange_half(late_cotangent)
    received = send_chunks(
        lambda source, first, count: (down_rows(source, middle, wd, first, count), source),
        1,
        hidden,
    )
    received, half_cot = tied(received, half_cot)
    kept, cot = forward(jnp.where(first_section, rows_in, received), join_halves(half_cot))
    second_out = down_rows(kept[-1], kept[5], wd, 0, blocks)
    (dq, dk, dv, middle_grad), outputs = backward(cot, kept, False, to_places(second_out))
    returned = send_chunks(
        lambda source, first, count: (
            heads_back(source, dk, dv, wqkv, kept[0], middle_grad, attn_row, first, count)[0],
            source,
        ),
        -1,
        dq,
    )
    input_grads, sums, gains = backward(jnp.where(first_section, returned, cot), kept, True)
    down, gate, up, out, query, kv = sums
    gains = reorder(gains, 1)
    for axis, size in (("dp", dsize), ("tensor", tsize)):
        for bit in bits_of(size):
            gains = gains + swapped(gains, axis, bit)
    return (
        outputs,
        input_grads,
        gains[:1],
        query.astype(f32)[None],
        kv[:, :dims].astype(f32)[None],
        kv[:, dims:].astype(f32)[None],
        out.astype(f32).T[None],
        gains[1:],
        gate.astype(f32)[None],
        up.astype(f32)[None],
        down.astype(f32).T[None],
    )


def solution(mesh):
    in_specs = (
        P(None, ("dp", "tensor"), None),
        P(None, ("dp", "tensor"), None),
        P("section", None),
        P("section", "dp", "tensor"),
        P("section", "dp", None),
        P("section", "dp", None),
        P("section", "tensor", "dp"),
        P("section", None),
        P("section", "dp", "tensor"),
        P("section", "dp", "tensor"),
        P("section", "tensor", "dp"),
    )
    out_specs = (
        P("section", None, ("dp", "tensor"), None),
        P("section", None, ("dp", "tensor"), None),
        P("section", None),
        P("section", "dp", "tensor"),
        P("section", "dp", None),
        P("section", "dp", None),
        P("section", "tensor", "dp"),
        P("section", None),
        P("section", "dp", "tensor"),
        P("section", "dp", "tensor"),
        P("section", "tensor", "dp"),
    )
    return jax.shard_map(local, mesh=mesh, in_specs=in_specs, out_specs=out_specs, check_vma=False)
```

```python
import functools

import jax
import jax.numpy as jnp
from jax import lax
from jax.experimental import pallas as pl
from jax.experimental.pallas import tpu as pltpu
from jax.sharding import PartitionSpec as P

HEADS = 16
KV_HEADS = 8
HD = 96
L = 1024

epsilon = 1e-05
rope_base = 100000.0
bf16 = jnp.bfloat16
f32 = jnp.float32


def shifted(array, axis, by):
    size = lax.axis_size(axis)
    pairs = [(i, i + by) for i in range(size) if 0 <= i + by < size]
    return lax.ppermute(array, axis, pairs)


def swapped(array, axis, bit):
    return lax.ppermute(array, axis, [(i, i ^ bit) for i in range(lax.axis_size(axis))])


def bits_of(size):
    return [1 << k for k in range(size.bit_length() - 1)]


def mm(left, right):
    return jnp.dot(left, right, preferred_element_type=f32)


def mm_nt(left, right):
    return lax.dot_general(
        left, right, (((1,), (1,)), ((), ())), preferred_element_type=f32
    )


def mm_tn(left, right):
    return lax.dot_general(
        left, right, (((0,), (0,)), ((), ())), preferred_element_type=f32
    )


QB = 256
ROWS = 512
HP = 128
LOG2E = 1.4426950408889634
MIB = 2**20


def whole(shape):
    rest = (0,) * len(shape)
    return pl.BlockSpec(tuple(shape), lambda *_: rest, pipeline_mode=pl.Buffered(1))


def rows_of(shape, first=0):
    return pl.BlockSpec(tuple(shape), lambda i: (first + i, 0))


def columns_of(shape, first=0):
    return pl.BlockSpec(tuple(shape), lambda i: (0, first + i))


def kernel_call(kernel, grid, in_specs, out_specs, out_shape, flops, name, scratch=(), trans=0):
    moved = sum(2 * shape.size for shape in out_shape)
    return pl.pallas_call(
        kernel,
        grid=grid,
        in_specs=in_specs,
        out_specs=out_specs,
        out_shape=out_shape,
        scratch_shapes=scratch,
        compiler_params=pltpu.CompilerParams(vmem_limit_bytes=56 * MIB),
        cost_estimate=pl.CostEstimate(
            flops=int(flops), bytes_accessed=int(moved + flops // 512), transcendentals=int(trans)
        ),
        name=name,
    )


def turned(values, cosine, sine):
    parts = []
    for at in range(0, values.shape[1], HP):
        head = values[:, at : at + HP]
        parts.append(head * cosine + pltpu.roll(head, HP // 2, 1) * sine)
    return parts[0] if len(parts) == 1 else jnp.concatenate(parts, axis=1)


def project_kernel(h_ref, gain_ref, w_ref, cos_ref, sin_ref, out_ref, normed_ref, *, turning):
    step = pl.program_id(0)

    @pl.when(step == 0)
    def _():
        rows = h_ref[...].astype(f32)
        inverse = lax.rsqrt(jnp.mean(rows * rows, axis=-1, keepdims=True) + epsilon)
        normed_ref[...] = (rows * inverse * gain_ref[...]).astype(bf16)

    values = mm(normed_ref[...], w_ref[...])

    @pl.when(step < turning)
    def _():
        out_ref[...] = turned(values, cos_ref[...], sin_ref[...]).astype(bf16)

    @pl.when(step >= turning)
    def _():
        out_ref[...] = values.astype(bf16)


def project(h, gain, w, cosine, sine, turned_columns):
    n, width = h.shape
    total = w.shape[1]
    block = 512
    out_shape = (
        jax.ShapeDtypeStruct((n, total), bf16),
        jax.ShapeDtypeStruct((n, width), bf16),
    )
    return kernel_call(
        functools.partial(project_kernel, turning=turned_columns // block),
        (total // block,),
        [
            whole(h.shape), whole(gain.shape), columns_of((width, block)),
            whole(cosine.shape), whole(sine.shape),
        ],
        [columns_of((n, block)), whole((n, width))],
        out_shape,
        2 * n * width * total,
        "project",
    )(h, gain, w, cosine, sine)


def join_kernel(mixed_ref, h_ref, w_ref, gain_ref, middle_ref, normed_ref):
    middle = h_ref[...].astype(f32) + mm_nt(mixed_ref[...], w_ref[...])
    middle_ref[...] = middle
    inverse = lax.rsqrt(jnp.mean(middle * middle, axis=-1, keepdims=True) + epsilon)
    normed_ref[...] = (middle * inverse * gain_ref[...]).astype(bf16)


def join(mixed, h, w, gain):
    n, width = h.shape
    block = min(ROWS, n)
    out_shape = (
        jax.ShapeDtypeStruct((n, width), f32),
        jax.ShapeDtypeStruct((n, width), bf16),
    )
    return kernel_call(
        join_kernel,
        (n // block,),
        [
            rows_of((block, mixed.shape[1])), rows_of((block, width)),
            whole(w.shape), whole(gain.shape),
        ],
        [rows_of((block, width))] * 2,
        out_shape,
        2 * n * width * mixed.shape[1],
        "join",
    )(mixed, h, w, gain)


def gate_up_kernel(x_ref, wg_ref, wu_ref, gate_ref, up_ref, hidden_ref):
    x = x_ref[...]
    gate = mm(x, wg_ref[...])
    upward = mm(x, wu_ref[...])
    gate_ref[...] = gate.astype(bf16)
    up_ref[...] = upward.astype(bf16)
    hidden_ref[...] = (gate * jax.nn.sigmoid(gate) * upward).astype(bf16)


def gate_up(x, wg, wu):
    n, width = x.shape
    total = wg.shape[1]
    block = 512
    return kernel_call(
        gate_up_kernel,
        (total // block,),
        [whole(x.shape), columns_of((width, block)), columns_of((width, block))],
        [columns_of((n, block))] * 3,
        (jax.ShapeDtypeStruct((n, total), bf16),) * 3,
        4 * n * width * total,
        "gate_up",
        trans=n * total,
    )(x, wg, wu)


def down_kernel(hidden_ref, middle_ref, w_ref, out_ref):
    out_ref[...] = (middle_ref[...] + mm_nt(hidden_ref[...], w_ref[...])).astype(bf16)


def down_rows(hidden, middle, w, first, count):
    n, width = middle.shape
    block = min(ROWS, n)
    return kernel_call(
        down_kernel,
        (count,),
        [
            rows_of((block, hidden.shape[1]), first), rows_of((block, width), first),
            whole(w.shape),
        ],
        [rows_of((block, width))],
        (jax.ShapeDtypeStruct((count * block, width), bf16),),
        2 * count * block * width * hidden.shape[1],
        "down_rows",
    )(hidden, middle, w)[0]


def hidden_back(grad_ref, gate_ref, up_ref, wd_ref):
    gate = gate_ref[...].astype(f32)
    hidden_grad = mm(grad_ref[...], wd_ref[...])
    sigma = jax.nn.sigmoid(gate)
    gate_grad = hidden_grad * up_ref[...].astype(f32) * (sigma * (1.0 + gate * (1.0 - sigma)))
    return gate_grad.astype(bf16), (hidden_grad * gate * sigma).astype(bf16)


def feed_back_kernel(
    grad_ref, gate_ref, up_ref, wd_ref, wg_ref, wu_ref, middle_ref, gain_ref,
    total_ref, low_ref, sum_ref
):
    step = pl.program_id(0)
    gate_grad, up_grad = hidden_back(grad_ref, gate_ref, up_ref, wd_ref)
    accumulate_back(step, gate_grad, up_grad, wg_ref, wu_ref, total_ref)
    finish_back(step, grad_ref, middle_ref, gain_ref, total_ref, low_ref, sum_ref)


def feed_grads_kernel(
    grad_ref, gate_ref, up_ref, wd_ref, normed_ref,
    gate_grad_ref, up_grad_ref, gate_sum_ref, up_sum_ref, turned_ref
):
    @pl.when(pl.program_id(0) == 0)
    def _():
        turned_ref[...] = normed_ref[...].T

    gate_grad, up_grad = hidden_back(grad_ref, gate_ref, up_ref, wd_ref)
    gate_grad_ref[...] = gate_grad
    up_grad_ref[...] = up_grad
    gate_sum_ref[...] = mm(turned_ref[...], gate_grad).astype(bf16)
    up_sum_ref[...] = mm(turned_ref[...], up_grad).astype(bf16)


def feed_grads(grad, gate, upward, wd, normed):
    n, width = grad.shape
    total = gate.shape[1]
    block = 512
    return kernel_call(
        feed_grads_kernel,
        (total // block,),
        [
            whole(grad.shape), columns_of((n, block)), columns_of((n, block)),
            columns_of((width, block)), whole(normed.shape),
        ],
        [columns_of((n, block))] * 2 + [columns_of((width, block))] * 2,
        (jax.ShapeDtypeStruct((n, total), bf16),) * 2
        + (jax.ShapeDtypeStruct((width, total), bf16),) * 2,
        6 * n * width * total,
        "feed_grads",
        scratch=[pltpu.VMEM((width, n), bf16)],
        trans=n * total,
    )(grad, gate, upward, wd, normed)


def rows_back_kernel(
    gate_grad_ref, up_grad_ref, wg_ref, wu_ref, grad_ref, middle_ref, gain_ref,
    total_ref, low_ref, sum_ref
):
    step = pl.program_id(0)
    accumulate_back(step, gate_grad_ref[...], up_grad_ref[...], wg_ref, wu_ref, total_ref)
    finish_back(step, grad_ref, middle_ref, gain_ref, total_ref, low_ref, sum_ref)


def back_outputs(n, width):
    return (
        jax.ShapeDtypeStruct((n, width), f32),
        jax.ShapeDtypeStruct((n, width), bf16),
        jax.ShapeDtypeStruct((1, width), f32),
    )


def rows_back(gate_grad, up_grad, wg, wu, grad, middle, gain):
    n, width = grad.shape
    total = wg.shape[1]
    block = 512
    return kernel_call(
        rows_back_kernel,
        (total // block,),
        [
            columns_of((n, block)), columns_of((n, block)),
            columns_of((width, block)), columns_of((width, block)),
            whole(grad.shape), whole(middle.shape), whole(gain.shape),
        ],
        [whole((n, width)), whole((n, width)), whole((1, width))],
        back_outputs(n, width),
        4 * n * width * total,
        "rows_back",
    )(gate_grad, up_grad, wg, wu, grad, middle, gain)


def accumulate_back(step, gate_grad, up_grad, wg_ref, wu_ref, total_ref):
    part = mm_nt(
        jnp.concatenate([gate_grad, up_grad], axis=1),
        jnp.concatenate([wg_ref[...], wu_ref[...]], axis=1),
    )

    @pl.when(step == 0)
    def _():
        total_ref[...] = part

    @pl.when(step > 0)
    def _():
        total_ref[...] += part


def finish_back(step, grad_ref, middle_ref, gain_ref, total_ref, low_ref, sum_ref):
    @pl.when(step == pl.num_programs(0) - 1)
    def _():
        n = total_ref.shape[0]
        size = min(QB, n)
        sums = 0.0
        for at in range(0, n, size):
            rows = slice(at, at + size)
            middle = middle_ref[rows]
            back = total_ref[rows]
            inverse = lax.rsqrt(jnp.mean(middle * middle, axis=-1, keepdims=True) + epsilon)
            sums = sums + jnp.sum(back * middle * inverse, axis=0, keepdims=True)
            scaled = back * gain_ref[...]
            mean_term = jnp.mean(scaled * middle, axis=-1, keepdims=True)
            branch = scaled * inverse - middle * (inverse * inverse * inverse * mean_term)
            result = grad_ref[rows].astype(f32) + branch
            total_ref[rows] = result
            low_ref[rows] = result.astype(bf16)
        sum_ref[...] = sums


def feed_back(grad, gate, upward, wd, wg, wu, middle, gain):
    n, width = grad.shape
    total = wg.shape[1]
    block = 512
    return kernel_call(
        feed_back_kernel,
        (total // block,),
        [
            whole(grad.shape), columns_of((n, block)), columns_of((n, block)),
            columns_of((width, block)), columns_of((width, block)), columns_of((width, block)),
            whole(middle.shape), whole(gain.shape),
        ],
        [whole((n, width)), whole((n, width)), whole((1, width))],
        back_outputs(n, width),
        6 * n * width * total,
        "feed_back",
        trans=n * total,
    )(grad, gate, upward, wd, wg, wu, middle, gain)


def heads_back_kernel(
    dq_ref, dk_ref, dv_ref, w_ref, h_ref, grad_ref, gain_ref, out_ref, sum_ref
):
    step = pl.program_id(0)
    back = 0.0
    at = 0
    for ref in (dq_ref, dk_ref, dv_ref):
        back = back + mm_nt(ref[...], w_ref[:, at : at + ref.shape[1]])
        at += ref.shape[1]
    rows = h_ref[...].astype(f32)
    inverse = lax.rsqrt(jnp.mean(rows * rows, axis=-1, keepdims=True) + epsilon)
    sums = jnp.sum(back * rows * inverse, axis=0, keepdims=True)
    scaled = back * gain_ref[...]
    mean_term = jnp.mean(scaled * rows, axis=-1, keepdims=True)
    branch = scaled * inverse - rows * (inverse * inverse * inverse * mean_term)
    out_ref[...] = (grad_ref[...] + branch).astype(bf16)

    @pl.when(step == 0)
    def _():
        sum_ref[...] = sums

    @pl.when(step > 0)
    def _():
        sum_ref[...] += sums


def heads_back(dq, dk, dv, w, h, grad, gain, first, count):
    n, width = h.shape
    block = min(ROWS, n)
    out_shape = (
        jax.ShapeDtypeStruct((count * block, width), bf16),
        jax.ShapeDtypeStruct((1, width), f32),
    )
    return kernel_call(
        heads_back_kernel,
        (count,),
        [rows_of((block, a.shape[1]), first) for a in (dq, dk, dv)]
        + [
            whole(w.shape), rows_of((block, width), first), rows_of((block, width), first),
            whole(gain.shape),
        ],
        [rows_of((block, width)), whole((1, width))],
        out_shape,
        2 * count * block * width * w.shape[1],
        "heads_back",
    )(dq, dk, dv, w, h, grad, gain)


def two_heads(ref, rows):
    return jnp.concatenate([ref[rows, :HP], ref[rows, HP:]], axis=0)


def score_parts(offset_ref, k_ref, q, i, size, single):
    cols = q.shape[0]
    first = i * size if single else 0
    count = size if single else k_ref.shape[0]
    parts = []
    if first:
        parts.append((0, first, mm_nt(k_ref[:first], q)))
    diagonal = mm_nt(k_ref[first : first + count], q)
    key_at = first + lax.broadcasted_iota(jnp.int32, (count, cols), 0)
    query_at = i * size + lax.rem(lax.broadcasted_iota(jnp.int32, (count, cols), 1), size)
    if not single:
        query_at = query_at + offset_ref[0]
    diagonal = jnp.where(key_at <= query_at, diagonal, -1e30)
    parts.append((first, count, diagonal))
    return parts


def attend_forward_kernel(offset_ref, q_ref, k_ref, v_ref, o_ref, lse_ref, *, single):
    n = q_ref.shape[0]
    size = min(QB, n)
    factor = HD ** (-0.5) * LOG2E
    vt = v_ref[...].T
    for i in range(n // size):
        rows = slice(i * size, (i + 1) * size)
        q = two_heads(q_ref, rows)
        parts = score_parts(offset_ref, k_ref, q, i, size, single)
        top = functools.reduce(
            jnp.maximum, [jnp.max(part, axis=0, keepdims=True) for _, _, part in parts]
        )
        total = 0.0
        mixed = 0.0
        for first, count, part in parts:
            weights = jnp.exp2((part - top) * factor)
            total = total + jnp.sum(weights, axis=0, keepdims=True)
            mixed = mixed + mm(vt[:, first : first + count], weights.astype(bf16))
        mixed = (mixed * (1.0 / total)).T.astype(bf16)
        o_ref[rows, :HP] = mixed[:size]
        o_ref[rows, HP:] = mixed[size:]
        lse_ref[0, i] = top * factor + jnp.log2(total)


def attend_backward_kernel(
    offset_ref, q_ref, k_ref, v_ref, g_ref, lse_ref, cosq_ref, sinq_ref, cosk_ref, sink_ref,
    dq_ref, dk_ref, dv_ref, dk_acc, dv_acc, *, single
):
    n = q_ref.shape[0]
    size = min(QB, n)
    scale = HD ** (-0.5)
    factor = scale * LOG2E
    kt = k_ref[...].T
    dk_acc[...] = jnp.zeros_like(dk_acc)
    dv_acc[...] = jnp.zeros_like(dv_acc)
    for i in range(n // size):
        rows = slice(i * size, (i + 1) * size)
        q = two_heads(q_ref, rows)
        g = two_heads(g_ref, rows)
        lse = lse_ref[0, i]
        kept = []
        centre = 0.0
        for first, count, part in score_parts(offset_ref, k_ref, q, i, size, single):
            keys = slice(first, first + count)
            probs = jnp.exp2(part * factor - lse)
            prob_grad = mm_nt(v_ref[keys], g)
            dv_acc[keys] += mm(probs.astype(bf16), g)
            centre = centre + jnp.sum(probs * prob_grad, axis=0, keepdims=True)
            kept.append((keys, probs, prob_grad))
        dqt = 0.0
        for keys, probs, prob_grad in kept:
            score_grad = (probs * (prob_grad - centre)).astype(bf16)
            dk_acc[keys] += mm(score_grad, q)
            dqt = dqt + mm(kt[:, keys], score_grad)
        dq = (dqt * scale).T
        for c in range(2):
            head = turned(dq[c * size : (c + 1) * size], cosq_ref[rows], sinq_ref[rows])
            dq_ref[rows, c * HP : (c + 1) * HP] = head.astype(bf16)
    dk_ref[...] = turned(dk_acc[...] * scale, cosk_ref[...], sink_ref[...]).astype(bf16)
    dv_ref[...] = dv_acc[...].astype(bf16)


SCALAR = pl.BlockSpec(memory_space=pltpu.SMEM)


def attention_forward(q, k, v, offset, single):
    n = q[0].shape[0]
    size = min(QB, n)
    count = k[0].shape[0]
    out_shape = (
        jax.ShapeDtypeStruct((n, HEADS * HP), bf16),
        jax.ShapeDtypeStruct((KV_HEADS, n // size, 1, 2 * size), f32),
    )
    return kernel_call(
        functools.partial(attend_forward_kernel, single=single),
        (KV_HEADS,),
        [
            SCALAR, columns_of((n, 2 * HP), q[1] // 2), columns_of((count, HP), k[1]),
            columns_of((count, HP), v[1]),
        ],
        [
            columns_of((n, 2 * HP)),
            pl.BlockSpec((1, n // size, 1, 2 * size), lambda h: (h, 0, 0, 0)),
        ],
        out_shape,
        4 * HEADS * n * count * HP,
        "attend_forward",
        trans=HEADS * n * count,
    )(offset, q[0], k[0], v[0])


def attention_backward(q, k, v, mixed_grad, lse, query_tables, key_tables, offset, single):
    n = q[0].shape[0]
    size = min(QB, n)
    count = k[0].shape[0]
    out_shape = (
        jax.ShapeDtypeStruct((n, HEADS * HP), bf16),
        jax.ShapeDtypeStruct((count, KV_HEADS * HP), bf16),
        jax.ShapeDtypeStruct((count, KV_HEADS * HP), bf16),
    )
    return kernel_call(
        functools.partial(attend_backward_kernel, single=single),
        (KV_HEADS,),
        [
            SCALAR, columns_of((n, 2 * HP), q[1] // 2), columns_of((count, HP), k[1]),
            columns_of((count, HP), v[1]), columns_of((n, 2 * HP)),
            pl.BlockSpec((1, n // size, 1, 2 * size), lambda h: (h, 0, 0, 0)),
        ]
        + [whole(table.shape) for table in query_tables + key_tables],
        [columns_of((n, 2 * HP)), columns_of((count, HP)), columns_of((count, HP))],
        out_shape,
        10 * HEADS * n * count * HP,
        "attend_backward",
        scratch=[pltpu.VMEM((count, HP), f32), pltpu.VMEM((count, HP), f32)],
        trans=HEADS * n * count,
    )(offset, q[0], k[0], v[0], mixed_grad, lse, *query_tables, *key_tables)


def padded(array):
    rows = array.shape[0]
    parts = array.reshape(rows, -1, HD // 2)
    parts = jnp.pad(parts, ((0, 0), (0, 0), (0, HP // 2 - HD // 2)))
    return parts.reshape(rows, -1)


def unpadded(array):
    rows = array.shape[0]
    return array.reshape(rows, -1, HP // 2)[:, :, : HD // 2].reshape(rows, -1)


def local(
    inputs, cotangent, attn_gain, w_query, w_key, w_value, w_out, mlp_gain, w_gate, w_up, w_down
):
    micro, nloc, width = inputs.shape
    tsize = lax.axis_size("tensor")
    dsize = lax.axis_size("dp")
    ranks = tsize // micro
    n = nloc * micro
    share = width // dsize
    first_section = lax.axis_index("section") == 0
    t = lax.axis_index("tensor")
    d = lax.axis_index("dp")
    seq = t % micro
    seg = t // micro
    copies = HEADS // KV_HEADS
    dims = KV_HEADS * HD
    low_bits = bits_of(dsize)[:1]
    high_bits = bits_of(dsize)[1:]
    same_seq = [[g + micro * r for r in range(ranks)] for g in range(micro)]

    def exchange(blocks):
        out = blocks
        for j in range(1, micro):
            sent = lax.dynamic_index_in_dim(blocks, seq ^ j, 0, keepdims=True)
            got = swapped(sent, "tensor", j)
            out = lax.dynamic_update_slice_in_dim(out, got, seq ^ j, 0)
        return out

    def reorder(array, axis):
        return jnp.concatenate(
            [lax.dynamic_slice_in_dim(array, (d ^ m) * share, share, axis) for m in range(dsize)],
            axis=axis,
        )

    def swap_in(parts, bit):
        parts = dict(parts)
        for m in sorted(parts):
            parts[m ^ bit] = swapped(parts[m], "dp", bit)
        return parts

    def spread_far(block):
        parts = {0: block}
        for bit in reversed(high_bits):
            parts = swap_in(parts, bit)
        return parts

    def spread_near(parts):
        for bit in low_bits:
            parts = swap_in(parts, bit)
        return jnp.concatenate([parts[m] for m in range(dsize)], axis=0)

    def gather_columns(shard):
        whole = lax.all_gather(shard, "tensor", axis=0)
        return whole.transpose(1, 0, 2).reshape(share, tsize * shard.shape[1])

    def tied(*arrays):
        return lax.optimization_barrier(arrays)

    def exchange_half(array):
        side = lax.axis_index("section")
        return exchange(lax.dynamic_slice_in_dim(array, side * (width // 2), width // 2, 2))

    def join_halves(mine):
        other = swapped(mine, "section", 1)
        whole = jnp.concatenate(
            [jnp.where(first_section, mine, other), jnp.where(first_section, other, mine)], axis=2
        )
        return reorder(whole.reshape(n, width), 1)

    def split_rows(grad):
        return {m: grad[m * share : (m + 1) * share].astype(bf16) for m in range(dsize)}

    def add_partner(parts, bits):
        for bit in bits:
            summed = {}
            for m in sorted(parts):
                if not m & bit:
                    got = swapped(parts[m ^ bit], "dp", bit)
                    summed[m] = (parts[m].astype(f32) + got.astype(f32)).astype(bf16)
            parts = summed
        return parts

    def rows_to_send(array):
        return jnp.concatenate(
            [array[:, m * share : (m + 1) * share] for m in range(dsize) if m & 1], axis=1
        )

    def rows_to_keep(array):
        return jnp.concatenate(
            [array[:, m * share : (m + 1) * share] for m in range(dsize) if not m & 1], axis=1
        )

    def swap_low(array):
        return swapped(array, "dp", 1)

    def add_low(mine, got):
        total = (mine.astype(f32) + got.astype(f32)).astype(bf16)
        return {2 * i: total[i * share : (i + 1) * share] for i in range(dsize // 2)}

    def send_far(parts):
        size = share // 2
        pairs = []
        for i in range(2):
            half = {m: part[i * size : (i + 1) * size] for m, part in parts.items()}
            bit = high_bits[0]
            kept = {m: part for m, part in half.items() if not m & bit}
            pairs.append([kept, {m: swapped(half[m ^ bit], "dp", bit) for m in kept}])
        return pairs

    def receive_far(pair):
        kept, got = pair
        parts = {m: (kept[m].astype(f32) + got[m].astype(f32)).astype(bf16) for m in kept}
        return add_partner(parts, high_bits[1:])[0]

    def scatter_columns(part):
        part = part.reshape(share, tsize, -1).transpose(1, 0, 2)
        return lax.psum_scatter(part, "tensor", scatter_dimension=0)

    attn_scale = reorder(attn_gain[0], 0)
    mlp_scale = reorder(mlp_gain[0], 0)
    last = spread_far(jnp.concatenate([w_key[0], w_value[0]], axis=1))
    wkv = spread_near(last)

    def spread_weight(shard, pieces, last):
        rows = share // pieces
        fars = []
        for i in range(pieces):
            whole = lax.all_gather(shard[i * rows : (i + 1) * rows], "tensor", axis=0)
            whole, last = tied(whole, last)
            if fars:
                fars[-1] = last
            whole = whole.transpose(1, 0, 2).reshape(rows, tsize * shard.shape[1])
            last = spread_far(whole)
            fars.append(last)
        return fars, last

    def settle(fars):
        parts = [dict(far) for far in fars]
        for bit in low_bits:
            parts = [swap_in(part, bit) for part in parts]
        return jnp.concatenate([part[m] for m in range(dsize) for part in parts], axis=0)

    fars, last = spread_weight(w_query[0], 1, last)
    wqkv = jnp.concatenate([padded(settle(fars)), padded(wkv)], axis=1)
    fars, last = spread_weight(w_out[0].T, 1, last)
    wo = padded(settle(fars))
    late_inputs, last = tied(inputs, last)
    rows_in = join_halves(exchange_half(late_inputs))
    fars, last = spread_weight(w_gate[0], 2, last)
    waits = [fars[1]]
    wg = settle(fars)
    fars, last = spread_weight(w_up[0], 2, last)
    waits += fars
    wu = settle(fars)
    far_down, last = spread_weight(w_down[0].T, 2, last)

    def tables(positions):
        half = HD // 2
        freqs = rope_base ** (-jnp.arange(half, dtype=f32) / half)
        angles = positions.astype(f32)[:, None] * freqs[None, :]
        blank = ((0, 0), (0, HP // 2 - half))
        cosine = jnp.pad(jnp.cos(angles), blank)
        sine = jnp.pad(jnp.sin(angles), blank)
        return (
            jnp.concatenate([cosine, cosine], axis=1),
            jnp.concatenate([-sine, sine], axis=1),
        )

    query_tables = tables(seg * n + jnp.arange(n))
    single = ranks == 1
    offset = (seg * n).astype(jnp.int32).reshape(1)

    back_tables = (query_tables[0], -query_tables[1])
    if single:
        key_tables = back_tables
    else:
        key_tables = tables(jnp.arange(L))
        key_tables = (key_tables[0], -key_tables[1])
    q_lanes = HEADS * HP
    k_lanes = KV_HEADS * HP
    blocks = n // min(ROWS, n)
    attn_row = attn_scale[None]
    mlp_row = mlp_scale[None]

    def head_arrays(qkv):
        if single:
            return (qkv, 0), (qkv, HEADS), (qkv, HEADS + KV_HEADS)
        both = lax.all_gather(
            qkv[:, q_lanes:], "tensor", axis=0, tiled=True, axis_index_groups=same_seq
        )
        return (qkv, 0), (both, 0), (both, KV_HEADS)

    def own_rows(array):
        if single:
            return array
        return lax.psum_scatter(
            array, "tensor", scatter_dimension=0, tiled=True, axis_index_groups=same_seq
        )

    def forward(h, extra=None, waits=None):
        if waits:
            h = tied(h, waits[0])[0]
        qkv, normed = project(h, attn_row, wqkv, *query_tables, q_lanes + k_lanes)
        if waits:
            qkv = tied(qkv, waits[1])[0]
        heads = head_arrays(qkv)
        mixed, lse = attention_forward(*heads, offset, single)
        if extra is not None:
            mixed, extra = tied(mixed, extra)
        if waits:
            mixed = tied(mixed, waits[2])[0]
        middle, normed_mlp = join(mixed, h, wo, mlp_row)
        gate, upward, hidden = gate_up(normed_mlp, wg, wu)
        kept = (h, normed, heads, lse, mixed, middle, normed_mlp, gate, upward, hidden)
        return kept, extra

    def sum_over_tensor(array):
        bits = bits_of(tsize)
        for bit in bits:
            side = (t & bit) != 0
            size = array.shape[1] // 2
            low, high = array[:, :size], array[:, size:]
            got = swapped(jnp.where(side, low, high), "tensor", bit)
            kept_half = jnp.where(side, high, low)
            array = (kept_half.astype(f32) + got.astype(f32)).astype(bf16)
        for bit in reversed(bits):
            side = (t & bit) != 0
            got = swapped(array, "tensor", bit)
            array = jnp.concatenate(
                [jnp.where(side, got, array), jnp.where(side, array, got)], axis=1
            )
        return array

    def to_places(rows):
        return exchange(reorder(rows, 1).reshape(micro, nloc, width))[None]

    def backward(grad, kept, extra):
        h, normed, heads, lse, mixed, middle, normed_mlp, gate, upward, hidden = kept
        middle_grad, middle_bf, _ = feed_back(grad, gate, upward, wd, wg, wu, middle, mlp_row)
        mixed_grad = mm(middle_bf, wo).astype(bf16)
        mixed_grad, extra = tied(mixed_grad, extra)
        dq, dk, dv = attention_backward(
            *heads, mixed_grad, lse, back_tables, key_tables, offset, single
        )
        return dq, own_rows(dk), own_rows(dv), middle_grad, extra

    def backward_all(grad, kept):
        h, normed, heads, lse, mixed, middle, normed_mlp, gate, upward, hidden = kept
        odd, even = rows_to_send(grad), rows_to_keep(grad)
        odd = mm_tn(odd, hidden).astype(bf16)
        even, odd = tied(even, odd)
        got = swap_low(odd)
        even = mm_tn(even, hidden).astype(bf16)
        even, grad = tied(even, grad)
        grad, down = tied(grad, add_low(even, got))
        down = add_partner(down, high_bits)[0]
        gate_grad, up_grad, gate_sum, up_sum = feed_grads(grad, gate, upward, wd, normed_mlp)
        gate_sum = add_partner(split_rows(gate_sum), low_bits)
        gate_grad, up_grad, gate_sum, down = tied(gate_grad, up_grad, gate_sum, down)
        down = scatter_columns(down)
        first, second = send_far(gate_sum)
        gate_sum = receive_far(first)
        up_sum = add_partner(split_rows(up_sum), low_bits)
        middle_grad, middle_bf, mlp_sum = rows_back(
            gate_grad, up_grad, wg, wu, grad, middle, mlp_row
        )
        middle_bf, gate_sum, second[0], up_sum = tied(middle_bf, gate_sum, second[0], up_sum)
        gate_sum = [gate_sum, receive_far(second)]
        mixed_grad = mm(middle_bf, wo).astype(bf16)
        mixed_grad, gate_sum[1], up_sum = tied(mixed_grad, gate_sum[1], up_sum)
        gate_sum = scatter_columns(jnp.concatenate(gate_sum, axis=0))
        first, second = send_far(up_sum)
        up_sum = receive_far(first)
        dq, dk, dv = attention_backward(
            *heads, mixed_grad, lse, back_tables, key_tables, offset, single
        )
        dk = own_rows(dk)
        dv = own_rows(dv)
        dq, dk, dv, down, up_sum, second[0] = tied(dq, dk, dv, down, up_sum, second[0])
        up_sum = [up_sum, receive_far(second)]
        outgoing, attn_sum = heads_back(dq, dk, dv, wqkv, h, middle_grad, attn_row, 0, blocks)
        outgoing, dk, dv, dq, middle_bf = tied(outgoing, dk, dv, dq, middle_bf)
        input_grads = to_places(outgoing)
        kv = jnp.concatenate(
            [unpadded(mm_tn(normed, dk).astype(bf16)), unpadded(mm_tn(normed, dv).astype(bf16))],
            axis=1,
        )
        dq, kv, up_sum[1] = tied(dq, kv, up_sum[1])
        up_sum = scatter_columns(jnp.concatenate(up_sum, axis=0))
        kv = add_partner(split_rows(kv), low_bits)
        query = unpadded(mm_tn(normed, dq).astype(bf16))
        middle_bf, kv, query = tied(middle_bf, kv, query)
        kv = add_partner(kv, high_bits)[0]
        query = add_partner(split_rows(query), low_bits)
        out = unpadded(mm_tn(middle_bf, mixed).astype(bf16))
        out, kv, query, gate_sum = tied(out, kv, query, gate_sum)
        kv = sum_over_tensor(kv)
        query = add_partner(query, high_bits)[0]
        out = add_partner(split_rows(out), low_bits + high_bits)[0]
        pair = jnp.concatenate(
            [out.reshape(share, tsize, -1), query.reshape(share, tsize, -1)], axis=2
        )
        pair, up_sum, input_grads, kv, attn_sum = tied(pair, up_sum, input_grads, kv, attn_sum)
        pair = scatter_columns(pair)
        gains = jnp.concatenate([attn_sum, mlp_sum], axis=0)
        half_cols = pair.shape[1] // 2
        sums = [down, gate_sum, up_sum, pair[:, :half_cols], pair[:, half_cols:]]
        return input_grads, sums + [kv], gains

    def row_chunks():
        if blocks < 2:
            return [(0, blocks)]
        return [(0, blocks // 2), (blocks // 2, blocks - blocks // 2)]

    def send_chunks(make, by, source):
        got = []
        for first, count in row_chunks():
            chunk, source = make(source, first, count)
            if got:
                chunk, got[-1] = tied(chunk, got[-1])
            source, chunk = tied(source, chunk)
            got.append(shifted(chunk, "section", by))
        return jnp.concatenate(got, axis=0)

    kept, _ = forward(rows_in, None, waits)
    far_down[-1], hidden, late_cotangent = tied(far_down[-1], kept[-1], cotangent)
    middle = kept[5]
    wd = settle(far_down)
    half_cot = exchange_half(late_cotangent)
    received = send_chunks(
        lambda source, first, count: (down_rows(source, middle, wd, first, count), source),
        1,
        hidden,
    )
    received, half_cot = tied(received, half_cot)
    kept, cot = forward(jnp.where(first_section, rows_in, received), join_halves(half_cot))
    second_out = down_rows(kept[-1], kept[5], wd, 0, blocks)
    dq, dk, dv, middle_grad, outputs = backward(cot, kept, to_places(second_out))
    returned = send_chunks(
        lambda source, first, count: (
            heads_back(source, dk, dv, wqkv, kept[0], middle_grad, attn_row, first, count)[0],
            source,
        ),
        -1,
        dq,
    )
    input_grads, sums, gains = backward_all(jnp.where(first_section, returned, cot), kept)
    down, gate, up, out, query, kv = sums
    gains = reorder(gains, 1)
    for axis, size in (("dp", dsize), ("tensor", tsize)):
        for bit in bits_of(size):
            gains = gains + swapped(gains, axis, bit)
    return (
        outputs,
        input_grads,
        gains[:1],
        query.astype(f32)[None],
        kv[:, :dims].astype(f32)[None],
        kv[:, dims:].astype(f32)[None],
        out.astype(f32).T[None],
        gains[1:],
        gate.astype(f32)[None],
        up.astype(f32)[None],
        down.astype(f32).T[None],
    )


def solution(mesh):
    in_specs = (
        P(None, ("dp", "tensor"), None),
        P(None, ("dp", "tensor"), None),
        P("section", None),
        P("section", "dp", "tensor"),
        P("section", "dp", None),
        P("section", "dp", None),
        P("section", "tensor", "dp"),
        P("section", None),
        P("section", "dp", "tensor"),
        P("section", "dp", "tensor"),
        P("section", "tensor", "dp"),
    )
    out_specs = (
        P("section", None, ("dp", "tensor"), None),
        P("section", None, ("dp", "tensor"), None),
        P("section", None),
        P("section", "dp", "tensor"),
        P("section", "dp", None),
        P("section", "dp", None),
        P("section", "tensor", "dp"),
        P("section", None),
        P("section", "dp", "tensor"),
        P("section", "dp", "tensor"),
        P("section", "tensor", "dp"),
    )
    return jax.shard_map(local, mesh=mesh, in_specs=in_specs, out_specs=out_specs, check_vma=False)
```

```python
import functools

import jax
import jax.numpy as jnp
from jax import lax
from jax.experimental import pallas as pl
from jax.experimental.pallas import tpu as pltpu
from jax.sharding import PartitionSpec as P

HEADS = 16
KV_HEADS = 8
HD = 96
L = 1024

epsilon = 1e-05
rope_base = 100000.0
bf16 = jnp.bfloat16
f32 = jnp.float32


def shifted(array, axis, by):
    size = lax.axis_size(axis)
    pairs = [(i, i + by) for i in range(size) if 0 <= i + by < size]
    return lax.ppermute(array, axis, pairs)


def swapped(array, axis, bit):
    return lax.ppermute(array, axis, [(i, i ^ bit) for i in range(lax.axis_size(axis))])


def bits_of(size):
    return [1 << k for k in range(size.bit_length() - 1)]


def mm(left, right):
    return jnp.dot(left, right, preferred_element_type=f32)


def mm_nt(left, right):
    return lax.dot_general(
        left, right, (((1,), (1,)), ((), ())), preferred_element_type=f32
    )


def mm_tn(left, right):
    return lax.dot_general(
        left, right, (((0,), (0,)), ((), ())), preferred_element_type=f32
    )


QB = 256
ROWS = 256
HP = 128
LOG2E = 1.4426950408889634
MIB = 2**20


def whole(shape):
    rest = (0,) * len(shape)
    return pl.BlockSpec(tuple(shape), lambda *_: rest, pipeline_mode=pl.Buffered(1))


def rows_of(shape, first=0):
    return pl.BlockSpec(tuple(shape), lambda i: (first + i, 0))


def columns_of(shape, first=0):
    return pl.BlockSpec(tuple(shape), lambda i: (0, first + i))


def kernel_call(kernel, grid, in_specs, out_specs, out_shape, flops, name, scratch=(), trans=0):
    moved = sum(2 * shape.size for shape in out_shape)
    return pl.pallas_call(
        kernel,
        grid=grid,
        in_specs=in_specs,
        out_specs=out_specs,
        out_shape=out_shape,
        scratch_shapes=scratch,
        compiler_params=pltpu.CompilerParams(vmem_limit_bytes=56 * MIB),
        cost_estimate=pl.CostEstimate(
            flops=int(flops), bytes_accessed=int(moved + flops // 512), transcendentals=int(trans)
        ),
        name=name,
    )


def turned(values, cosine, sine):
    parts = []
    for at in range(0, values.shape[1], HP):
        head = values[:, at : at + HP]
        parts.append(head * cosine + pltpu.roll(head, HP // 2, 1) * sine)
    return parts[0] if len(parts) == 1 else jnp.concatenate(parts, axis=1)


def project_kernel(h_ref, gain_ref, w_ref, cos_ref, sin_ref, out_ref, normed_ref, *, turning):
    step = pl.program_id(0)

    @pl.when(step == 0)
    def _():
        rows = h_ref[...].astype(f32)
        inverse = lax.rsqrt(jnp.mean(rows * rows, axis=-1, keepdims=True) + epsilon)
        normed_ref[...] = (rows * inverse * gain_ref[...]).astype(bf16)

    values = mm(normed_ref[...], w_ref[...])

    @pl.when(step < turning)
    def _():
        out_ref[...] = turned(values, cos_ref[...], sin_ref[...]).astype(bf16)

    @pl.when(step >= turning)
    def _():
        out_ref[...] = values.astype(bf16)


def project(h, gain, w, cosine, sine, turned_columns):
    n, width = h.shape
    total = w.shape[1]
    block = 512
    out_shape = (
        jax.ShapeDtypeStruct((n, total), bf16),
        jax.ShapeDtypeStruct((n, width), bf16),
    )
    return kernel_call(
        functools.partial(project_kernel, turning=turned_columns // block),
        (total // block,),
        [
            whole(h.shape), whole(gain.shape), columns_of((width, block)),
            whole(cosine.shape), whole(sine.shape),
        ],
        [columns_of((n, block)), whole((n, width))],
        out_shape,
        2 * n * width * total,
        "project",
    )(h, gain, w, cosine, sine)


def join_kernel(mixed_ref, h_ref, w_ref, gain_ref, middle_ref, normed_ref):
    middle = h_ref[...].astype(f32) + mm_nt(mixed_ref[...], w_ref[...])
    middle_ref[...] = middle
    inverse = lax.rsqrt(jnp.mean(middle * middle, axis=-1, keepdims=True) + epsilon)
    normed_ref[...] = (middle * inverse * gain_ref[...]).astype(bf16)


def join(mixed, h, w, gain):
    n, width = h.shape
    block = min(ROWS, n)
    out_shape = (
        jax.ShapeDtypeStruct((n, width), f32),
        jax.ShapeDtypeStruct((n, width), bf16),
    )
    return kernel_call(
        join_kernel,
        (n // block,),
        [
            rows_of((block, mixed.shape[1])), rows_of((block, width)),
            whole(w.shape), whole(gain.shape),
        ],
        [rows_of((block, width))] * 2,
        out_shape,
        2 * n * width * mixed.shape[1],
        "join",
    )(mixed, h, w, gain)


def gate_up_kernel(x_ref, wg_ref, wu_ref, gate_ref, up_ref, hidden_ref):
    x = x_ref[...]
    gate = mm(x, wg_ref[...])
    upward = mm(x, wu_ref[...])
    gate_ref[...] = gate.astype(bf16)
    up_ref[...] = upward.astype(bf16)
    hidden_ref[...] = (gate * jax.nn.sigmoid(gate) * upward).astype(bf16)


def gate_up(x, wg, wu):
    n, width = x.shape
    total = wg.shape[1]
    block = 512
    return kernel_call(
        gate_up_kernel,
        (total // block,),
        [whole(x.shape), columns_of((width, block)), columns_of((width, block))],
        [columns_of((n, block))] * 3,
        (jax.ShapeDtypeStruct((n, total), bf16),) * 3,
        4 * n * width * total,
        "gate_up",
        trans=n * total,
    )(x, wg, wu)


def down_kernel(hidden_ref, middle_ref, w_ref, out_ref):
    out_ref[...] = (middle_ref[...] + mm_nt(hidden_ref[...], w_ref[...])).astype(bf16)


def down_rows(hidden, middle, w, first, count):
    n, width = middle.shape
    block = min(ROWS, n)
    return kernel_call(
        down_kernel,
        (count,),
        [
            rows_of((block, hidden.shape[1]), first), rows_of((block, width), first),
            whole(w.shape),
        ],
        [rows_of((block, width))],
        (jax.ShapeDtypeStruct((count * block, width), bf16),),
        2 * count * block * width * hidden.shape[1],
        "down_rows",
    )(hidden, middle, w)[0]


def hidden_back(grad_ref, gate_ref, up_ref, wd_ref):
    gate = gate_ref[...].astype(f32)
    hidden_grad = mm(grad_ref[...], wd_ref[...])
    sigma = jax.nn.sigmoid(gate)
    gate_grad = hidden_grad * up_ref[...].astype(f32) * (sigma * (1.0 + gate * (1.0 - sigma)))
    return gate_grad.astype(bf16), (hidden_grad * gate * sigma).astype(bf16)


def feed_back_kernel(
    grad_ref, gate_ref, up_ref, wd_ref, wg_ref, wu_ref, middle_ref, gain_ref,
    total_ref, low_ref, sum_ref
):
    step = pl.program_id(0)
    gate_grad, up_grad = hidden_back(grad_ref, gate_ref, up_ref, wd_ref)
    accumulate_back(step, gate_grad, up_grad, wg_ref, wu_ref, total_ref)
    finish_back(step, grad_ref, middle_ref, gain_ref, total_ref, low_ref, sum_ref)


def feed_grads_kernel(
    grad_ref, gate_ref, up_ref, wd_ref, normed_ref,
    gate_grad_ref, up_grad_ref, gate_sum_ref, up_sum_ref, turned_ref
):
    @pl.when(pl.program_id(0) == 0)
    def _():
        turned_ref[...] = normed_ref[...].T

    gate_grad, up_grad = hidden_back(grad_ref, gate_ref, up_ref, wd_ref)
    gate_grad_ref[...] = gate_grad
    up_grad_ref[...] = up_grad
    gate_sum_ref[...] = mm(turned_ref[...], gate_grad).astype(bf16)
    up_sum_ref[...] = mm(turned_ref[...], up_grad).astype(bf16)


def feed_grads(grad, gate, upward, wd, normed):
    n, width = grad.shape
    total = gate.shape[1]
    block = 512
    return kernel_call(
        feed_grads_kernel,
        (total // block,),
        [
            whole(grad.shape), columns_of((n, block)), columns_of((n, block)),
            columns_of((width, block)), whole(normed.shape),
        ],
        [columns_of((n, block))] * 2 + [columns_of((width, block))] * 2,
        (jax.ShapeDtypeStruct((n, total), bf16),) * 2
        + (jax.ShapeDtypeStruct((width, total), bf16),) * 2,
        6 * n * width * total,
        "feed_grads",
        scratch=[pltpu.VMEM((width, n), bf16)],
        trans=n * total,
    )(grad, gate, upward, wd, normed)


def rows_back_kernel(
    gate_grad_ref, up_grad_ref, wg_ref, wu_ref, grad_ref, middle_ref, gain_ref,
    total_ref, low_ref, sum_ref
):
    step = pl.program_id(0)
    accumulate_back(step, gate_grad_ref[...], up_grad_ref[...], wg_ref, wu_ref, total_ref)
    finish_back(step, grad_ref, middle_ref, gain_ref, total_ref, low_ref, sum_ref)


def back_outputs(n, width):
    return (
        jax.ShapeDtypeStruct((n, width), f32),
        jax.ShapeDtypeStruct((n, width), bf16),
        jax.ShapeDtypeStruct((1, width), f32),
    )


def rows_back(gate_grad, up_grad, wg, wu, grad, middle, gain):
    n, width = grad.shape
    total = wg.shape[1]
    block = 512
    return kernel_call(
        rows_back_kernel,
        (total // block,),
        [
            columns_of((n, block)), columns_of((n, block)),
            columns_of((width, block)), columns_of((width, block)),
            whole(grad.shape), whole(middle.shape), whole(gain.shape),
        ],
        [whole((n, width)), whole((n, width)), whole((1, width))],
        back_outputs(n, width),
        4 * n * width * total,
        "rows_back",
    )(gate_grad, up_grad, wg, wu, grad, middle, gain)


def accumulate_back(step, gate_grad, up_grad, wg_ref, wu_ref, total_ref):
    part = mm_nt(gate_grad, wg_ref[...]) + mm_nt(up_grad, wu_ref[...])

    @pl.when(step == 0)
    def _():
        total_ref[...] = part

    @pl.when(step > 0)
    def _():
        total_ref[...] += part


def finish_back(step, grad_ref, middle_ref, gain_ref, total_ref, low_ref, sum_ref):
    @pl.when(step == pl.num_programs(0) - 1)
    def _():
        n = total_ref.shape[0]
        size = min(QB, n)
        sums = 0.0
        for at in range(0, n, size):
            rows = slice(at, at + size)
            middle = middle_ref[rows]
            back = total_ref[rows]
            inverse = lax.rsqrt(jnp.mean(middle * middle, axis=-1, keepdims=True) + epsilon)
            sums = sums + jnp.sum(back * middle * inverse, axis=0, keepdims=True)
            scaled = back * gain_ref[...]
            mean_term = jnp.mean(scaled * middle, axis=-1, keepdims=True)
            branch = scaled * inverse - middle * (inverse * inverse * inverse * mean_term)
            result = grad_ref[rows].astype(f32) + branch
            total_ref[rows] = result
            low_ref[rows] = result.astype(bf16)
        sum_ref[...] = sums


def feed_back(grad, gate, upward, wd, wg, wu, middle, gain):
    n, width = grad.shape
    total = wg.shape[1]
    block = 512
    return kernel_call(
        feed_back_kernel,
        (total // block,),
        [
            whole(grad.shape), columns_of((n, block)), columns_of((n, block)),
            columns_of((width, block)), columns_of((width, block)), columns_of((width, block)),
            whole(middle.shape), whole(gain.shape),
        ],
        [whole((n, width)), whole((n, width)), whole((1, width))],
        back_outputs(n, width),
        6 * n * width * total,
        "feed_back",
        trans=n * total,
    )(grad, gate, upward, wd, wg, wu, middle, gain)


def heads_back_kernel(
    dq_ref, dk_ref, dv_ref, w_ref, h_ref, grad_ref, gain_ref, out_ref, sum_ref
):
    step = pl.program_id(0)
    back = 0.0
    at = 0
    for ref in (dq_ref, dk_ref, dv_ref):
        back = back + mm_nt(ref[...], w_ref[:, at : at + ref.shape[1]])
        at += ref.shape[1]
    rows = h_ref[...].astype(f32)
    inverse = lax.rsqrt(jnp.mean(rows * rows, axis=-1, keepdims=True) + epsilon)
    sums = jnp.sum(back * rows * inverse, axis=0, keepdims=True)
    scaled = back * gain_ref[...]
    mean_term = jnp.mean(scaled * rows, axis=-1, keepdims=True)
    branch = scaled * inverse - rows * (inverse * inverse * inverse * mean_term)
    out_ref[...] = (grad_ref[...] + branch).astype(bf16)

    @pl.when(step == 0)
    def _():
        sum_ref[...] = sums

    @pl.when(step > 0)
    def _():
        sum_ref[...] += sums


def heads_back(dq, dk, dv, w, h, grad, gain, first, count):
    n, width = h.shape
    block = min(ROWS, n)
    out_shape = (
        jax.ShapeDtypeStruct((count * block, width), bf16),
        jax.ShapeDtypeStruct((1, width), f32),
    )
    return kernel_call(
        heads_back_kernel,
        (count,),
        [rows_of((block, a.shape[1]), first) for a in (dq, dk, dv)]
        + [
            whole(w.shape), rows_of((block, width), first), rows_of((block, width), first),
            whole(gain.shape),
        ],
        [rows_of((block, width)), whole((1, width))],
        out_shape,
        2 * count * block * width * w.shape[1],
        "heads_back",
    )(dq, dk, dv, w, h, grad, gain)


def two_heads(ref, rows):
    return jnp.concatenate([ref[rows, :HP], ref[rows, HP:]], axis=0)


def score_parts(offset_ref, k_ref, q, i, size, single):
    cols = q.shape[0]
    first = i * size if single else 0
    count = size if single else k_ref.shape[0]
    parts = []
    if first:
        parts.append((0, first, mm_nt(k_ref[:first], q)))
    diagonal = mm_nt(k_ref[first : first + count], q)
    key_at = first + lax.broadcasted_iota(jnp.int32, (count, cols), 0)
    query_at = i * size + lax.rem(lax.broadcasted_iota(jnp.int32, (count, cols), 1), size)
    if not single:
        query_at = query_at + offset_ref[0]
    diagonal = jnp.where(key_at <= query_at, diagonal, -1e30)
    parts.append((first, count, diagonal))
    return parts


def attend_forward_kernel(offset_ref, q_ref, k_ref, v_ref, o_ref, lse_ref, *, single):
    n = q_ref.shape[0]
    size = min(QB, n)
    factor = HD ** (-0.5) * LOG2E
    vt = v_ref[...].T
    for i in range(n // size):
        rows = slice(i * size, (i + 1) * size)
        q = two_heads(q_ref, rows)
        parts = score_parts(offset_ref, k_ref, q, i, size, single)
        top = functools.reduce(
            jnp.maximum, [jnp.max(part, axis=0, keepdims=True) for _, _, part in parts]
        )
        total = 0.0
        mixed = 0.0
        for first, count, part in parts:
            weights = jnp.exp2((part - top) * factor)
            total = total + jnp.sum(weights, axis=0, keepdims=True)
            mixed = mixed + mm(vt[:, first : first + count], weights.astype(bf16))
        mixed = (mixed * (1.0 / total)).T.astype(bf16)
        o_ref[rows, :HP] = mixed[:size]
        o_ref[rows, HP:] = mixed[size:]
        lse_ref[0, i] = top * factor + jnp.log2(total)


def attend_backward_kernel(
    offset_ref, q_ref, k_ref, v_ref, g_ref, lse_ref, cosq_ref, sinq_ref, cosk_ref, sink_ref,
    dq_ref, dk_ref, dv_ref, dk_acc, dv_acc, *, single
):
    n = q_ref.shape[0]
    size = min(QB, n)
    scale = HD ** (-0.5)
    factor = scale * LOG2E
    kt = k_ref[...].T
    dk_acc[...] = jnp.zeros_like(dk_acc)
    dv_acc[...] = jnp.zeros_like(dv_acc)
    for i in range(n // size):
        rows = slice(i * size, (i + 1) * size)
        q = two_heads(q_ref, rows)
        g = two_heads(g_ref, rows)
        lse = lse_ref[0, i]
        kept = []
        centre = 0.0
        for first, count, part in score_parts(offset_ref, k_ref, q, i, size, single):
            keys = slice(first, first + count)
            probs = jnp.exp2(part * factor - lse)
            prob_grad = mm_nt(v_ref[keys], g)
            dv_acc[keys] += mm(probs.astype(bf16), g)
            centre = centre + jnp.sum(probs * prob_grad, axis=0, keepdims=True)
            kept.append((keys, probs, prob_grad))
        dqt = 0.0
        for keys, probs, prob_grad in kept:
            score_grad = (probs * (prob_grad - centre)).astype(bf16)
            dk_acc[keys] += mm(score_grad, q)
            dqt = dqt + mm(kt[:, keys], score_grad)
        dq = (dqt * scale).T
        for c in range(2):
            head = turned(dq[c * size : (c + 1) * size], cosq_ref[rows], sinq_ref[rows])
            dq_ref[rows, c * HP : (c + 1) * HP] = head.astype(bf16)
    dk_ref[...] = turned(dk_acc[...] * scale, cosk_ref[...], sink_ref[...]).astype(bf16)
    dv_ref[...] = dv_acc[...].astype(bf16)


SCALAR = pl.BlockSpec(memory_space=pltpu.SMEM)


def attention_forward(q, k, v, offset, single):
    n = q[0].shape[0]
    size = min(QB, n)
    count = k[0].shape[0]
    out_shape = (
        jax.ShapeDtypeStruct((n, HEADS * HP), bf16),
        jax.ShapeDtypeStruct((KV_HEADS, n // size, 1, 2 * size), f32),
    )
    return kernel_call(
        functools.partial(attend_forward_kernel, single=single),
        (KV_HEADS,),
        [
            SCALAR, columns_of((n, 2 * HP), q[1] // 2), columns_of((count, HP), k[1]),
            columns_of((count, HP), v[1]),
        ],
        [
            columns_of((n, 2 * HP)),
            pl.BlockSpec((1, n // size, 1, 2 * size), lambda h: (h, 0, 0, 0)),
        ],
        out_shape,
        4 * HEADS * n * count * HP,
        "attend_forward",
        trans=HEADS * n * count,
    )(offset, q[0], k[0], v[0])


def attention_backward(q, k, v, mixed_grad, lse, query_tables, key_tables, offset, single):
    n = q[0].shape[0]
    size = min(QB, n)
    count = k[0].shape[0]
    out_shape = (
        jax.ShapeDtypeStruct((n, HEADS * HP), bf16),
        jax.ShapeDtypeStruct((count, KV_HEADS * HP), bf16),
        jax.ShapeDtypeStruct((count, KV_HEADS * HP), bf16),
    )
    return kernel_call(
        functools.partial(attend_backward_kernel, single=single),
        (KV_HEADS,),
        [
            SCALAR, columns_of((n, 2 * HP), q[1] // 2), columns_of((count, HP), k[1]),
            columns_of((count, HP), v[1]), columns_of((n, 2 * HP)),
            pl.BlockSpec((1, n // size, 1, 2 * size), lambda h: (h, 0, 0, 0)),
        ]
        + [whole(table.shape) for table in query_tables + key_tables],
        [columns_of((n, 2 * HP)), columns_of((count, HP)), columns_of((count, HP))],
        out_shape,
        10 * HEADS * n * count * HP,
        "attend_backward",
        scratch=[pltpu.VMEM((count, HP), f32), pltpu.VMEM((count, HP), f32)],
        trans=HEADS * n * count,
    )(offset, q[0], k[0], v[0], mixed_grad, lse, *query_tables, *key_tables)


def padded(array):
    rows = array.shape[0]
    parts = array.reshape(rows, -1, HD // 2)
    parts = jnp.pad(parts, ((0, 0), (0, 0), (0, HP // 2 - HD // 2)))
    return parts.reshape(rows, -1)


def unpadded(array):
    rows = array.shape[0]
    return array.reshape(rows, -1, HP // 2)[:, :, : HD // 2].reshape(rows, -1)


def local(
    inputs, cotangent, attn_gain, w_query, w_key, w_value, w_out, mlp_gain, w_gate, w_up, w_down
):
    micro, nloc, width = inputs.shape
    tsize = lax.axis_size("tensor")
    dsize = lax.axis_size("dp")
    ranks = tsize // micro
    n = nloc * micro
    share = width // dsize
    first_section = lax.axis_index("section") == 0
    t = lax.axis_index("tensor")
    d = lax.axis_index("dp")
    seq = t % micro
    seg = t // micro
    copies = HEADS // KV_HEADS
    dims = KV_HEADS * HD
    low_bits = bits_of(dsize)[:1]
    high_bits = bits_of(dsize)[1:]
    same_seq = [[g + micro * r for r in range(ranks)] for g in range(micro)]

    def arrivals(blocks):
        return [
            swapped(lax.dynamic_index_in_dim(blocks, seq ^ j, 0, keepdims=True), "tensor", j)
            for j in range(1, micro)
        ]

    def settled(blocks, got):
        for j in range(1, micro):
            blocks = lax.dynamic_update_slice_in_dim(blocks, got[j - 1], seq ^ j, 0)
        return blocks

    def exchange(blocks):
        return settled(blocks, arrivals(blocks))

    def reorder(array, axis):
        return jnp.concatenate(
            [lax.dynamic_slice_in_dim(array, (d ^ m) * share, share, axis) for m in range(dsize)],
            axis=axis,
        )

    def swap_in(parts, bit):
        parts = dict(parts)
        for m in sorted(parts):
            parts[m ^ bit] = swapped(parts[m], "dp", bit)
        return parts

    def spread_far(block):
        parts = {0: block}
        for bit in reversed(high_bits):
            parts = swap_in(parts, bit)
        return parts

    def spread_near(parts):
        for bit in low_bits:
            parts = swap_in(parts, bit)
        return jnp.concatenate([parts[m] for m in range(dsize)], axis=0)

    def gather_columns(shard):
        whole = lax.all_gather(shard, "tensor", axis=0)
        return whole.transpose(1, 0, 2).reshape(share, tsize * shard.shape[1])

    def tied(*arrays):
        return lax.optimization_barrier(arrays)

    def exchange_half(array):
        side = lax.axis_index("section")
        return exchange(lax.dynamic_slice_in_dim(array, side * (width // 2), width // 2, 2))

    def join_halves(mine):
        other = swapped(mine, "section", 1)
        whole = jnp.concatenate(
            [jnp.where(first_section, mine, other), jnp.where(first_section, other, mine)], axis=2
        )
        return reorder(whole.reshape(n, width), 1)

    def split_rows(grad):
        return {m: grad[m * share : (m + 1) * share].astype(bf16) for m in range(dsize)}

    def add_partner(parts, bits):
        for bit in bits:
            summed = {}
            for m in sorted(parts):
                if not m & bit:
                    got = swapped(parts[m ^ bit], "dp", bit)
                    summed[m] = (parts[m].astype(f32) + got.astype(f32)).astype(bf16)
            parts = summed
        return parts

    def rows_to_send(array):
        return jnp.concatenate(
            [array[:, m * share : (m + 1) * share] for m in range(dsize) if m & 1], axis=1
        )

    def rows_to_keep(array):
        return jnp.concatenate(
            [array[:, m * share : (m + 1) * share] for m in range(dsize) if not m & 1], axis=1
        )

    def swap_low(array):
        return swapped(array, "dp", 1)

    def add_low(mine, got):
        total = (mine.astype(f32) + got.astype(f32)).astype(bf16)
        return {2 * i: total[i * share : (i + 1) * share] for i in range(dsize // 2)}

    def send_far(parts, size):
        pairs = []
        for rows in (slice(0, size), slice(size, share)):
            half = {m: part[rows] for m, part in parts.items()}
            bit = high_bits[0]
            kept = {m: part for m, part in half.items() if not m & bit}
            pairs.append([kept, {m: swapped(half[m ^ bit], "dp", bit) for m in kept}])
        return pairs

    def receive_far(pair):
        kept, got = pair
        parts = {m: (kept[m].astype(f32) + got[m].astype(f32)).astype(bf16) for m in kept}
        return add_partner(parts, high_bits[1:])[0]

    def scatter_columns(part):
        part = part.reshape(share, tsize, -1).transpose(1, 0, 2)
        return lax.psum_scatter(part, "tensor", scatter_dimension=0)

    attn_scale = reorder(attn_gain[0], 0)
    mlp_scale = reorder(mlp_gain[0], 0)
    mine = exchange_half(inputs)
    last = spread_far(jnp.concatenate([w_key[0], w_value[0]], axis=1))
    mine, last = tied(mine, last)
    wkv = spread_near(last)
    rows_in = join_halves(mine)

    def spread_weight(shard, pieces, last):
        rows = share // pieces
        fars = []
        for i in range(pieces):
            whole = lax.all_gather(shard[i * rows : (i + 1) * rows], "tensor", axis=0)
            whole, last = tied(whole, last)
            if fars:
                fars[-1] = last
            whole = whole.transpose(1, 0, 2).reshape(rows, tsize * shard.shape[1])
            last = spread_far(whole)
            fars.append(last)
        return fars, last

    def settle(fars):
        parts = [dict(far) for far in fars]
        for bit in low_bits:
            parts = [swap_in(part, bit) for part in parts]
        return jnp.concatenate([part[m] for m in range(dsize) for part in parts], axis=0)

    fars, last = spread_weight(w_query[0], 1, last)
    wqkv = jnp.concatenate([padded(settle(fars)), padded(wkv)], axis=1)
    fars, last = spread_weight(w_out[0].T, 1, last)
    wo = padded(settle(fars))
    fars, last = spread_weight(w_gate[0], 2, last)
    waits = list(fars)
    wg = settle(fars)
    fars, last = spread_weight(w_up[0], 2, last)
    waits.append(fars[0])
    wu = settle(fars)
    far_down, last = spread_weight(w_down[0].T, 2, last)

    def tables(positions):
        half = HD // 2
        freqs = rope_base ** (-jnp.arange(half, dtype=f32) / half)
        angles = positions.astype(f32)[:, None] * freqs[None, :]
        blank = ((0, 0), (0, HP // 2 - half))
        cosine = jnp.pad(jnp.cos(angles), blank)
        sine = jnp.pad(jnp.sin(angles), blank)
        return (
            jnp.concatenate([cosine, cosine], axis=1),
            jnp.concatenate([-sine, sine], axis=1),
        )

    query_tables = tables(seg * n + jnp.arange(n))
    single = ranks == 1
    offset = (seg * n).astype(jnp.int32).reshape(1)

    back_tables = (query_tables[0], -query_tables[1])
    if single:
        key_tables = back_tables
    else:
        key_tables = tables(jnp.arange(L))
        key_tables = (key_tables[0], -key_tables[1])
    q_lanes = HEADS * HP
    k_lanes = KV_HEADS * HP
    blocks = n // min(ROWS, n)
    attn_row = attn_scale[None]
    mlp_row = mlp_scale[None]

    def head_arrays(qkv):
        if single:
            return (qkv, 0), (qkv, HEADS), (qkv, HEADS + KV_HEADS)
        both = lax.all_gather(
            qkv[:, q_lanes:], "tensor", axis=0, tiled=True, axis_index_groups=same_seq
        )
        return (qkv, 0), (both, 0), (both, KV_HEADS)

    def own_rows(array):
        if single:
            return array
        return lax.psum_scatter(
            array, "tensor", scatter_dimension=0, tiled=True, axis_index_groups=same_seq
        )

    def forward(h, extra=None, waits=None):
        if waits:
            h = tied(h, waits[0])[0]
        qkv, normed = project(h, attn_row, wqkv, *query_tables, q_lanes + k_lanes)
        if waits:
            qkv = tied(qkv, waits[1])[0]
        heads = head_arrays(qkv)
        mixed, lse = attention_forward(*heads, offset, single)
        if extra is not None:
            mixed, extra = tied(mixed, extra)
        if waits:
            mixed = tied(mixed, waits[2])[0]
        middle, normed_mlp = join(mixed, h, wo, mlp_row)
        gate, upward, hidden = gate_up(normed_mlp, wg, wu)
        kept = (h, normed, heads, lse, mixed, middle, normed_mlp, gate, upward, hidden)
        return kept, extra

    def sum_over_tensor(array):
        bits = bits_of(tsize)
        for bit in bits:
            side = (t & bit) != 0
            size = array.shape[1] // 2
            low, high = array[:, :size], array[:, size:]
            got = swapped(jnp.where(side, low, high), "tensor", bit)
            kept_half = jnp.where(side, high, low)
            array = (kept_half.astype(f32) + got.astype(f32)).astype(bf16)
        for bit in reversed(bits):
            side = (t & bit) != 0
            got = swapped(array, "tensor", bit)
            array = jnp.concatenate(
                [jnp.where(side, got, array), jnp.where(side, array, got)], axis=1
            )
        return array

    def to_places(rows):
        return exchange(reorder(rows, 1).reshape(micro, nloc, width))[None]

    def backward(grad, kept, extra):
        h, normed, heads, lse, mixed, middle, normed_mlp, gate, upward, hidden = kept
        middle_grad, middle_bf, _ = feed_back(grad, gate, upward, wd, wg, wu, middle, mlp_row)
        mixed_grad = mm(middle_bf, wo).astype(bf16)
        mixed_grad, extra = tied(mixed_grad, extra)
        dq, dk, dv = attention_backward(
            *heads, mixed_grad, lse, back_tables, key_tables, offset, single
        )
        return dq, own_rows(dk), own_rows(dv), middle_grad, extra

    def backward_all(grad, kept):
        h, normed, heads, lse, mixed, middle, normed_mlp, gate, upward, hidden = kept
        odd, even = rows_to_send(grad), rows_to_keep(grad)
        odd = mm_tn(odd, hidden).astype(bf16)
        even, odd = tied(even, odd)
        got = swap_low(odd)
        even = mm_tn(even, hidden).astype(bf16)
        even, grad = tied(even, grad)
        grad, down = tied(grad, add_low(even, got))
        down = add_partner(down, high_bits)[0]
        gate_grad, up_grad, gate_sum, up_sum = feed_grads(grad, gate, upward, wd, normed_mlp)
        gate_sum = add_partner(split_rows(gate_sum), low_bits)
        gate_grad, up_grad, gate_sum, down = tied(gate_grad, up_grad, gate_sum, down)
        down = scatter_columns(down)
        first, second = send_far(gate_sum, share // 2)
        gate_sum = receive_far(first)
        up_sum = add_partner(split_rows(up_sum), low_bits)
        middle_grad, middle_bf, mlp_sum = rows_back(
            gate_grad, up_grad, wg, wu, grad, middle, mlp_row
        )
        middle_bf, gate_sum, second[0], up_sum = tied(middle_bf, gate_sum, second[0], up_sum)
        gate_sum = [gate_sum, receive_far(second)]
        mixed_grad = mm(middle_bf, wo).astype(bf16)
        mixed_grad, gate_sum[1], up_sum = tied(mixed_grad, gate_sum[1], up_sum)
        gate_sum = scatter_columns(jnp.concatenate(gate_sum, axis=0))
        first, second = send_far(up_sum, share // 4)
        up_sum = receive_far(first)
        dq, dk, dv = attention_backward(
            *heads, mixed_grad, lse, back_tables, key_tables, offset, single
        )
        dk = own_rows(dk)
        dv = own_rows(dv)
        dq, dk, dv, down, up_sum, second[0] = tied(dq, dk, dv, down, up_sum, second[0])
        up_sum = [up_sum, receive_far(second)]
        outgoing, attn_sum = heads_back(dq, dk, dv, wqkv, h, middle_grad, attn_row, 0, blocks)
        outgoing, dk, dv, dq, middle_bf, up_sum[1] = tied(
            outgoing, dk, dv, dq, middle_bf, up_sum[1]
        )
        blocks_out = reorder(outgoing, 1).reshape(micro, nloc, width)
        got = arrivals(blocks_out)
        up_sum = scatter_columns(jnp.concatenate(up_sum, axis=0))
        kv = jnp.concatenate(
            [unpadded(mm_tn(normed, dk).astype(bf16)), unpadded(mm_tn(normed, dv).astype(bf16))],
            axis=1,
        )
        dq, kv = tied(dq, kv)
        kv = add_partner(split_rows(kv), low_bits)
        query = unpadded(mm_tn(normed, dq).astype(bf16))
        middle_bf, kv, query, got[0] = tied(middle_bf, kv, query, got[0])
        kv = add_partner(kv, high_bits)[0]
        query = add_partner(split_rows(query), low_bits)
        out = unpadded(mm_tn(middle_bf, mixed).astype(bf16))
        out, kv, query, gate_sum, got[1:-1] = tied(out, kv, query, gate_sum, got[1:-1])
        query = add_partner(query, high_bits)[0]
        out = add_partner(split_rows(out), low_bits + high_bits)[0]
        out, query, got[-1:] = tied(out, query, got[-1:])
        input_grads = settled(blocks_out, got)[None]
        kv = sum_over_tensor(kv)
        pair = jnp.concatenate(
            [out.reshape(share, tsize, -1), query.reshape(share, tsize, -1)], axis=2
        )
        pair, up_sum, attn_sum = tied(pair, up_sum, attn_sum)
        pair = scatter_columns(pair)
        gains = jnp.concatenate([attn_sum, mlp_sum], axis=0)
        half_cols = pair.shape[1] // 2
        sums = [down, gate_sum, up_sum, pair[:, :half_cols], pair[:, half_cols:]]
        return input_grads, sums + [kv], gains

    def row_chunks():
        if blocks < 2:
            return [(0, blocks)]
        return [(0, blocks // 2), (blocks // 2, blocks - blocks // 2)]

    def send_chunks(make, by, source):
        got = []
        for first, count in row_chunks():
            chunk, source = make(source, first, count)
            if got:
                chunk, got[-1] = tied(chunk, got[-1])
            source, chunk = tied(source, chunk)
            got.append(shifted(chunk, "section", by))
        return jnp.concatenate(got, axis=0)

    kept, _ = forward(rows_in, None, waits)
    far_down[-1], hidden, late_cotangent = tied(far_down[-1], kept[-1], cotangent)
    middle = kept[5]
    wd = settle(far_down)
    half_cot = exchange_half(late_cotangent)
    received = send_chunks(
        lambda source, first, count: (down_rows(source, middle, wd, first, count), source),
        1,
        hidden,
    )
    received, half_cot = tied(received, half_cot)
    kept, cot = forward(jnp.where(first_section, rows_in, received), join_halves(half_cot))
    second_out = down_rows(kept[-1], kept[5], wd, 0, blocks)
    dq, dk, dv, middle_grad, outputs = backward(cot, kept, to_places(second_out))
    returned = send_chunks(
        lambda source, first, count: (
            heads_back(source, dk, dv, wqkv, kept[0], middle_grad, attn_row, first, count)[0],
            source,
        ),
        -1,
        dq,
    )
    input_grads, sums, gains = backward_all(jnp.where(first_section, returned, cot), kept)
    down, gate, up, out, query, kv = sums
    gains = reorder(gains, 1)
    for axis, size in (("dp", dsize), ("tensor", tsize)):
        for bit in bits_of(size):
            gains = gains + swapped(gains, axis, bit)
    return (
        outputs,
        input_grads,
        gains[:1],
        query.astype(f32)[None],
        kv[:, :dims].astype(f32)[None],
        kv[:, dims:].astype(f32)[None],
        out.astype(f32).T[None],
        gains[1:],
        gate.astype(f32)[None],
        up.astype(f32)[None],
        down.astype(f32).T[None],
    )


def solution(mesh):
    in_specs = (
        P(None, ("dp", "tensor"), None),
        P(None, ("dp", "tensor"), None),
        P("section", None),
        P("section", "dp", "tensor"),
        P("section", "dp", None),
        P("section", "dp", None),
        P("section", "tensor", "dp"),
        P("section", None),
        P("section", "dp", "tensor"),
        P("section", "dp", "tensor"),
        P("section", "tensor", "dp"),
    )
    out_specs = (
        P("section", None, ("dp", "tensor"), None),
        P("section", None, ("dp", "tensor"), None),
        P("section", None),
        P("section", "dp", "tensor"),
        P("section", "dp", None),
        P("section", "dp", None),
        P("section", "tensor", "dp"),
        P("section", None),
        P("section", "dp", "tensor"),
        P("section", "dp", "tensor"),
        P("section", "tensor", "dp"),
    )
    return jax.shard_map(local, mesh=mesh, in_specs=in_specs, out_specs=out_specs, check_vma=False)
```
